32 devices in a mesh: seq: 8 (over z, x), mp: 2 (over y), role: 2 (over core).
Axes of the slice: x: 2, y: 2, z: 4, core: 2. Of those that a mesh axis runs over, the one named last changes fastest.
Arguments:
- gen_hidden: bfloat16 [8, 16, 3072], P('seq', None, ('mp', 'role')), may hold values from -6 to 6
- gen_out_weight: bfloat16 [3072, 128], P(('mp', 'role')), may hold values from -0.109375 to 0.109375
- patch_order: int32 [8], replicated, may hold values from 0 to 7, each once
- frame_block: int32 [16], replicated, may hold values from 0 to 8, as said below
- embed_weight: bfloat16 [128, 3072], replicated, may hold values from -0.5 to 0.5
- pos_table: bfloat16 [8, 3072], replicated, may hold values from -3 to 3
- norm_gain: bfloat16 [3072], replicated, may hold values from 0.099609375 to 1.8984375
- qkv_weight: bfloat16 [3072, 3, 2048], P(None, None, ('mp', 'role')), may hold values from -0.109375 to 0.109375
- out_weight: bfloat16 [2048, 3072], P(('mp', 'role')), may hold values from -0.125 to 0.125
Outputs:
- disc_out: bfloat16 [128, 3072], P(('seq', 'mp', 'role'))
The draws below stay inside these ranges and needn't reach their ends.
Inputs may be any that keep to these rules, and one draw needn't show every extreme that they name: `patch_order`: each patch position appears in exactly one slot. `frame_block`: blocks are runs of consecutive frames with indices never falling, each of 1 to 4 frames, at least one of exactly 4; frames share a block iff their indices are equal.
All inputs are finite; a program needn't handle non-finite values.
Results may differ from the reference program's by a relative error of at most 0.006.
Values may be sent and summed in bfloat16 or wider, within the bound.
No kernel may reach another device: no remote copies, remote signals or barrier semaphores. Data moves between devices by JAX's collectives and lax.ppermute only.
A program may use at most 64 MiB of HBM per device.

```python
import jax
import jax.numpy as jnp
from jax import lax

D = 3072
HEADS = 16
HS = 128
P_SIZE = 128
MOSTB = 4
PATCHES = 8
FRAMES = 16
TOKENS = 128


def draw_frame_block(key, part):
    frame = jnp.arange(FRAMES, dtype=jnp.int32)
    pairs = (frame + 1) // 2
    quads = pairs // 2
    second = pairs % 2
    merged = jax.random.randint(jax.random.fold_in(key, 7), (FRAMES // 4 + 2,), 0, 2, dtype=jnp.int32)
    merged = merged.at[1].set(1)
    merged = merged.at[FRAMES // 4].set(0)
    joined = merged[quads]
    return (2 * quads + second * (1 - joined)).astype(jnp.int32)


def steps_of(key, shape, cuts, least, top_value):
    factor_of = 1.0
    for axis_at, blocks in cuts:
        draws = jax.random.uniform(jax.random.fold_in(jax.random.fold_in(key, 6), axis_at), (blocks,), jnp.float32, least / len(cuts), top_value / len(cuts))
        factor_of = factor_of * jnp.repeat(jnp.exp(draws), shape[axis_at] // blocks).reshape((-1,) + (1,) * (len(shape) - 1 - axis_at))
    return factor_of


def noise(key, shape, spread, bound, split=(), kind=jnp.bfloat16):
    loudness = steps_of(key, shape, split, -0.22, 0.18) if split else 1.0
    drawn = jax.random.normal(key, shape, jnp.float32) * spread * loudness
    return jnp.minimum(jnp.maximum(drawn, -bound), bound).astype(kind)


def setup_inputs(seed: int = 0) -> dict:
    splits = jax.random.split(jax.random.key(seed), 10)
    return {
        "gen_hidden": noise(splits[0], (PATCHES, FRAMES, D), 1.0, 6.0, ((0, 8), (2, 4))),
        "gen_out_weight": noise(splits[1], (D, P_SIZE), D ** -0.5, 0.109375, ((0, 4),)),
        "patch_order": jax.random.permutation(splits[2], PATCHES).astype(jnp.int32),
        "frame_block": draw_frame_block(jax.random.fold_in(splits[9], 71), 0),
        "embed_weight": noise(splits[4], (P_SIZE, D), P_SIZE ** -0.5, 0.5),
        "pos_table": noise(splits[5], (PATCHES, D), 0.5, 3.0),
        "norm_gain": jnp.clip(1.0 + 0.18 * jax.random.normal(splits[6], (D,), jnp.float32), 0.099609375, 1.8984375).astype(jnp.bfloat16),
        "qkv_weight": noise(splits[7], (D, 3, HEADS * HS), D ** -0.5, 0.109375, ((2, 4),)),
        "out_weight": noise(splits[8], (HEADS * HS, D), (HEADS * HS) ** -0.5, 0.125, ((0, 4),)),
    }


def frame_attention(query, keys, values, mask, head_size):
    tq = query.shape[0]
    scores = jnp.einsum('qhe,khe->hqk', query.astype(jnp.float32), keys.astype(jnp.float32)) / jnp.sqrt(jnp.float32(head_size))
    scores = jnp.where(mask[None], scores, jnp.float32(-1e+30))
    top = lax.optimization_barrier(jnp.max(scores, axis=-1, keepdims=True))
    expo = jnp.where(mask[None], jnp.exp(scores - top), jnp.float32(0.0))
    probs = (expo / lax.optimization_barrier(jnp.sum(expo, axis=-1, keepdims=True))).astype(jnp.bfloat16)
    mixed = jnp.einsum('hqk,khe->qhe', probs.astype(jnp.float32), values.astype(jnp.float32))
    return mixed.astype(jnp.bfloat16).reshape(tq, -1)

def reference(gen_hidden, gen_out_weight, patch_order, frame_block, embed_weight, pos_table, norm_gain, qkv_weight, out_weight):
    slot_latents = jnp.dot(gen_hidden.reshape(-1, D), gen_out_weight, preferred_element_type=jnp.float32)
    slot_latents = slot_latents.astype(jnp.bfloat16).reshape(PATCHES, FRAMES, P_SIZE)
    inverse = jnp.zeros((PATCHES,), jnp.int32).at[patch_order].set(jnp.arange(PATCHES, dtype=jnp.int32))
    latents = jnp.transpose(slot_latents[inverse], (1, 0, 2))
    embedded = jnp.dot(latents.reshape(-1, P_SIZE), embed_weight, preferred_element_type=jnp.float32).reshape(FRAMES, PATCHES, D)
    embedded = embedded + pos_table.astype(jnp.float32)[None]
    scale = lax.rsqrt(lax.optimization_barrier(jnp.mean(embedded * embedded, axis=-1, keepdims=True)) + 1e-06)
    normed = (embedded * scale * norm_gain.astype(jnp.float32)).astype(jnp.bfloat16)
    proj = jnp.dot(normed.reshape(-1, D), qkv_weight.reshape(D, 3 * HEADS * HS), preferred_element_type=jnp.float32)
    proj = proj.astype(jnp.bfloat16).reshape(FRAMES, PATCHES, 3, HEADS, HS)
    query = proj[:, :, 0]
    reach = MOSTB - 1
    width = 2 * reach + 1
    keys = jnp.pad(proj[:, :, 1], ((reach, reach), (0, 0), (0, 0), (0, 0)))
    values = jnp.pad(proj[:, :, 2], ((reach, reach), (0, 0), (0, 0), (0, 0)))
    blocks = jnp.pad(frame_block, (reach, reach), constant_values=-1)

    def one_frame(frame):
        start = frame.astype(jnp.int32)
        near_k = lax.dynamic_slice_in_dim(keys, start, width, 0).reshape(width * PATCHES, HEADS, HS)
        near_v = lax.dynamic_slice_in_dim(values, start, width, 0).reshape(width * PATCHES, HEADS, HS)
        near_b = lax.dynamic_slice_in_dim(blocks, start, width, 0)
        own_b = lax.dynamic_slice_in_dim(frame_block, start, 1, 0)
        frame_mask = jnp.repeat(near_b == own_b, PATCHES)
        mask = jnp.broadcast_to(frame_mask[None, :], (PATCHES, width * PATCHES))
        own_q = lax.dynamic_slice_in_dim(query, start, 1, 0)[0]
        return frame_attention(own_q, near_k, near_v, mask, HS)
    attn = lax.map(one_frame, jnp.arange(FRAMES, dtype=jnp.int32)).reshape(TOKENS, HEADS * HS)
    mixed = jnp.dot(attn, out_weight, preferred_element_type=jnp.float32)
    return (embedded.reshape(TOKENS, D) + mixed).astype(jnp.bfloat16)
```

```python
import functools

import jax
import jax.numpy as jnp
from jax import lax
from jax.experimental import pallas as pl
from jax.experimental.pallas import tpu as pltpu
from jax.sharding import PartitionSpec as P

HS = 128
MOSTB = 4
REACH = MOSTB - 1
GROUP = ("mp", "role")
EVERY = ("seq", "mp", "role")
CHUNK = 8
VMEM = pl.BlockSpec(memory_space=pltpu.VMEM)
SMEM = pl.BlockSpec(memory_space=pltpu.SMEM)


def dot(a, b):
    return jnp.dot(a, b, preferred_element_type=jnp.float32)


def latent_kernel(frame_dev, hidden_ref, weight_ref, out_ref, padded_ref):
    slots, frames, depth = hidden_ref.shape
    seqs, group, _, window, channels = out_ref.shape
    padded_ref[...] = jnp.zeros_like(padded_ref)
    for slot in range(slots):
        padded_ref[slot, REACH : REACH + frames] = dot(hidden_ref[slot], weight_ref[...])
    for to in range(seqs):
        piece = padded_ref[:, to * frame_dev : to * frame_dev + window]
        for member in range(group):
            out_ref[to, member] = piece


def weights_kernel(embed_ref, pos_ref, gain_ref, weight_ref, scaled_ref, offset_ref):
    channels = embed_ref.shape[0]
    gain = gain_ref[...].astype(jnp.float32)
    left = jnp.concatenate(
        [embed_ref[...].astype(jnp.float32) * gain, pos_ref[...].astype(jnp.float32) * gain], axis=0
    ).astype(jnp.bfloat16)
    both = dot(left, weight_ref[0])
    scaled = both[:channels]
    high = scaled.astype(jnp.bfloat16)
    scaled_ref[0, :channels] = high
    scaled_ref[0, channels:] = (scaled - high.astype(jnp.float32)).astype(jnp.bfloat16)
    offset_ref[0] = both[channels:]


def attend_kernel(
    frame_dev,
    order_ref,
    block_ref,
    partial_ref,
    embed_ref,
    pos_ref,
    scaled_ref,
    offset_ref,
    out_weight_ref,
    mixed_ref,
    mine_ref,
    latent_ref,
    scale_ref,
    own_ref,
):
    seqs, group, slots, window, channels = partial_ref.shape
    patches = seqs * slots
    rows = patches * window
    own_rows = frame_dev * patches
    model = embed_ref.shape[1]
    cols = out_weight_ref.shape[0]
    frames = block_ref.shape[0]
    device = lax.axis_index("seq")
    member = lax.axis_index(GROUP)

    def place(slot):
        total = partial_ref[slot // slots, 0, slot % slots]
        for other in range(1, group):
            total = total + partial_ref[slot // slots, other, slot % slots]
        latent_ref[order_ref[slot]] = total

    if patches <= 16:
        for slot in range(patches):
            place(slot)
    else:
        pl.loop(0, patches)(place)

    chunk = min(CHUNK, patches)

    def measure(step):
        start = step * chunk
        part = latent_ref[pl.ds(start, chunk)].reshape(chunk * window, channels)
        embedded = dot(part.astype(jnp.bfloat16), embed_ref[...]).reshape(chunk, window, model)
        embedded = embedded + pos_ref[pl.ds(start, chunk)].astype(jnp.float32)[:, None]
        mean = jnp.sum(embedded * embedded, axis=-1, keepdims=True) / model
        scale = jnp.broadcast_to(lax.rsqrt(mean + 1e-06), (chunk, window, channels))
        scale_ref[pl.ds(start, chunk)] = scale

    if chunk == patches:
        measure(0)
    else:
        pl.loop(0, patches // chunk)(measure)

    latents = latent_ref[...].reshape(rows, channels).astype(jnp.bfloat16)
    twice = jnp.concatenate([latents, latents], axis=1)
    scale = scale_ref[...].reshape(rows, channels)[:, :1]

    def project(index):
        flat = dot(twice, scaled_ref[index]).reshape(patches, window, cols)
        flat = (flat + offset_ref[index][:, None]).reshape(rows, cols)
        return (flat * scale).astype(jnp.bfloat16)

    key, value = project(1), project(2)

    own = jnp.concatenate(
        [latent_ref[:, REACH + frame, :] for frame in range(frame_dev)], axis=0
    ).astype(jnp.bfloat16)
    pos = pos_ref[...].astype(jnp.float32)
    own_embedded = dot(own, embed_ref[...]) + jnp.concatenate([pos] * frame_dev, axis=0)
    share = own_rows // group
    for other in range(group):
        own_ref[other] = own_embedded[other * share : (other + 1) * share]
    own_mean = jnp.sum(own_embedded * own_embedded, axis=-1, keepdims=True) / model
    own_scale = lax.rsqrt(own_mean + 1e-06)
    query = dot(jnp.concatenate([own, own], axis=1), scaled_ref[0])
    query = (query + jnp.concatenate([offset_ref[0]] * frame_dev, axis=0)) * own_scale
    query = query.astype(jnp.bfloat16)

    def block_of(frame):
        inside = jnp.logical_and(frame >= 0, frame < frames)
        return jnp.where(inside, block_ref[jnp.clip(frame, 0, frames - 1)], -1)

    row_frame = lax.broadcasted_iota(jnp.int32, (own_rows, rows), 0) // patches
    col_frame = lax.broadcasted_iota(jnp.int32, (own_rows, rows), 1) % window
    row_block = jnp.full((own_rows, rows), -2, jnp.int32)
    col_block = jnp.full((own_rows, rows), -1, jnp.int32)
    for frame in range(frame_dev):
        row_block = jnp.where(row_frame == frame, block_of(device * frame_dev + frame), row_block)
    for frame in range(window):
        col_block = jnp.where(
            col_frame == frame, block_of(device * frame_dev - REACH + frame), col_block
        )
    mask = row_block == col_block

    heads = []
    for head in range(cols // HS):
        at = slice(head * HS, (head + 1) * HS)
        scores = lax.dot_general(
            query[:, at], key[:, at], (((1,), (1,)), ((), ())), preferred_element_type=jnp.float32
        ) * (HS**-0.5)
        scores = jnp.where(mask, scores, -1e30)
        top = jnp.max(scores, axis=-1, keepdims=True)
        expo = jnp.where(mask, jnp.exp(scores - top), 0.0)
        probs = (expo / jnp.sum(expo, axis=-1, keepdims=True)).astype(jnp.bfloat16)
        heads.append(dot(probs, value[:, at]).astype(jnp.bfloat16))
    mixed = dot(jnp.concatenate(heads, axis=1), out_weight_ref[...])
    for other in range(group):
        mixed_ref[other] = mixed[other * share : (other + 1) * share].astype(jnp.bfloat16)
    mine_ref[...] = own_ref[member]


def sum_kernel(mine_ref, mixed_ref, out_ref):
    total = mine_ref[...]
    for member in range(mixed_ref.shape[0]):
        total = total + mixed_ref[member].astype(jnp.float32)
    out_ref[...] = total.astype(jnp.bfloat16)


def on_device(
    gen_hidden,
    gen_out_weight,
    patch_order,
    frame_block,
    embed_weight,
    pos_table,
    norm_gain,
    qkv_weight,
    out_weight,
):
    slots, frames, _ = gen_hidden.shape
    channels, model = embed_weight.shape
    cols = qkv_weight.shape[2]
    seqs = lax.axis_size("seq")
    group = lax.axis_size(GROUP)
    patches = seqs * slots
    frame_dev = frames // seqs
    window = frame_dev + 2 * REACH
    own_rows = frame_dev * patches
    share = own_rows // group
    big = pltpu.CompilerParams(vmem_limit_bytes=48 * 1024 * 1024)

    windows = pl.pallas_call(
        functools.partial(latent_kernel, frame_dev),
        out_shape=jax.ShapeDtypeStruct((seqs, group, slots, window, channels), jnp.float32),
        in_specs=[VMEM] * 2,
        out_specs=VMEM,
        scratch_shapes=[pltpu.VMEM((slots, frames + 2 * REACH, channels), jnp.float32)],
        compiler_params=big,
        name="partial_latents",
    )(gen_hidden, gen_out_weight)
    moved = lax.all_to_all(
        windows.reshape(seqs * group, slots, window, channels),
        EVERY,
        split_axis=0,
        concat_axis=0,
        tiled=True,
    ).reshape(seqs, group, slots, window, channels)

    width = cols // 2
    scaled, offset = pl.pallas_call(
        weights_kernel,
        grid=(3, cols // width),
        out_shape=(
            jax.ShapeDtypeStruct((3, 2 * channels, cols), jnp.bfloat16),
            jax.ShapeDtypeStruct((3, patches, cols), jnp.float32),
        ),
        in_specs=[
            pl.BlockSpec((channels, model), lambda i, j: (0, 0)),
            pl.BlockSpec((patches, model), lambda i, j: (0, 0)),
            pl.BlockSpec((1, model), lambda i, j: (0, 0)),
            pl.BlockSpec((1, model, width), lambda i, j: (i, 0, j)),
        ],
        out_specs=(
            pl.BlockSpec((1, 2 * channels, width), lambda i, j: (i, 0, j)),
            pl.BlockSpec((1, patches, width), lambda i, j: (i, 0, j)),
        ),
        compiler_params=pltpu.CompilerParams(vmem_limit_bytes=32 * 1024 * 1024),
        cost_estimate=pl.CostEstimate(
            flops=2 * (channels + patches) * model * 3 * cols,
            bytes_accessed=2 * model * 3 * cols,
            transcendentals=0,
        ),
        name="weight_products",
    )(embed_weight, pos_table, norm_gain.reshape(1, model), jnp.transpose(qkv_weight, (1, 0, 2)))

    mixed, mine = pl.pallas_call(
        functools.partial(attend_kernel, frame_dev),
        out_shape=(
            jax.ShapeDtypeStruct((group, share, model), jnp.bfloat16),
            jax.ShapeDtypeStruct((share, model), jnp.float32),
        ),
        in_specs=[SMEM] * 2 + [VMEM] * 6,
        out_specs=(VMEM, VMEM),
        scratch_shapes=[
            pltpu.VMEM((patches, window, channels), jnp.float32),
            pltpu.VMEM((patches, window, channels), jnp.float32),
            pltpu.VMEM((group, share, model), jnp.float32),
        ],
        compiler_params=big,
        name="attend",
    )(patch_order, frame_block, moved, embed_weight, pos_table, scaled, offset, out_weight)
    mixed = lax.all_to_all(mixed, GROUP, split_axis=0, concat_axis=0, tiled=True)
    return pl.pallas_call(
        sum_kernel,
        out_shape=jax.ShapeDtypeStruct((share, model), jnp.bfloat16),
        in_specs=[VMEM] * 2,
        out_specs=VMEM,
        name="final_sum",
    )(mine, mixed)


def solution(mesh):
    in_specs = (
        P("seq", None, ("mp", "role")),
        P(("mp", "role"), None),
        P(),
        P(),
        P(),
        P(),
        P(),
        P(None, None, ("mp", "role")),
        P(("mp", "role"), None),
    )
    out_specs = P(("seq", "mp", "role"), None)
    return jax.shard_map(
        on_device, mesh=mesh, in_specs=in_specs, out_specs=out_specs, check_vma=False
    )
```

```python
import functools

import jax
import jax.numpy as jnp
from jax import lax
from jax.experimental import pallas as pl
from jax.experimental.pallas import tpu as pltpu
from jax.sharding import PartitionSpec as P

HS = 128
MOSTB = 4
REACH = MOSTB - 1
GROUP = ("mp", "role")
EVERY = ("seq", "mp", "role")
LANES = 128
STEP_ROWS = 256
MIB = 1024 * 1024
VMEM = pl.BlockSpec(memory_space=pltpu.VMEM)
SMEM = pl.BlockSpec(memory_space=pltpu.SMEM)
HBM = pl.BlockSpec(memory_space=pltpu.HBM)


def dot(a, b):
    return jnp.dot(a, b, preferred_element_type=jnp.float32)


def latent_kernel(
    frame_dev, hidden_hbm, weight_hbm, out_ref, hidden_ref, weight_ref, padded_ref, sems
):
    copies = [
        pltpu.make_async_copy(hidden_hbm, hidden_ref, sems.at[0]),
        pltpu.make_async_copy(weight_hbm, weight_ref, sems.at[1]),
    ]
    for copy in copies:
        copy.start()
    slots, frames, depth = hidden_ref.shape
    seqs, group, _, window, channels = out_ref.shape
    padded_ref[...] = jnp.zeros_like(padded_ref)
    for copy in copies:
        copy.wait()
    for slot in range(slots):
        padded_ref[slot, REACH : REACH + frames] = dot(hidden_ref[slot], weight_ref[...])
    for to in range(seqs):
        piece = padded_ref[:, to * frame_dev : to * frame_dev + window]
        for member in range(group):
            out_ref[to, member] = piece


def attend_kernel(
    frame_dev,
    order_ref,
    block_ref,
    partial_ref,
    embed_ref,
    pos_ref,
    gain_ref,
    weight_ref,
    out_weight_ref,
    mixed_ref,
    mine_ref,
    latent_ref,
    embedded_ref,
    normed_ref,
    key_ref,
    value_ref,
    own_ref,
):
    seqs, group, slots, window, channels = partial_ref.shape
    patches = seqs * slots
    rows = patches * window
    own_rows = frame_dev * patches
    share = own_rows // group
    model = embed_ref.shape[1]
    cols = out_weight_ref.shape[0]
    frames = block_ref.shape[0]
    device = lax.axis_index("seq")
    member = lax.axis_index(GROUP)

    def place(slot):
        total = partial_ref[slot // slots, 0, slot % slots]
        for other in range(1, group):
            total = total + partial_ref[slot // slots, other, slot % slots]
        at = order_ref[slot]
        for frame in range(window):
            latent_ref[frame, pl.ds(at, 1), :] = total[frame : frame + 1]

    if patches <= 16:
        for slot in range(patches):
            place(slot)
    else:
        pl.loop(0, patches)(place)

    gain = jnp.concatenate(
        [gain_ref[at : at + 1, :].astype(jnp.float32) for at in range(model // LANES)], axis=1
    )
    pos = pos_ref[...].astype(jnp.float32)
    chunk = max(1, min(window, STEP_ROWS // patches))

    def project(step):
        start = step * chunk
        part = latent_ref[pl.ds(start, chunk)].reshape(chunk * patches, channels)
        embedded = dot(part.astype(jnp.bfloat16), embed_ref[...])
        embedded = embedded.reshape(chunk, patches, model) + pos[None]
        embedded_ref[pl.ds(start, chunk)] = embedded
        mean = jnp.sum(embedded * embedded, axis=-1, keepdims=True) / model
        normed = embedded * lax.rsqrt(mean + 1e-06) * gain[None]
        normed = normed.reshape(chunk * patches, model).astype(jnp.bfloat16)
        at = pl.ds(start * patches, chunk * patches)
        normed_ref[at] = normed
        key_ref[at] = dot(normed, weight_ref[1]).astype(jnp.bfloat16)
        value_ref[at] = dot(normed, weight_ref[2]).astype(jnp.bfloat16)

    if chunk == window:
        project(0)
    else:
        pl.loop(0, window // chunk)(project)

    query = dot(normed_ref[REACH * patches : REACH * patches + own_rows], weight_ref[0])
    query = query.astype(jnp.bfloat16)
    key, value = key_ref[...], value_ref[...]

    def block_of(frame):
        inside = jnp.logical_and(frame >= 0, frame < frames)
        return jnp.where(inside, block_ref[jnp.clip(frame, 0, frames - 1)], -1)

    row_frame = lax.broadcasted_iota(jnp.int32, (own_rows, rows), 0) // patches
    col_frame = lax.broadcasted_iota(jnp.int32, (own_rows, rows), 1) // patches
    row_block = jnp.full((own_rows, rows), -2, jnp.int32)
    col_block = jnp.full((own_rows, rows), -1, jnp.int32)
    for frame in range(frame_dev):
        row_block = jnp.where(row_frame == frame, block_of(device * frame_dev + frame), row_block)
    for frame in range(window):
        col_block = jnp.where(
            col_frame == frame, block_of(device * frame_dev - REACH + frame), col_block
        )
    mask = row_block == col_block

    heads = []
    for head in range(cols // HS):
        at = slice(head * HS, (head + 1) * HS)
        scores = lax.dot_general(
            query[:, at], key[:, at], (((1,), (1,)), ((), ())), preferred_element_type=jnp.float32
        ) * (HS**-0.5)
        scores = jnp.where(mask, scores, -1e30)
        top = jnp.max(scores, axis=-1, keepdims=True)
        expo = jnp.where(mask, jnp.exp(scores - top), 0.0)
        probs = (expo / jnp.sum(expo, axis=-1, keepdims=True)).astype(jnp.bfloat16)
        heads.append(dot(probs, value[:, at]).astype(jnp.bfloat16))
    mixed = dot(jnp.concatenate(heads, axis=1), out_weight_ref[...])
    own = embedded_ref[REACH : REACH + frame_dev].reshape(own_rows, model)
    for other in range(group):
        at = slice(other * share, (other + 1) * share)
        mixed_ref[other] = mixed[at].astype(jnp.bfloat16)
        own_ref[other] = own[at]
    mine_ref[...] = own_ref[member]


def sum_kernel(mine_ref, mixed_ref, out_ref):
    total = mine_ref[...]
    for member in range(mixed_ref.shape[0]):
        total = total + mixed_ref[member].astype(jnp.float32)
    out_ref[...] = total.astype(jnp.bfloat16)


def on_device(
    gen_hidden,
    gen_out_weight,
    patch_order,
    frame_block,
    embed_weight,
    pos_table,
    norm_gain,
    qkv_weight,
    out_weight,
):
    slots, frames, depth = gen_hidden.shape
    channels, model = embed_weight.shape
    cols = qkv_weight.shape[2]
    seqs = lax.axis_size("seq")
    group = lax.axis_size(GROUP)
    patches = seqs * slots
    frame_dev = frames // seqs
    window = frame_dev + 2 * REACH
    rows = window * patches
    own_rows = frame_dev * patches
    share = own_rows // group

    windows = pl.pallas_call(
        functools.partial(latent_kernel, frame_dev),
        out_shape=jax.ShapeDtypeStruct((seqs, group, slots, window, channels), jnp.float32),
        in_specs=[HBM] * 2,
        out_specs=VMEM,
        scratch_shapes=[
            pltpu.VMEM((slots, frames, depth), jnp.bfloat16),
            pltpu.VMEM((depth, channels), jnp.bfloat16),
            pltpu.VMEM((slots, frames + 2 * REACH, channels), jnp.float32),
            pltpu.SemaphoreType.DMA((2,)),
        ],
        compiler_params=pltpu.CompilerParams(vmem_limit_bytes=12 * MIB),
        cost_estimate=pl.CostEstimate(
            flops=20_000_000_000, bytes_accessed=40_000_000, transcendentals=0
        ),
        name="partial_latents",
    )(gen_hidden, gen_out_weight)
    moved = lax.all_to_all(
        windows.reshape(seqs * group, slots, window, channels),
        EVERY,
        split_axis=0,
        concat_axis=0,
        tiled=True,
    ).reshape(seqs, group, slots, window, channels)

    mixed, mine = pl.pallas_call(
        functools.partial(attend_kernel, frame_dev),
        out_shape=(
            jax.ShapeDtypeStruct((group, share, model), jnp.bfloat16),
            jax.ShapeDtypeStruct((share, model), jnp.float32),
        ),
        in_specs=[SMEM] * 2 + [VMEM] * 6,
        out_specs=(VMEM, VMEM),
        scratch_shapes=[
            pltpu.VMEM((window, patches, channels), jnp.float32),
            pltpu.VMEM((window, patches, model), jnp.float32),
            pltpu.VMEM((rows, model), jnp.bfloat16),
            pltpu.VMEM((rows, cols), jnp.bfloat16),
            pltpu.VMEM((rows, cols), jnp.bfloat16),
            pltpu.VMEM((group, share, model), jnp.float32),
        ],
        compiler_params=pltpu.CompilerParams(
            vmem_limit_bytes=(24 if rows <= STEP_ROWS else 56) * MIB
        ),
        name="attend",
    )(
        patch_order,
        frame_block,
        moved,
        embed_weight,
        pos_table,
        norm_gain.reshape(model // LANES, LANES),
        jnp.transpose(qkv_weight, (1, 0, 2)),
        out_weight,
    )
    mixed = lax.all_to_all(mixed, GROUP, split_axis=0, concat_axis=0, tiled=True)
    return pl.pallas_call(
        sum_kernel,
        out_shape=jax.ShapeDtypeStruct((share, model), jnp.bfloat16),
        in_specs=[VMEM] * 2,
        out_specs=VMEM,
        compiler_params=pltpu.CompilerParams(vmem_limit_bytes=8 * MIB),
        name="final_sum",
    )(mine, mixed)


def solution(mesh):
    in_specs = (
        P("seq", None, ("mp", "role")),
        P(("mp", "role"), None),
        P(),
        P(),
        P(),
        P(),
        P(),
        P(None, None, ("mp", "role")),
        P(("mp", "role"), None),
    )
    out_specs = P(("seq", "mp", "role"), None)
    return jax.shard_map(
        on_device, mesh=mesh, in_specs=in_specs, out_specs=out_specs, check_vma=False
    )
```

```python
import functools

import jax
import jax.numpy as jnp
from jax import lax
from jax.experimental import pallas as pl
from jax.experimental.pallas import tpu as pltpu
from jax.sharding import PartitionSpec as P

HS = 128
MOSTB = 4
REACH = MOSTB - 1
GROUP = ("mp", "role")
EVERY = ("seq", "mp", "role")
LANES = 128
STEP_ROWS = 256
MIB = 1024 * 1024
VMEM = pl.BlockSpec(memory_space=pltpu.VMEM)
SMEM = pl.BlockSpec(memory_space=pltpu.SMEM)
HBM = pl.BlockSpec(memory_space=pltpu.HBM)


def dot(a, b):
    return jnp.dot(a, b, preferred_element_type=jnp.float32)


def latent_kernel(
    frame_dev, hidden_hbm, weight_hbm, out_ref, hidden_ref, weight_ref, padded_ref, sems
):
    copies = [
        pltpu.make_async_copy(hidden_hbm, hidden_ref, sems.at[0]),
        pltpu.make_async_copy(weight_hbm, weight_ref, sems.at[1]),
    ]
    for copy in copies:
        copy.start()
    slots, frames, depth = hidden_ref.shape
    seqs, group, _, window, channels = out_ref.shape
    padded_ref[...] = jnp.zeros_like(padded_ref)
    for copy in copies:
        copy.wait()
    for slot in range(slots):
        padded_ref[slot, REACH : REACH + frames] = dot(hidden_ref[slot], weight_ref[...])
    for to in range(seqs):
        piece = padded_ref[:, to * frame_dev : to * frame_dev + window]
        for member in range(group):
            out_ref[to, member] = piece.astype(out_ref.dtype)


def attend_kernel(
    frame_dev,
    order_ref,
    block_ref,
    partial_ref,
    embed_ref,
    pos_ref,
    gain_ref,
    weight_ref,
    out_weight_ref,
    mixed_ref,
    mine_ref,
    latent_ref,
    embedded_ref,
    normed_ref,
    key_ref,
    value_ref,
    own_ref,
):
    seqs, group, slots, window, channels = partial_ref.shape
    patches = seqs * slots
    rows = patches * window
    own_rows = frame_dev * patches
    share = own_rows // group
    model = embed_ref.shape[1]
    cols = out_weight_ref.shape[0]
    frames = block_ref.shape[0]
    device = lax.axis_index("seq")
    member = lax.axis_index(GROUP)

    def place(slot):
        total = partial_ref[slot // slots, 0, slot % slots].astype(jnp.float32)
        for other in range(1, group):
            total = total + partial_ref[slot // slots, other, slot % slots].astype(jnp.float32)
        at = order_ref[slot]
        for frame in range(window):
            latent_ref[frame, pl.ds(at, 1), :] = total[frame : frame + 1]

    if patches <= 16:
        for slot in range(patches):
            place(slot)
    else:
        pl.loop(0, patches)(place)

    gain = jnp.concatenate(
        [gain_ref[at : at + 1, :].astype(jnp.float32) for at in range(model // LANES)], axis=1
    )
    pos = pos_ref[...].astype(jnp.float32)
    chunk = max(1, min(window, STEP_ROWS // patches))

    def project(step):
        start = step * chunk
        part = latent_ref[pl.ds(start, chunk)].reshape(chunk * patches, channels)
        embedded = dot(part.astype(jnp.bfloat16), embed_ref[...])
        embedded = embedded.reshape(chunk, patches, model) + pos[None]
        embedded_ref[pl.ds(start, chunk)] = embedded
        mean = jnp.sum(embedded * embedded, axis=-1, keepdims=True) / model
        normed = embedded * lax.rsqrt(mean + 1e-06) * gain[None]
        normed = normed.reshape(chunk * patches, model).astype(jnp.bfloat16)
        at = pl.ds(start * patches, chunk * patches)
        normed_ref[at] = normed
        key_ref[at] = dot(normed, weight_ref[1]).astype(jnp.bfloat16)
        value_ref[at] = dot(normed, weight_ref[2]).astype(jnp.bfloat16)

    if chunk == window:
        project(0)
    else:
        pl.loop(0, window // chunk)(project)

    query = dot(normed_ref[REACH * patches : REACH * patches + own_rows], weight_ref[0])
    query = query.astype(jnp.bfloat16)
    key, value = key_ref[...], value_ref[...]

    def block_of(frame):
        inside = jnp.logical_and(frame >= 0, frame < frames)
        return jnp.where(inside, block_ref[jnp.clip(frame, 0, frames - 1)], -1)

    row_frame = lax.broadcasted_iota(jnp.int32, (own_rows, rows), 0) // patches
    col_frame = lax.broadcasted_iota(jnp.int32, (own_rows, rows), 1) // patches
    row_block = jnp.full((own_rows, rows), -2, jnp.int32)
    col_block = jnp.full((own_rows, rows), -1, jnp.int32)
    for frame in range(frame_dev):
        row_block = jnp.where(row_frame == frame, block_of(device * frame_dev + frame), row_block)
    for frame in range(window):
        col_block = jnp.where(
            col_frame == frame, block_of(device * frame_dev - REACH + frame), col_block
        )
    mask = row_block == col_block

    heads = []
    for head in range(cols // HS):
        at = slice(head * HS, (head + 1) * HS)
        scores = lax.dot_general(
            query[:, at], key[:, at], (((1,), (1,)), ((), ())), preferred_element_type=jnp.float32
        ) * (HS**-0.5)
        scores = jnp.where(mask, scores, -1e30)
        top = jnp.max(scores, axis=-1, keepdims=True)
        expo = jnp.where(mask, jnp.exp(scores - top), 0.0)
        probs = (expo / jnp.sum(expo, axis=-1, keepdims=True)).astype(jnp.bfloat16)
        heads.append(dot(probs, value[:, at]).astype(jnp.bfloat16))
    mixed = dot(jnp.concatenate(heads, axis=1), out_weight_ref[...])
    own = embedded_ref[REACH : REACH + frame_dev].reshape(own_rows, model)
    for other in range(group):
        at = slice(other * share, (other + 1) * share)
        mixed_ref[other] = mixed[at].astype(jnp.bfloat16)
        own_ref[other] = own[at]
    mine_ref[...] = own_ref[member]


def sum_kernel(mine_ref, mixed_ref, out_ref):
    total = mine_ref[...]
    for member in range(mixed_ref.shape[0]):
        total = total + mixed_ref[member].astype(jnp.float32)
    out_ref[...] = total.astype(jnp.bfloat16)


def on_device(
    gen_hidden,
    gen_out_weight,
    patch_order,
    frame_block,
    embed_weight,
    pos_table,
    norm_gain,
    qkv_weight,
    out_weight,
):
    slots, frames, depth = gen_hidden.shape
    channels, model = embed_weight.shape
    cols = qkv_weight.shape[2]
    seqs = lax.axis_size("seq")
    group = lax.axis_size(GROUP)
    patches = seqs * slots
    frame_dev = frames // seqs
    window = frame_dev + 2 * REACH
    rows = window * patches
    own_rows = frame_dev * patches
    share = own_rows // group

    windows = pl.pallas_call(
        functools.partial(latent_kernel, frame_dev),
        out_shape=jax.ShapeDtypeStruct((seqs, group, slots, window, channels), jnp.bfloat16),
        in_specs=[HBM] * 2,
        out_specs=VMEM,
        scratch_shapes=[
            pltpu.VMEM((slots, frames, depth), jnp.bfloat16),
            pltpu.VMEM((depth, channels), jnp.bfloat16),
            pltpu.VMEM((slots, frames + 2 * REACH, channels), jnp.float32),
            pltpu.SemaphoreType.DMA((2,)),
        ],
        compiler_params=pltpu.CompilerParams(vmem_limit_bytes=12 * MIB),
        cost_estimate=pl.CostEstimate(
            flops=20_000_000_000, bytes_accessed=40_000_000, transcendentals=0
        ),
        name="partial_latents",
    )(
        pltpu.with_memory_space_constraint(gen_hidden, pltpu.HBM),
        pltpu.with_memory_space_constraint(gen_out_weight, pltpu.HBM),
    )
    moved = lax.all_to_all(
        windows.reshape(seqs * group, slots, window, channels),
        EVERY,
        split_axis=0,
        concat_axis=0,
        tiled=True,
    ).reshape(seqs, group, slots, window, channels)

    mixed, mine = pl.pallas_call(
        functools.partial(attend_kernel, frame_dev),
        out_shape=(
            jax.ShapeDtypeStruct((group, share, model), jnp.bfloat16),
            jax.ShapeDtypeStruct((share, model), jnp.float32),
        ),
        in_specs=[SMEM] * 2 + [VMEM] * 6,
        out_specs=(VMEM, VMEM),
        scratch_shapes=[
            pltpu.VMEM((window, patches, channels), jnp.float32),
            pltpu.VMEM((window, patches, model), jnp.float32),
            pltpu.VMEM((rows, model), jnp.bfloat16),
            pltpu.VMEM((rows, cols), jnp.bfloat16),
            pltpu.VMEM((rows, cols), jnp.bfloat16),
            pltpu.VMEM((group, share, model), jnp.float32),
        ],
        compiler_params=pltpu.CompilerParams(
            vmem_limit_bytes=(24 if rows <= STEP_ROWS else 56) * MIB
        ),
        name="attend",
    )(
        patch_order,
        frame_block,
        moved,
        embed_weight,
        pos_table,
        norm_gain.reshape(model // LANES, LANES),
        jnp.transpose(qkv_weight, (1, 0, 2)),
        out_weight,
    )
    mixed = lax.all_to_all(mixed, GROUP, split_axis=0, concat_axis=0, tiled=True)
    return pl.pallas_call(
        sum_kernel,
        out_shape=jax.ShapeDtypeStruct((share, model), jnp.bfloat16),
        in_specs=[VMEM] * 2,
        out_specs=VMEM,
        compiler_params=pltpu.CompilerParams(vmem_limit_bytes=8 * MIB),
        name="final_sum",
    )(mine, mixed)


def solution(mesh):
    in_specs = (
        P("seq", None, ("mp", "role")),
        P(("mp", "role"), None),
        P(),
        P(),
        P(),
        P(),
        P(),
        P(None, None, ("mp", "role")),
        P(("mp", "role"), None),
    )
    out_specs = P(("seq", "mp", "role"), None)
    return jax.shard_map(
        on_device, mesh=mesh, in_specs=in_specs, out_specs=out_specs, check_vma=False
    )
```

```python
import functools

import jax
import jax.numpy as jnp
from jax import lax
from jax.experimental import pallas as pl
from jax.experimental.pallas import tpu as pltpu
from jax.sharding import PartitionSpec as P

HS = 128
MOSTB = 4
REACH = MOSTB - 1
GROUP = ("mp", "role")
EVERY = ("seq", "mp", "role")
LANES = 128
STEP_ROWS = 256
MIB = 1024 * 1024
VMEM = pl.BlockSpec(memory_space=pltpu.VMEM)
SMEM = pl.BlockSpec(memory_space=pltpu.SMEM)
HBM = pl.BlockSpec(memory_space=pltpu.HBM)


def dot(a, b):
    return jnp.dot(a, b, preferred_element_type=jnp.float32)


def latent_kernel(
    frame_dev, hidden_hbm, weight_hbm, out_ref, hidden_ref, weight_ref, padded_ref, sems
):
    copies = [
        pltpu.make_async_copy(hidden_hbm, hidden_ref, sems.at[0]),
        pltpu.make_async_copy(weight_hbm, weight_ref, sems.at[1]),
    ]
    for copy in copies:
        copy.start()
    slots, frames, depth = hidden_ref.shape
    seqs, group, _, window, channels = out_ref.shape
    padded_ref[...] = jnp.zeros_like(padded_ref)
    for copy in copies:
        copy.wait()
    for slot in range(slots):
        padded_ref[slot, REACH : REACH + frames] = dot(hidden_ref[slot], weight_ref[...])
    for to in range(seqs):
        piece = padded_ref[:, to * frame_dev : to * frame_dev + window]
        for member in range(group):
            out_ref[to, member] = piece.astype(out_ref.dtype)


def weights_kernel(
    frame_dev,
    window,
    order_ref,
    block_ref,
    embed_ref,
    pos_ref,
    gain_ref,
    weight_ref,
    scaled_ref,
    offset_ref,
    pos_slot_ref,
    pos_mine_ref,
    select_ref,
    select_mine_ref,
    bias_ref,
    natural_ref,
    pos_all_ref,
):
    channels, model = embed_ref.shape
    patches = pos_ref.shape[0]
    frames = block_ref.shape[0]
    own_rows, rows = bias_ref.shape
    share = select_mine_ref.shape[0]
    device = lax.axis_index("seq")
    member = lax.axis_index(GROUP)

    gain = jnp.concatenate(
        [gain_ref[at : at + 1, :].astype(jnp.float32) for at in range(model // LANES)], axis=1
    )
    pos = pos_ref[...].astype(jnp.float32)
    left = jnp.concatenate([embed_ref[...].astype(jnp.float32) * gain, pos * gain], axis=0)
    left = left.astype(jnp.bfloat16)
    for index in range(3):
        both = dot(left, weight_ref[index])
        scaled = both[:channels]
        high = scaled.astype(jnp.bfloat16)
        scaled_ref[index, :channels] = high
        scaled_ref[index, channels:] = (scaled - high.astype(jnp.float32)).astype(jnp.bfloat16)
        natural_ref[index] = both[channels:]
    pos_all_ref[...] = pos

    def place(slot):
        at = pl.ds(order_ref[slot], 1)
        pos_slot_ref[pl.ds(slot, 1), :] = pos_all_ref[at, :]
        for index in range(3):
            offset_ref[index, pl.ds(slot, 1), :] = natural_ref[index, at, :]

    if patches <= 16:
        for slot in range(patches):
            place(slot)
    else:
        pl.loop(0, patches)(place)

    column = lax.broadcasted_iota(jnp.int32, (1, rows), 1)
    column_slot, column_frame = column // window, column % window

    def patch_at(slot, found):
        return jnp.where(column_slot == slot, order_ref[slot], found)

    column_patch = jnp.zeros((1, rows), jnp.int32)
    if patches <= 16:
        for slot in range(patches):
            column_patch = patch_at(slot, column_patch)
    else:
        column_patch = lax.fori_loop(0, patches, patch_at, column_patch)

    def select(count, first):
        row = lax.broadcasted_iota(jnp.int32, (count, rows), 0) + first
        hit = jnp.logical_and(
            column_patch == row % patches, column_frame == row // patches + REACH
        )
        return jnp.where(hit, 1.0, 0.0).astype(jnp.bfloat16)

    select_ref[...] = select(own_rows, 0)
    select_mine_ref[...] = select(share, member * share)
    for frame in range(frame_dev * patches // share):
        row = frame * share

        @pl.when(member == frame)
        def _():
            for at in range(share):
                mine = (row + at) % patches
                pos_mine_ref[at : at + 1, :] = pos_all_ref[mine : mine + 1, :]

    def block_of(frame):
        inside = jnp.logical_and(frame >= 0, frame < frames)
        return jnp.where(inside, block_ref[jnp.clip(frame, 0, frames - 1)], -1)

    column_block = jnp.full((1, rows), -1, jnp.int32)
    for frame in range(window):
        found = block_of(device * frame_dev - REACH + frame)
        column_block = jnp.where(column_frame == frame, found, column_block)
    row_frame = lax.broadcasted_iota(jnp.int32, (own_rows, rows), 0) // patches
    row_block = jnp.full((own_rows, rows), -2, jnp.int32)
    for frame in range(frame_dev):
        row_block = jnp.where(row_frame == frame, block_of(device * frame_dev + frame), row_block)
    bias_ref[...] = jnp.where(row_block == column_block, 0.0, -1e30)


def attend_kernel(
    partial_ref,
    embed_ref,
    scaled_ref,
    offset_ref,
    pos_slot_ref,
    pos_mine_ref,
    select_ref,
    select_mine_ref,
    bias_ref,
    out_weight_ref,
    mixed_ref,
    mine_ref,
    latent_ref,
    scale_ref,
):
    seqs, group, slots, window, channels = partial_ref.shape
    patches = seqs * slots
    rows = patches * window
    share, model = mine_ref.shape
    cols = out_weight_ref.shape[0]

    total = partial_ref[:, 0].astype(jnp.float32)
    for other in range(1, group):
        total = total + partial_ref[:, other].astype(jnp.float32)
    latent_ref[...] = total.reshape(patches, window, channels)
    chunk = min(patches, STEP_ROWS // window)

    def measure(step):
        at = pl.ds(step * chunk, chunk)
        part = latent_ref[at].reshape(chunk * window, channels).astype(jnp.bfloat16)
        embedded = dot(part, embed_ref[...]).reshape(chunk, window, model)
        embedded = embedded + pos_slot_ref[at][:, None]
        mean = jnp.sum(embedded * embedded, axis=-1, keepdims=True) / model
        scale_ref[at] = jnp.broadcast_to(lax.rsqrt(mean + 1e-06), (chunk, window, LANES))

    if chunk == patches:
        measure(0)
    else:
        pl.loop(0, patches // chunk)(measure)

    latents = latent_ref[...].reshape(rows, channels).astype(jnp.bfloat16)
    twice = jnp.concatenate([latents, latents], axis=1)
    scale = scale_ref[...].reshape(rows, LANES)[:, :1]

    def project(index):
        flat = dot(twice, scaled_ref[index]).reshape(patches, window, cols)
        flat = (flat + offset_ref[index][:, None]).reshape(rows, cols)
        return (flat * scale).astype(jnp.bfloat16)

    query = dot(select_ref[...], project(0)).astype(jnp.bfloat16)
    key, value = project(1), project(2)
    bias = bias_ref[...]
    heads = []
    for head in range(cols // HS):
        at = slice(head * HS, (head + 1) * HS)
        scores = lax.dot_general(
            query[:, at], key[:, at], (((1,), (1,)), ((), ())), preferred_element_type=jnp.float32
        )
        scores = scores * (HS**-0.5) + bias
        expo = jnp.exp(scores - jnp.max(scores, axis=-1, keepdims=True))
        probs = (expo / jnp.sum(expo, axis=-1, keepdims=True)).astype(jnp.bfloat16)
        heads.append(dot(probs, value[:, at]).astype(jnp.bfloat16))
    mixed = dot(jnp.concatenate(heads, axis=1), out_weight_ref[...])
    for other in range(group):
        mixed_ref[other] = mixed[other * share : (other + 1) * share].astype(jnp.bfloat16)
    mine = dot(select_mine_ref[...], latents).astype(jnp.bfloat16)
    mine_ref[...] = dot(mine, embed_ref[...]) + pos_mine_ref[...]


def sum_kernel(mine_ref, mixed_ref, out_ref):
    total = mine_ref[...]
    for member in range(mixed_ref.shape[0]):
        total = total + mixed_ref[member].astype(jnp.float32)
    out_ref[...] = total.astype(jnp.bfloat16)


def on_device(
    gen_hidden,
    gen_out_weight,
    patch_order,
    frame_block,
    embed_weight,
    pos_table,
    norm_gain,
    qkv_weight,
    out_weight,
):
    slots, frames, depth = gen_hidden.shape
    channels, model = embed_weight.shape
    cols = qkv_weight.shape[2]
    seqs = lax.axis_size("seq")
    group = lax.axis_size(GROUP)
    patches = seqs * slots
    frame_dev = frames // seqs
    window = frame_dev + 2 * REACH
    rows = window * patches
    own_rows = frame_dev * patches
    share = own_rows // group
    f32, bf16 = jnp.float32, jnp.bfloat16
    array = jax.ShapeDtypeStruct
    grant = (16 if rows <= STEP_ROWS else 40) * MIB

    windows = pl.pallas_call(
        functools.partial(latent_kernel, frame_dev),
        out_shape=array((seqs, group, slots, window, channels), bf16),
        in_specs=[HBM] * 2,
        out_specs=VMEM,
        scratch_shapes=[
            pltpu.VMEM((slots, frames, depth), bf16),
            pltpu.VMEM((depth, channels), bf16),
            pltpu.VMEM((slots, frames + 2 * REACH, channels), f32),
            pltpu.SemaphoreType.DMA((2,)),
        ],
        compiler_params=pltpu.CompilerParams(vmem_limit_bytes=12 * MIB),
        cost_estimate=pl.CostEstimate(
            flops=20_000_000_000, bytes_accessed=40_000_000, transcendentals=0
        ),
        name="partial_latents",
    )(
        pltpu.with_memory_space_constraint(gen_hidden, pltpu.HBM),
        pltpu.with_memory_space_constraint(gen_out_weight, pltpu.HBM),
    )
    moved = lax.all_to_all(
        windows.reshape(seqs * group, slots, window, channels),
        EVERY,
        split_axis=0,
        concat_axis=0,
        tiled=True,
    ).reshape(seqs, group, slots, window, channels)

    products = pl.pallas_call(
        functools.partial(weights_kernel, frame_dev, window),
        out_shape=(
            array((3, 2 * channels, cols), bf16),
            array((3, patches, cols), f32),
            array((patches, model), f32),
            array((share, model), f32),
            array((own_rows, rows), bf16),
            array((share, rows), bf16),
            array((own_rows, rows), f32),
        ),
        in_specs=[SMEM] * 2 + [VMEM] * 4,
        out_specs=(VMEM,) * 7,
        scratch_shapes=[pltpu.VMEM((3, patches, cols), f32), pltpu.VMEM((patches, model), f32)],
        compiler_params=pltpu.CompilerParams(vmem_limit_bytes=24 * MIB),
        cost_estimate=pl.CostEstimate(
            flops=2 * (channels + patches) * model * 3 * cols,
            bytes_accessed=2 * model * 3 * cols,
            transcendentals=0,
        ),
        name="weight_products",
    )(
        patch_order,
        frame_block,
        embed_weight,
        pos_table,
        norm_gain.reshape(model // LANES, LANES),
        jnp.transpose(qkv_weight, (1, 0, 2)),
    )

    mixed, mine = pl.pallas_call(
        attend_kernel,
        out_shape=(array((group, share, model), bf16), array((share, model), f32)),
        in_specs=[VMEM] * 10,
        out_specs=(VMEM, VMEM),
        scratch_shapes=[
            pltpu.VMEM((patches, window, channels), f32),
            pltpu.VMEM((patches, window, LANES), f32),
        ],
        compiler_params=pltpu.CompilerParams(vmem_limit_bytes=grant),
        name="attend",
    )(moved, embed_weight, *products, out_weight)
    mixed = lax.all_to_all(mixed, GROUP, split_axis=0, concat_axis=0, tiled=True)
    return pl.pallas_call(
        sum_kernel,
        out_shape=array((share, model), bf16),
        in_specs=[VMEM] * 2,
        out_specs=VMEM,
        compiler_params=pltpu.CompilerParams(vmem_limit_bytes=8 * MIB),
        name="final_sum",
    )(mine, mixed)


def solution(mesh):
    in_specs = (
        P("seq", None, ("mp", "role")),
        P(("mp", "role"), None),
        P(),
        P(),
        P(),
        P(),
        P(),
        P(None, None, ("mp", "role")),
        P(("mp", "role"), None),
    )
    out_specs = P(("seq", "mp", "role"), None)
    return jax.shard_map(
        on_device, mesh=mesh, in_specs=in_specs, out_specs=out_specs, check_vma=False
    )
```

```python
import functools

import jax
import jax.numpy as jnp
from jax import lax
from jax.experimental import pallas as pl
from jax.experimental.pallas import tpu as pltpu
from jax.sharding import PartitionSpec as P

HS = 128
MOSTB = 4
REACH = MOSTB - 1
GROUP = ("mp", "role")
EVERY = ("seq", "mp", "role")
LANES = 128
STEP_ROWS = 256
WIDTH = 256
AHEAD = 3
MIB = 1024 * 1024
VMEM = pl.BlockSpec(memory_space=pltpu.VMEM)
SMEM = pl.BlockSpec(memory_space=pltpu.SMEM)
HBM = pl.BlockSpec(memory_space=pltpu.HBM)


def dot(a, b):
    return jnp.dot(a, b, preferred_element_type=jnp.float32)


def latent_kernel(
    frame_dev, hidden_hbm, weight_hbm, out_ref, hidden_ref, weight_ref, padded_ref, sems
):
    copies = [
        pltpu.make_async_copy(hidden_hbm, hidden_ref, sems.at[0]),
        pltpu.make_async_copy(weight_hbm, weight_ref, sems.at[1]),
    ]
    for copy in copies:
        copy.start()
    slots, frames, depth = hidden_ref.shape
    seqs, group, _, window, channels = out_ref.shape
    padded_ref[...] = jnp.zeros_like(padded_ref)
    for copy in copies:
        copy.wait()
    for slot in range(slots):
        padded_ref[slot, REACH : REACH + frames] = dot(hidden_ref[slot], weight_ref[...])
    for to in range(seqs):
        piece = padded_ref[:, to * frame_dev : to * frame_dev + window]
        for member in range(group):
            out_ref[to, member] = piece.astype(out_ref.dtype)


def weights_kernel(
    frame_dev,
    window,
    order_ref,
    block_ref,
    embed_ref,
    pos_ref,
    gain_ref,
    weight_hbm,
    scaled_ref,
    offset_ref,
    pos_slot_ref,
    pos_mine_ref,
    select_ref,
    select_mine_ref,
    bias_ref,
    natural_ref,
    pos_all_ref,
    weight_ref,
    sems,
):
    channels, model = embed_ref.shape
    patches = pos_ref.shape[0]
    frames = block_ref.shape[0]
    own_rows, rows = bias_ref.shape
    share = select_mine_ref.shape[0]
    device = lax.axis_index("seq")
    member = lax.axis_index(GROUP)

    cols = weight_ref.shape[2]
    width = min(cols, WIDTH)
    parts = [(index, at) for index in range(3) for at in range(0, cols, width)]

    def arrival(part):
        index, at = parts[part]
        place = (index, slice(None), pl.ds(at, width))
        return pltpu.make_async_copy(weight_hbm.at[place], weight_ref.at[place], sems.at[part])

    for part in range(AHEAD):
        arrival(part).start()

    gain = jnp.concatenate(
        [gain_ref[at : at + 1, :].astype(jnp.float32) for at in range(model // LANES)], axis=1
    )
    pos = pos_ref[...].astype(jnp.float32)
    left = jnp.concatenate([embed_ref[...].astype(jnp.float32) * gain, pos * gain], axis=0)
    left = left.astype(jnp.bfloat16)
    for part, (index, at) in enumerate(parts):
        arrival(part).wait()
        if part + AHEAD < len(parts):
            arrival(part + AHEAD).start()
        here = slice(at, at + width)
        both = dot(left, weight_ref[index, :, here])
        scaled = both[:channels]
        high = scaled.astype(jnp.bfloat16)
        scaled_ref[index, :channels, here] = high
        scaled_ref[index, channels:, here] = (scaled - high.astype(jnp.float32)).astype(jnp.bfloat16)
        natural_ref[index, :, here] = both[channels:]
    pos_all_ref[...] = pos

    def place(slot):
        at = pl.ds(order_ref[slot], 1)
        pos_slot_ref[pl.ds(slot, 1), :] = pos_all_ref[at, :]
        for index in range(3):
            offset_ref[index, pl.ds(slot, 1), :] = natural_ref[index, at, :]

    if patches <= 16:
        for slot in range(patches):
            place(slot)
    else:
        pl.loop(0, patches)(place)

    column = lax.broadcasted_iota(jnp.int32, (1, rows), 1)
    column_slot, column_frame = column // window, column % window

    def patch_at(slot, found):
        return jnp.where(column_slot == slot, order_ref[slot], found)

    column_patch = jnp.zeros((1, rows), jnp.int32)
    if patches <= 16:
        for slot in range(patches):
            column_patch = patch_at(slot, column_patch)
    else:
        column_patch = lax.fori_loop(0, patches, patch_at, column_patch)

    def select(count, first):
        row = lax.broadcasted_iota(jnp.int32, (count, rows), 0) + first
        hit = jnp.logical_and(
            column_patch == row % patches, column_frame == row // patches + REACH
        )
        return jnp.where(hit, 1.0, 0.0).astype(jnp.bfloat16)

    select_ref[...] = select(own_rows, 0)
    select_mine_ref[...] = select(share, member * share)
    for frame in range(frame_dev * patches // share):
        row = frame * share

        @pl.when(member == frame)
        def _():
            for at in range(share):
                mine = (row + at) % patches
                pos_mine_ref[at : at + 1, :] = pos_all_ref[mine : mine + 1, :]

    def block_of(frame):
        inside = jnp.logical_and(frame >= 0, frame < frames)
        return jnp.where(inside, block_ref[jnp.clip(frame, 0, frames - 1)], -1)

    column_block = jnp.full((1, rows), -1, jnp.int32)
    for frame in range(window):
        found = block_of(device * frame_dev - REACH + frame)
        column_block = jnp.where(column_frame == frame, found, column_block)
    row_frame = lax.broadcasted_iota(jnp.int32, (own_rows, rows), 0) // patches
    row_block = jnp.full((own_rows, rows), -2, jnp.int32)
    for frame in range(frame_dev):
        row_block = jnp.where(row_frame == frame, block_of(device * frame_dev + frame), row_block)
    bias_ref[...] = jnp.where(row_block == column_block, 0.0, -1e30)


def attend_kernel(
    partial_ref,
    embed_ref,
    scaled_ref,
    offset_ref,
    pos_slot_ref,
    pos_mine_ref,
    select_ref,
    select_mine_ref,
    bias_ref,
    out_weight_hbm,
    mixed_ref,
    mine_ref,
    latent_ref,
    scale_ref,
    out_weight_ref,
    sem,
):
    arrival = pltpu.make_async_copy(out_weight_hbm, out_weight_ref, sem)
    arrival.start()
    seqs, group, slots, window, channels = partial_ref.shape
    patches = seqs * slots
    rows = patches * window
    share, model = mine_ref.shape
    cols = out_weight_ref.shape[0]

    total = partial_ref[:, 0].astype(jnp.float32)
    for other in range(1, group):
        total = total + partial_ref[:, other].astype(jnp.float32)
    latent_ref[...] = total.reshape(patches, window, channels)
    chunk = min(patches, STEP_ROWS // window)

    def measure(step):
        at = pl.ds(step * chunk, chunk)
        part = latent_ref[at].reshape(chunk * window, channels).astype(jnp.bfloat16)
        embedded = dot(part, embed_ref[...]).reshape(chunk, window, model)
        embedded = embedded + pos_slot_ref[at][:, None]
        mean = jnp.sum(embedded * embedded, axis=-1, keepdims=True) / model
        scale_ref[at] = jnp.broadcast_to(lax.rsqrt(mean + 1e-06), (chunk, window, LANES))

    if chunk == patches:
        measure(0)
    else:
        pl.loop(0, patches // chunk)(measure)

    latents = latent_ref[...].reshape(rows, channels).astype(jnp.bfloat16)
    twice = jnp.concatenate([latents, latents], axis=1)
    scale = scale_ref[...].reshape(rows, LANES)[:, :1]

    def project(index):
        flat = dot(twice, scaled_ref[index]).reshape(patches, window, cols)
        flat = (flat + offset_ref[index][:, None]).reshape(rows, cols)
        return (flat * scale).astype(jnp.bfloat16)

    query = dot(select_ref[...], project(0)).astype(jnp.bfloat16)
    key, value = project(1), project(2)
    bias = bias_ref[...]
    heads = []
    for head in range(cols // HS):
        at = slice(head * HS, (head + 1) * HS)
        scores = lax.dot_general(
            query[:, at], key[:, at], (((1,), (1,)), ((), ())), preferred_element_type=jnp.float32
        )
        scores = scores * (HS**-0.5) + bias
        expo = jnp.exp(scores - jnp.max(scores, axis=-1, keepdims=True))
        probs = (expo / jnp.sum(expo, axis=-1, keepdims=True)).astype(jnp.bfloat16)
        heads.append(dot(probs, value[:, at]).astype(jnp.bfloat16))
    mine = dot(select_mine_ref[...], latents).astype(jnp.bfloat16)
    mine_ref[...] = dot(mine, embed_ref[...]) + pos_mine_ref[...]
    arrival.wait()
    mixed = dot(jnp.concatenate(heads, axis=1), out_weight_ref[...])
    for other in range(group):
        mixed_ref[other] = mixed[other * share : (other + 1) * share].astype(jnp.bfloat16)


def sum_kernel(mine_ref, mixed_ref, out_ref):
    total = mine_ref[...]
    for member in range(mixed_ref.shape[0]):
        total = total + mixed_ref[member].astype(jnp.float32)
    out_ref[...] = total.astype(jnp.bfloat16)


def on_device(
    gen_hidden,
    gen_out_weight,
    patch_order,
    frame_block,
    embed_weight,
    pos_table,
    norm_gain,
    qkv_weight,
    out_weight,
):
    slots, frames, depth = gen_hidden.shape
    channels, model = embed_weight.shape
    cols = qkv_weight.shape[2]
    seqs = lax.axis_size("seq")
    group = lax.axis_size(GROUP)
    patches = seqs * slots
    frame_dev = frames // seqs
    window = frame_dev + 2 * REACH
    rows = window * patches
    own_rows = frame_dev * patches
    share = own_rows // group
    f32, bf16 = jnp.float32, jnp.bfloat16
    array = jax.ShapeDtypeStruct
    grant = (16 if rows <= STEP_ROWS else 40) * MIB

    windows = pl.pallas_call(
        functools.partial(latent_kernel, frame_dev),
        out_shape=array((seqs, group, slots, window, channels), bf16),
        in_specs=[HBM] * 2,
        out_specs=VMEM,
        scratch_shapes=[
            pltpu.VMEM((slots, frames, depth), bf16),
            pltpu.VMEM((depth, channels), bf16),
            pltpu.VMEM((slots, frames + 2 * REACH, channels), f32),
            pltpu.SemaphoreType.DMA((2,)),
        ],
        compiler_params=pltpu.CompilerParams(vmem_limit_bytes=12 * MIB),
        cost_estimate=pl.CostEstimate(
            flops=20_000_000_000, bytes_accessed=40_000_000, transcendentals=0
        ),
        name="partial_latents",
    )(
        pltpu.with_memory_space_constraint(gen_hidden, pltpu.HBM),
        pltpu.with_memory_space_constraint(gen_out_weight, pltpu.HBM),
    )
    moved = lax.all_to_all(
        windows.reshape(seqs * group, slots, window, channels),
        EVERY,
        split_axis=0,
        concat_axis=0,
        tiled=True,
    ).reshape(seqs, group, slots, window, channels)

    products = pl.pallas_call(
        functools.partial(weights_kernel, frame_dev, window),
        out_shape=(
            array((3, 2 * channels, cols), bf16),
            array((3, patches, cols), f32),
            array((patches, model), f32),
            array((share, model), f32),
            array((own_rows, rows), bf16),
            array((share, rows), bf16),
            array((own_rows, rows), f32),
        ),
        in_specs=[SMEM] * 2 + [VMEM] * 3 + [HBM],
        out_specs=(VMEM,) * 7,
        scratch_shapes=[
            pltpu.VMEM((3, patches, cols), f32),
            pltpu.VMEM((patches, model), f32),
            pltpu.VMEM((3, model, cols), bf16),
            pltpu.SemaphoreType.DMA((3 * (cols // min(cols, WIDTH)),)),
        ],
        compiler_params=pltpu.CompilerParams(vmem_limit_bytes=24 * MIB),
        cost_estimate=pl.CostEstimate(
            flops=2 * (channels + patches) * model * 3 * cols,
            bytes_accessed=2 * model * 3 * cols,
            transcendentals=0,
        ),
        name="weight_products",
    )(
        patch_order,
        frame_block,
        embed_weight,
        pos_table,
        norm_gain.reshape(model // LANES, LANES),
        pltpu.with_memory_space_constraint(jnp.transpose(qkv_weight, (1, 0, 2)), pltpu.HBM),
    )

    mixed, mine = pl.pallas_call(
        attend_kernel,
        out_shape=(array((group, share, model), bf16), array((share, model), f32)),
        in_specs=[VMEM] * 9 + [HBM],
        out_specs=(VMEM, VMEM),
        scratch_shapes=[
            pltpu.VMEM((patches, window, channels), f32),
            pltpu.VMEM((patches, window, LANES), f32),
            pltpu.VMEM((cols, model), bf16),
            pltpu.SemaphoreType.DMA(()),
        ],
        compiler_params=pltpu.CompilerParams(vmem_limit_bytes=grant),
        name="attend",
    )(
        moved,
        embed_weight,
        *products,
        pltpu.with_memory_space_constraint(out_weight, pltpu.HBM),
    )
    mixed = lax.all_to_all(mixed, GROUP, split_axis=0, concat_axis=0, tiled=True)
    return pl.pallas_call(
        sum_kernel,
        out_shape=array((share, model), bf16),
        in_specs=[VMEM] * 2,
        out_specs=VMEM,
        compiler_params=pltpu.CompilerParams(vmem_limit_bytes=8 * MIB),
        name="final_sum",
    )(mine, mixed)


def solution(mesh):
    in_specs = (
        P("seq", None, ("mp", "role")),
        P(("mp", "role"), None),
        P(),
        P(),
        P(),
        P(),
        P(),
        P(None, None, ("mp", "role")),
        P(("mp", "role"), None),
    )
    out_specs = P(("seq", "mp", "role"), None)
    return jax.shard_map(
        on_device, mesh=mesh, in_specs=in_specs, out_specs=out_specs, check_vma=False
    )
```

```python
import functools

import jax
import jax.numpy as jnp
from jax import lax
from jax.experimental import pallas as pl
from jax.experimental.pallas import tpu as pltpu
from jax.sharding import PartitionSpec as P

HS = 128
MOSTB = 4
REACH = MOSTB - 1
GROUP = ("mp", "role")
SCATTERED = ("role", "mp", "seq")
LANES = 128
STEP_ROWS = 256
WIDTH = 256
AHEAD = 3
MIB = 1024 * 1024
VMEM = pl.BlockSpec(memory_space=pltpu.VMEM)
SMEM = pl.BlockSpec(memory_space=pltpu.SMEM)
HBM = pl.BlockSpec(memory_space=pltpu.HBM)


def dot(a, b):
    return jnp.dot(a, b, preferred_element_type=jnp.float32)


def latent_kernel(
    frame_dev, hidden_hbm, weight_hbm, out_ref, hidden_ref, weight_ref, padded_ref, sems
):
    copies = [
        pltpu.make_async_copy(hidden_hbm, hidden_ref, sems.at[0]),
        pltpu.make_async_copy(weight_hbm, weight_ref, sems.at[1]),
    ]
    for copy in copies:
        copy.start()
    slots, frames, depth = hidden_ref.shape
    group, seqs, _, window, channels = out_ref.shape
    padded_ref[...] = jnp.zeros_like(padded_ref)
    for copy in copies:
        copy.wait()
    for slot in range(slots):
        padded_ref[slot, REACH : REACH + frames] = dot(hidden_ref[slot], weight_ref[...])
    for to in range(seqs):
        piece = padded_ref[:, to * frame_dev : to * frame_dev + window]
        for member in range(group):
            out_ref[member, to] = piece.astype(out_ref.dtype)


def weights_kernel(
    frame_dev,
    window,
    order_ref,
    block_ref,
    embed_ref,
    pos_ref,
    gain_ref,
    weight_hbm,
    out_weight_hbm,
    scaled_ref,
    offset_ref,
    pos_slot_ref,
    pos_mine_ref,
    select_ref,
    select_mine_ref,
    bias_ref,
    first_ref,
    natural_ref,
    pos_all_ref,
    weight_ref,
    sems,
    first_sem,
):
    channels, model = embed_ref.shape
    patches = pos_ref.shape[0]
    frames = block_ref.shape[0]
    own_rows, rows = bias_ref.shape
    share = select_mine_ref.shape[0]
    device = lax.axis_index("seq")
    member = lax.axis_index(GROUP)

    cols = weight_ref.shape[2]
    width = min(cols, WIDTH)
    parts = [(index, at) for index in range(3) for at in range(0, cols, width)]

    def arrival(part):
        index, at = parts[part]
        place = (index, slice(None), pl.ds(at, width))
        return pltpu.make_async_copy(weight_hbm.at[place], weight_ref.at[place], sems.at[part])

    first = pltpu.make_async_copy(
        out_weight_hbm.at[pl.ds(0, first_ref.shape[0])], first_ref, first_sem
    )
    for part in range(AHEAD):
        arrival(part).start()

    gain = jnp.concatenate(
        [gain_ref[at : at + 1, :].astype(jnp.float32) for at in range(model // LANES)], axis=1
    )
    pos = pos_ref[...].astype(jnp.float32)
    left = jnp.concatenate([embed_ref[...].astype(jnp.float32) * gain, pos * gain], axis=0)
    left = left.astype(jnp.bfloat16)
    pos_all_ref[...] = pos

    column = lax.broadcasted_iota(jnp.int32, (1, rows), 1)
    column_slot, column_frame = column // window, column % window

    def patch_at(slot, found):
        return jnp.where(column_slot == slot, order_ref[slot], found)

    column_patch = jnp.zeros((1, rows), jnp.int32)
    if patches <= 16:
        for slot in range(patches):
            column_patch = patch_at(slot, column_patch)
    else:
        column_patch = lax.fori_loop(0, patches, patch_at, column_patch)

    def select(count, first):
        row = lax.broadcasted_iota(jnp.int32, (count, rows), 0) + first
        hit = jnp.logical_and(
            column_patch == row % patches, column_frame == row // patches + REACH
        )
        return jnp.where(hit, 1.0, 0.0).astype(jnp.bfloat16)

    select_ref[...] = select(own_rows, 0)
    select_mine_ref[...] = select(share, member * share)
    for frame in range(frame_dev * patches // share):
        row = frame * share

        @pl.when(member == frame)
        def _():
            for at in range(share):
                mine = (row + at) % patches
                pos_mine_ref[at : at + 1, :] = pos_all_ref[mine : mine + 1, :]

    def block_of(frame):
        inside = jnp.logical_and(frame >= 0, frame < frames)
        return jnp.where(inside, block_ref[jnp.clip(frame, 0, frames - 1)], -1)

    column_block = jnp.full((1, rows), -1, jnp.int32)
    for frame in range(window):
        found = block_of(device * frame_dev - REACH + frame)
        column_block = jnp.where(column_frame == frame, found, column_block)
    row_frame = lax.broadcasted_iota(jnp.int32, (own_rows, rows), 0) // patches
    row_block = jnp.full((own_rows, rows), -2, jnp.int32)
    for frame in range(frame_dev):
        row_block = jnp.where(row_frame == frame, block_of(device * frame_dev + frame), row_block)
    bias_ref[...] = jnp.where(row_block == column_block, 0.0, -1e30)

    for part, (index, at) in enumerate(parts):
        arrival(part).wait()
        if part + AHEAD < len(parts):
            arrival(part + AHEAD).start()
        if part + AHEAD == len(parts) - 1:
            first.start()
        here = slice(at, at + width)
        both = dot(left, weight_ref[index, :, here])
        scaled = both[:channels]
        high = scaled.astype(jnp.bfloat16)
        scaled_ref[index, :channels, here] = high
        scaled_ref[index, channels:, here] = (scaled - high.astype(jnp.float32)).astype(jnp.bfloat16)
        natural_ref[index, :, here] = both[channels:]

    def place(slot):
        at = pl.ds(order_ref[slot], 1)
        pos_slot_ref[pl.ds(slot, 1), :] = pos_all_ref[at, :]
        for index in range(3):
            offset_ref[index, pl.ds(slot, 1), :] = natural_ref[index, at, :]

    if patches <= 16:
        for slot in range(patches):
            place(slot)
    else:
        pl.loop(0, patches)(place)
    first.wait()


def attend_kernel(
    partial_ref,
    embed_ref,
    scaled_ref,
    offset_ref,
    pos_slot_ref,
    pos_mine_ref,
    select_ref,
    select_mine_ref,
    bias_ref,
    first_ref,
    out_weight_hbm,
    mixed_ref,
    mine_ref,
    latent_ref,
    scale_ref,
    second_ref,
    sem,
):
    half = first_ref.shape[0]
    arrival = pltpu.make_async_copy(out_weight_hbm.at[pl.ds(half, half)], second_ref, sem)
    arrival.start()
    everyone, slots, window, channels = partial_ref.shape
    group = mixed_ref.shape[0]
    seqs = everyone // group
    patches = seqs * slots
    rows = patches * window
    share, model = mine_ref.shape
    cols = out_weight_hbm.shape[0]

    total = partial_ref[:seqs].astype(jnp.float32)
    for other in range(1, group):
        total = total + partial_ref[other * seqs : (other + 1) * seqs].astype(jnp.float32)
    latent_ref[...] = total.reshape(patches, window, channels)
    chunk = min(patches, STEP_ROWS // window)

    latents = latent_ref[...].reshape(rows, channels).astype(jnp.bfloat16)
    mine = dot(select_mine_ref[...], latents).astype(jnp.bfloat16)

    def measure(start, part):
        embedded = embedded_rows(part)[: chunk * window].reshape(chunk, window, model)
        embedded = embedded + pos_slot_ref[pl.ds(start, chunk)][:, None]
        mean = jnp.sum(embedded * embedded, axis=-1, keepdims=True) / model
        scale = jnp.broadcast_to(lax.rsqrt(mean + 1e-06), (chunk, window, LANES))
        scale_ref[pl.ds(start, chunk)] = scale

    def embedded_rows(part):
        both = dot(jnp.concatenate([part, mine], axis=0), embed_ref[...])
        mine_ref[...] = both[part.shape[0] :] + pos_mine_ref[...]
        return both

    if chunk == patches:
        measure(0, latents)
    else:

        @pl.loop(0, patches // chunk)
        def _(step):
            part = latent_ref[pl.ds(step * chunk, chunk)]
            measure(step * chunk, part.reshape(chunk * window, channels).astype(jnp.bfloat16))

    twice = jnp.concatenate([latents, latents], axis=1)
    scale = scale_ref[...].reshape(rows, LANES)[:, :1]

    def project(index):
        flat = dot(twice, scaled_ref[index]).reshape(patches, window, cols)
        flat = (flat + offset_ref[index][:, None]).reshape(rows, cols)
        return (flat * scale).astype(jnp.bfloat16)

    query = dot(select_ref[...], project(0)).astype(jnp.bfloat16)
    key, value = project(1), project(2)
    bias = bias_ref[...]
    heads = []
    for head in range(cols // HS):
        at = slice(head * HS, (head + 1) * HS)
        scores = lax.dot_general(
            query[:, at], key[:, at], (((1,), (1,)), ((), ())), preferred_element_type=jnp.float32
        )
        scores = scores * (HS**-0.5) + bias
        expo = jnp.exp(scores - jnp.max(scores, axis=-1, keepdims=True))
        probs = (expo / jnp.sum(expo, axis=-1, keepdims=True)).astype(jnp.bfloat16)
        heads.append(dot(probs, value[:, at]).astype(jnp.bfloat16))
    heads = jnp.concatenate(heads, axis=1)
    mixed = dot(heads[:, :half], first_ref[...])
    arrival.wait()
    mixed = mixed + dot(heads[:, half:], second_ref[...])
    for other in range(group):
        mixed_ref[other] = mixed[other * share : (other + 1) * share].astype(jnp.bfloat16)


def sum_kernel(mine_ref, mixed_ref, out_ref):
    total = mine_ref[...]
    for member in range(mixed_ref.shape[0]):
        total = total + mixed_ref[member].astype(jnp.float32)
    out_ref[...] = total.astype(jnp.bfloat16)


def on_device(
    gen_hidden,
    gen_out_weight,
    patch_order,
    frame_block,
    embed_weight,
    pos_table,
    norm_gain,
    qkv_weight,
    out_weight,
):
    slots, frames, depth = gen_hidden.shape
    channels, model = embed_weight.shape
    cols = qkv_weight.shape[2]
    out_weight = pltpu.with_memory_space_constraint(out_weight, pltpu.HBM)
    seqs = lax.axis_size("seq")
    group = lax.axis_size(GROUP)
    patches = seqs * slots
    frame_dev = frames // seqs
    window = frame_dev + 2 * REACH
    rows = window * patches
    own_rows = frame_dev * patches
    share = own_rows // group
    f32, bf16 = jnp.float32, jnp.bfloat16
    array = jax.ShapeDtypeStruct
    grant = (16 if rows <= STEP_ROWS else 40) * MIB

    windows = pl.pallas_call(
        functools.partial(latent_kernel, frame_dev),
        out_shape=array((group, seqs, slots, window, channels), bf16),
        in_specs=[HBM] * 2,
        out_specs=VMEM,
        scratch_shapes=[
            pltpu.VMEM((slots, frames, depth), bf16),
            pltpu.VMEM((depth, channels), bf16),
            pltpu.VMEM((slots, frames + 2 * REACH, channels), f32),
            pltpu.SemaphoreType.DMA((2,)),
        ],
        compiler_params=pltpu.CompilerParams(vmem_limit_bytes=12 * MIB),
        cost_estimate=pl.CostEstimate(
            flops=20_000_000_000, bytes_accessed=40_000_000, transcendentals=0
        ),
        name="partial_latents",
    )(
        pltpu.with_memory_space_constraint(gen_hidden, pltpu.HBM),
        pltpu.with_memory_space_constraint(gen_out_weight, pltpu.HBM),
    )
    moved = lax.all_to_all(
        pltpu.with_memory_space_constraint(
            windows.reshape(group * seqs, slots, window, channels), pltpu.VMEM
        ),
        SCATTERED,
        split_axis=0,
        concat_axis=0,
        tiled=True,
    )

    products = pl.pallas_call(
        functools.partial(weights_kernel, frame_dev, window),
        out_shape=(
            array((3, 2 * channels, cols), bf16),
            array((3, patches, cols), f32),
            array((patches, model), f32),
            array((share, model), f32),
            array((own_rows, rows), bf16),
            array((share, rows), bf16),
            array((own_rows, rows), f32),
            array((cols // 2, model), bf16),
        ),
        in_specs=[SMEM] * 2 + [VMEM] * 3 + [HBM] * 2,
        out_specs=(VMEM,) * 8,
        scratch_shapes=[
            pltpu.VMEM((3, patches, cols), f32),
            pltpu.VMEM((patches, model), f32),
            pltpu.VMEM((3, model, cols), bf16),
            pltpu.SemaphoreType.DMA((3 * (cols // min(cols, WIDTH)),)),
            pltpu.SemaphoreType.DMA(()),
        ],
        compiler_params=pltpu.CompilerParams(vmem_limit_bytes=24 * MIB),
        cost_estimate=pl.CostEstimate(
            flops=2 * (channels + patches) * model * 3 * cols,
            bytes_accessed=2 * model * 3 * cols,
            transcendentals=0,
        ),
        name="weight_products",
    )(
        patch_order,
        frame_block,
        embed_weight,
        pos_table,
        norm_gain.reshape(model // LANES, LANES),
        pltpu.with_memory_space_constraint(jnp.transpose(qkv_weight, (1, 0, 2)), pltpu.HBM),
        out_weight,
    )

    mixed, mine = pl.pallas_call(
        attend_kernel,
        out_shape=(array((group, share, model), bf16), array((share, model), f32)),
        in_specs=[VMEM] * 10 + [HBM],
        out_specs=(VMEM, VMEM),
        scratch_shapes=[
            pltpu.VMEM((patches, window, channels), f32),
            pltpu.VMEM((patches, window, LANES), f32),
            pltpu.VMEM((cols - cols // 2, model), bf16),
            pltpu.SemaphoreType.DMA(()),
        ],
        compiler_params=pltpu.CompilerParams(vmem_limit_bytes=grant),
        name="attend",
    )(
        moved,
        embed_weight,
        *products,
        out_weight,
    )
    mixed = lax.all_to_all(mixed, GROUP, split_axis=0, concat_axis=0, tiled=True)
    return pl.pallas_call(
        sum_kernel,
        out_shape=array((share, model), bf16),
        in_specs=[VMEM] * 2,
        out_specs=VMEM,
        compiler_params=pltpu.CompilerParams(vmem_limit_bytes=8 * MIB),
        name="final_sum",
    )(mine, mixed)


def solution(mesh):
    in_specs = (
        P("seq", None, ("mp", "role")),
        P(("mp", "role"), None),
        P(),
        P(),
        P(),
        P(),
        P(),
        P(None, None, ("mp", "role")),
        P(("mp", "role"), None),
    )
    out_specs = P(("seq", "mp", "role"), None)
    return jax.shard_map(
        on_device, mesh=mesh, in_specs=in_specs, out_specs=out_specs, check_vma=False
    )
```

```python
import functools

import jax
import jax.numpy as jnp
from jax import lax
from jax.experimental import pallas as pl
from jax.experimental.pallas import tpu as pltpu
from jax.sharding import PartitionSpec as P

HS = 128
MOSTB = 4
REACH = MOSTB - 1
GROUP = ("mp", "role")
SCATTERED = ("role", "mp", "seq")
LANES = 128
STEP_ROWS = 256
WIDTH = 256
AHEAD = 3
MIB = 1024 * 1024
VMEM = pl.BlockSpec(memory_space=pltpu.VMEM)
SMEM = pl.BlockSpec(memory_space=pltpu.SMEM)
HBM = pl.BlockSpec(memory_space=pltpu.HBM)


def dot(a, b):
    return jnp.dot(a, b, preferred_element_type=jnp.float32)


def latent_kernel(
    frame_dev, hidden_hbm, weight_hbm, out_ref, hidden_ref, weight_ref, padded_ref, sems
):
    copies = [
        pltpu.make_async_copy(hidden_hbm, hidden_ref, sems.at[0]),
        pltpu.make_async_copy(weight_hbm, weight_ref, sems.at[1]),
    ]
    for copy in copies:
        copy.start()
    slots, frames, depth = hidden_ref.shape
    everyone, _, window, channels = out_ref.shape
    seqs = frames // frame_dev
    padded_ref[...] = jnp.zeros_like(padded_ref)
    for copy in copies:
        copy.wait()
    for slot in range(slots):
        padded_ref[slot, REACH : REACH + frames] = dot(hidden_ref[slot], weight_ref[...])
    for to in range(seqs):
        piece = padded_ref[:, to * frame_dev : to * frame_dev + window]
        for at in range(to, everyone, seqs):
            out_ref[at] = piece.astype(out_ref.dtype)


def weights_kernel(
    frame_dev,
    window,
    order_ref,
    block_ref,
    pos_ref,
    gain_ref,
    embed_hbm,
    weight_hbm,
    scaled_ref,
    offset_ref,
    pos_slot_ref,
    pos_mine_ref,
    select_ref,
    select_mine_ref,
    bias_ref,
    embed_ref,
    natural_ref,
    pos_all_ref,
    weight_ref,
    sems,
    embed_sem,
):
    channels, model = embed_ref.shape
    patches = pos_ref.shape[0]
    frames = block_ref.shape[0]
    own_rows, rows = bias_ref.shape
    share = select_mine_ref.shape[0]
    device = lax.axis_index("seq")
    member = lax.axis_index(GROUP)

    cols = weight_ref.shape[2]
    width = min(cols, WIDTH)
    parts = [(index, at) for index in range(3) for at in range(0, cols, width)]

    def arrival(part):
        index, at = parts[part]
        place = (index, slice(None), pl.ds(at, width))
        return pltpu.make_async_copy(weight_hbm.at[place], weight_ref.at[place], sems.at[part])

    embed_arrival = pltpu.make_async_copy(embed_hbm, embed_ref, embed_sem)
    embed_arrival.start()
    for part in range(AHEAD):
        arrival(part).start()

    pos = pos_ref[...].astype(jnp.float32)
    pos_all_ref[...] = pos

    column = lax.broadcasted_iota(jnp.int32, (1, rows), 1)
    column_slot, column_frame = column // window, column % window

    def patch_at(slot, found):
        return jnp.where(column_slot == slot, order_ref[slot], found)

    column_patch = jnp.zeros((1, rows), jnp.int32)
    if patches <= 16:
        for slot in range(patches):
            column_patch = patch_at(slot, column_patch)
    else:
        column_patch = lax.fori_loop(0, patches, patch_at, column_patch)

    def select(count, first):
        row = lax.broadcasted_iota(jnp.int32, (count, rows), 0) + first
        hit = jnp.logical_and(
            column_patch == row % patches, column_frame == row // patches + REACH
        )
        return jnp.where(hit, 1.0, 0.0).astype(jnp.bfloat16)

    select_ref[...] = select(own_rows, 0)
    select_mine_ref[...] = select(share, member * share)
    for frame in range(frame_dev * patches // share):
        row = frame * share

        @pl.when(member == frame)
        def _():
            for at in range(share):
                mine = (row + at) % patches
                pos_mine_ref[at : at + 1, :] = pos_all_ref[mine : mine + 1, :]

    def block_of(frame):
        inside = jnp.logical_and(frame >= 0, frame < frames)
        return jnp.where(inside, block_ref[jnp.clip(frame, 0, frames - 1)], -1)

    column_block = jnp.full((1, rows), -1, jnp.int32)
    for frame in range(window):
        found = block_of(device * frame_dev - REACH + frame)
        column_block = jnp.where(column_frame == frame, found, column_block)
    row_frame = lax.broadcasted_iota(jnp.int32, (own_rows, rows), 0) // patches
    row_block = jnp.full((own_rows, rows), -2, jnp.int32)
    for frame in range(frame_dev):
        row_block = jnp.where(row_frame == frame, block_of(device * frame_dev + frame), row_block)
    bias_ref[...] = jnp.where(row_block == column_block, 0.0, -1e30)

    gain = jnp.concatenate(
        [gain_ref[at : at + 1, :].astype(jnp.float32) for at in range(model // LANES)], axis=1
    )
    embed_arrival.wait()
    left = jnp.concatenate([embed_ref[...].astype(jnp.float32) * gain, pos * gain], axis=0)
    left = left.astype(jnp.bfloat16)
    for part, (index, at) in enumerate(parts):
        arrival(part).wait()
        if part + AHEAD < len(parts):
            arrival(part + AHEAD).start()
        here = slice(at, at + width)
        both = dot(left, weight_ref[index, :, here])
        scaled = both[:channels]
        high = scaled.astype(jnp.bfloat16)
        scaled_ref[index, :channels, here] = high
        scaled_ref[index, channels:, here] = (scaled - high.astype(jnp.float32)).astype(jnp.bfloat16)
        natural_ref[index, :, here] = both[channels:]

    def place(slot):
        at = pl.ds(order_ref[slot], 1)
        pos_slot_ref[pl.ds(slot, 1), :] = pos_all_ref[at, :]
        for index in range(3):
            offset_ref[index, pl.ds(slot, 1), :] = natural_ref[index, at, :]

    if patches <= 16:
        for slot in range(patches):
            place(slot)
    else:
        pl.loop(0, patches)(place)


def attend_kernel(
    partial_ref,
    scaled_ref,
    offset_ref,
    pos_slot_ref,
    pos_mine_ref,
    select_ref,
    select_mine_ref,
    bias_ref,
    embed_ref,
    out_weight_hbm,
    mixed_ref,
    mine_ref,
    latent_ref,
    scale_ref,
    out_weight_ref,
    sem,
):
    arrival = pltpu.make_async_copy(out_weight_hbm, out_weight_ref, sem)
    arrival.start()
    everyone, slots, window, channels = partial_ref.shape
    group = mixed_ref.shape[0]
    seqs = everyone // group
    patches = seqs * slots
    rows = patches * window
    share, model = mine_ref.shape
    cols = out_weight_ref.shape[0]

    total = partial_ref[:seqs].astype(jnp.float32)
    for other in range(1, group):
        total = total + partial_ref[other * seqs : (other + 1) * seqs].astype(jnp.float32)
    latent_ref[...] = total.reshape(patches, window, channels)
    chunk = min(patches, STEP_ROWS // window)

    def measure(step):
        at = pl.ds(step * chunk, chunk)
        part = latent_ref[at].reshape(chunk * window, channels).astype(jnp.bfloat16)
        embedded = dot(part, embed_ref[...]).reshape(chunk, window, model)
        embedded = embedded + pos_slot_ref[at][:, None]
        mean = jnp.sum(embedded * embedded, axis=-1, keepdims=True) / model
        scale_ref[at] = jnp.broadcast_to(lax.rsqrt(mean + 1e-06), (chunk, window, LANES))

    if chunk == patches:
        measure(0)
    else:
        pl.loop(0, patches // chunk)(measure)

    latents = latent_ref[...].reshape(rows, channels).astype(jnp.bfloat16)
    twice = jnp.concatenate([latents, latents], axis=1)
    scale = scale_ref[...].reshape(rows, LANES)[:, :1]

    def project(index):
        flat = dot(twice, scaled_ref[index]).reshape(patches, window, cols)
        flat = (flat + offset_ref[index][:, None]).reshape(rows, cols)
        return (flat * scale).astype(jnp.bfloat16)

    query = dot(select_ref[...], project(0)).astype(jnp.bfloat16)
    key, value = project(1), project(2)
    bias = bias_ref[...]
    heads = []
    for head in range(cols // HS):
        at = slice(head * HS, (head + 1) * HS)
        scores = lax.dot_general(
            query[:, at], key[:, at], (((1,), (1,)), ((), ())), preferred_element_type=jnp.float32
        )
        scores = scores * (HS**-0.5) + bias
        expo = jnp.exp(scores - jnp.max(scores, axis=-1, keepdims=True))
        probs = (expo / jnp.sum(expo, axis=-1, keepdims=True)).astype(jnp.bfloat16)
        heads.append(dot(probs, value[:, at]).astype(jnp.bfloat16))
    mine = dot(select_mine_ref[...], latents).astype(jnp.bfloat16)
    mine_ref[...] = dot(mine, embed_ref[...]) + pos_mine_ref[...]
    arrival.wait()
    mixed = dot(jnp.concatenate(heads, axis=1), out_weight_ref[...])
    for other in range(group):
        mixed_ref[other] = mixed[other * share : (other + 1) * share].astype(jnp.bfloat16)


def sum_kernel(mine_ref, mixed_ref, out_ref):
    total = mine_ref[...]
    for member in range(mixed_ref.shape[0]):
        total = total + mixed_ref[member].astype(jnp.float32)
    out_ref[...] = total.astype(jnp.bfloat16)


def on_device(
    gen_hidden,
    gen_out_weight,
    patch_order,
    frame_block,
    embed_weight,
    pos_table,
    norm_gain,
    qkv_weight,
    out_weight,
):
    slots, frames, depth = gen_hidden.shape
    channels, model = embed_weight.shape
    cols = qkv_weight.shape[2]
    out_weight = pltpu.with_memory_space_constraint(out_weight, pltpu.HBM)
    seqs = lax.axis_size("seq")
    group = lax.axis_size(GROUP)
    patches = seqs * slots
    frame_dev = frames // seqs
    window = frame_dev + 2 * REACH
    rows = window * patches
    own_rows = frame_dev * patches
    share = own_rows // group
    f32, bf16 = jnp.float32, jnp.bfloat16
    array = jax.ShapeDtypeStruct
    grant = (16 if rows <= STEP_ROWS else 40) * MIB

    windows = pl.pallas_call(
        functools.partial(latent_kernel, frame_dev),
        out_shape=pltpu.VMEM((group * seqs, slots, window, channels), bf16),
        in_specs=[HBM] * 2,
        out_specs=VMEM,
        scratch_shapes=[
            pltpu.VMEM((slots, frames, depth), bf16),
            pltpu.VMEM((depth, channels), bf16),
            pltpu.VMEM((slots, frames + 2 * REACH, channels), f32),
            pltpu.SemaphoreType.DMA((2,)),
        ],
        compiler_params=pltpu.CompilerParams(vmem_limit_bytes=12 * MIB),
        cost_estimate=pl.CostEstimate(
            flops=20_000_000_000, bytes_accessed=40_000_000, transcendentals=0
        ),
        name="partial_latents",
    )(
        pltpu.with_memory_space_constraint(gen_hidden, pltpu.HBM),
        pltpu.with_memory_space_constraint(gen_out_weight, pltpu.HBM),
    )
    moved = lax.all_to_all(
        windows,
        SCATTERED,
        split_axis=0,
        concat_axis=0,
        tiled=True,
    )

    products = pl.pallas_call(
        functools.partial(weights_kernel, frame_dev, window),
        out_shape=(
            array((3, 2 * channels, cols), bf16),
            array((3, patches, cols), f32),
            array((patches, model), f32),
            array((share, model), f32),
            array((own_rows, rows), bf16),
            array((share, rows), bf16),
            array((own_rows, rows), f32),
            array((channels, model), bf16),
        ),
        in_specs=[SMEM] * 2 + [VMEM] * 2 + [HBM] * 2,
        out_specs=(VMEM,) * 8,
        scratch_shapes=[
            pltpu.VMEM((3, patches, cols), f32),
            pltpu.VMEM((patches, model), f32),
            pltpu.VMEM((3, model, cols), bf16),
            pltpu.SemaphoreType.DMA((3 * (cols // min(cols, WIDTH)),)),
            pltpu.SemaphoreType.DMA(()),
        ],
        compiler_params=pltpu.CompilerParams(vmem_limit_bytes=24 * MIB),
        cost_estimate=pl.CostEstimate(
            flops=2 * (channels + patches) * model * 3 * cols,
            bytes_accessed=2 * model * 3 * cols,
            transcendentals=0,
        ),
        name="weight_products",
    )(
        patch_order,
        frame_block,
        pos_table,
        norm_gain.reshape(model // LANES, LANES),
        pltpu.with_memory_space_constraint(embed_weight, pltpu.HBM),
        pltpu.with_memory_space_constraint(jnp.transpose(qkv_weight, (1, 0, 2)), pltpu.HBM),
    )

    mixed, mine = pl.pallas_call(
        attend_kernel,
        out_shape=(array((group, share, model), bf16), array((share, model), f32)),
        in_specs=[VMEM] * 9 + [HBM],
        out_specs=(VMEM, VMEM),
        scratch_shapes=[
            pltpu.VMEM((patches, window, channels), f32),
            pltpu.VMEM((patches, window, LANES), f32),
            pltpu.VMEM((cols, model), bf16),
            pltpu.SemaphoreType.DMA(()),
        ],
        compiler_params=pltpu.CompilerParams(vmem_limit_bytes=grant),
        name="attend",
    )(
        moved,
        *products,
        out_weight,
    )
    mixed = lax.all_to_all(mixed, GROUP, split_axis=0, concat_axis=0, tiled=True)
    return pl.pallas_call(
        sum_kernel,
        out_shape=array((share, model), bf16),
        in_specs=[VMEM] * 2,
        out_specs=VMEM,
        compiler_params=pltpu.CompilerParams(vmem_limit_bytes=8 * MIB),
        name="final_sum",
    )(mine, mixed)


def solution(mesh):
    in_specs = (
        P("seq", None, ("mp", "role")),
        P(("mp", "role"), None),
        P(),
        P(),
        P(),
        P(),
        P(),
        P(None, None, ("mp", "role")),
        P(("mp", "role"), None),
    )
    out_specs = P(("seq", "mp", "role"), None)
    return jax.shard_map(
        on_device, mesh=mesh, in_specs=in_specs, out_specs=out_specs, check_vma=False
    )
```

```python
import functools

import jax
import jax.numpy as jnp
from jax import lax
from jax.experimental import pallas as pl
from jax.experimental.pallas import tpu as pltpu
from jax.sharding import PartitionSpec as P

HS = 128
MOSTB = 4
REACH = MOSTB - 1
GROUP = ("mp", "role")
SCATTERED = ("role", "mp", "seq")
LANES = 128
STEP_ROWS = 256
WIDTH = 256
AHEAD = 3
MIB = 1024 * 1024
VMEM = pl.BlockSpec(memory_space=pltpu.VMEM)
SMEM = pl.BlockSpec(memory_space=pltpu.SMEM)
HBM = pl.BlockSpec(memory_space=pltpu.HBM)


def dot(a, b):
    return jnp.dot(a, b, preferred_element_type=jnp.float32)


def latent_kernel(
    frame_dev, hidden_hbm, weight_hbm, out_ref, hidden_ref, weight_ref, padded_ref, sems
):
    copies = [
        pltpu.make_async_copy(hidden_hbm, hidden_ref, sems.at[0]),
        pltpu.make_async_copy(weight_hbm, weight_ref, sems.at[1]),
    ]
    for copy in copies:
        copy.start()
    slots, frames, depth = hidden_ref.shape
    everyone, _, window, channels = out_ref.shape
    seqs = frames // frame_dev
    padded_ref[...] = jnp.zeros_like(padded_ref)
    for copy in copies:
        copy.wait()
    for slot in range(slots):
        padded_ref[slot, REACH : REACH + frames] = dot(hidden_ref[slot], weight_ref[...])
    for to in range(seqs):
        piece = padded_ref[:, to * frame_dev : to * frame_dev + window]
        for at in range(to, everyone, seqs):
            out_ref[at] = piece.astype(out_ref.dtype)


def weights_kernel(
    frame_dev,
    window,
    order_ref,
    block_ref,
    pos_ref,
    gain_ref,
    embed_hbm,
    weight_hbm,
    scaled_ref,
    offset_ref,
    pos_slot_ref,
    pos_all_ref,
    select_ref,
    bias_ref,
    embed_ref,
    natural_ref,
    weight_ref,
    sems,
    embed_sem,
):
    channels, model = embed_ref.shape
    patches = pos_ref.shape[0]
    frames = block_ref.shape[0]
    own_rows, rows = bias_ref.shape
    device = lax.axis_index("seq")

    cols = weight_ref.shape[2]
    width = min(cols, WIDTH)
    parts = [(index, at) for index in range(3) for at in range(0, cols, width)]

    def arrival(part):
        index, at = parts[part]
        place = (index, slice(None), pl.ds(at, width))
        return pltpu.make_async_copy(weight_hbm.at[place], weight_ref.at[place], sems.at[part])

    embed_arrival = pltpu.make_async_copy(embed_hbm, embed_ref, embed_sem)
    embed_arrival.start()
    for part in range(AHEAD):
        arrival(part).start()

    pos = pos_ref[...].astype(jnp.float32)
    pos_all_ref[...] = pos

    column = lax.broadcasted_iota(jnp.int32, (1, rows), 1)
    column_slot, column_frame = column // window, column % window

    def patch_at(slot, found):
        return jnp.where(column_slot == slot, order_ref[slot], found)

    column_patch = jnp.zeros((1, rows), jnp.int32)
    if patches <= 16:
        for slot in range(patches):
            column_patch = patch_at(slot, column_patch)
    else:
        column_patch = lax.fori_loop(0, patches, patch_at, column_patch)

    row = lax.broadcasted_iota(jnp.int32, (own_rows, rows), 0)
    hit = jnp.logical_and(column_patch == row % patches, column_frame == row // patches + REACH)
    select_ref[...] = jnp.where(hit, 1.0, 0.0).astype(jnp.bfloat16)

    def block_of(frame):
        inside = jnp.logical_and(frame >= 0, frame < frames)
        return jnp.where(inside, block_ref[jnp.clip(frame, 0, frames - 1)], -1)

    column_block = jnp.full((1, rows), -1, jnp.int32)
    for frame in range(window):
        found = block_of(device * frame_dev - REACH + frame)
        column_block = jnp.where(column_frame == frame, found, column_block)
    row_frame = row // patches
    row_block = jnp.full((own_rows, rows), -2, jnp.int32)
    for frame in range(frame_dev):
        row_block = jnp.where(row_frame == frame, block_of(device * frame_dev + frame), row_block)
    bias_ref[...] = jnp.where(row_block == column_block, 0.0, -1e30)

    gain = jnp.concatenate(
        [gain_ref[at : at + 1, :].astype(jnp.float32) for at in range(model // LANES)], axis=1
    )
    embed_arrival.wait()
    left = jnp.concatenate([embed_ref[...].astype(jnp.float32) * gain, pos * gain], axis=0)
    left = left.astype(jnp.bfloat16)
    for part, (index, at) in enumerate(parts):
        arrival(part).wait()
        if part + AHEAD < len(parts):
            arrival(part + AHEAD).start()
        here = slice(at, at + width)
        both = dot(left, weight_ref[index, :, here])
        scaled = both[:channels]
        high = scaled.astype(jnp.bfloat16)
        scaled_ref[index, :channels, here] = high
        scaled_ref[index, channels:, here] = (scaled - high.astype(jnp.float32)).astype(jnp.bfloat16)
        natural_ref[index, :, here] = both[channels:]

    offset_ref[0] = natural_ref[0]

    def place(slot):
        at = pl.ds(order_ref[slot], 1)
        pos_slot_ref[pl.ds(slot, 1), :] = pos_all_ref[at, :]
        for index in range(1, 3):
            offset_ref[index, pl.ds(slot, 1), :] = natural_ref[index, at, :]

    if patches <= 16:
        for slot in range(patches):
            place(slot)
    else:
        pl.loop(0, patches)(place)


def attend_kernel(
    partial_ref,
    scaled_ref,
    offset_ref,
    pos_slot_ref,
    pos_all_ref,
    select_ref,
    bias_ref,
    embed_ref,
    out_weight_hbm,
    mixed_ref,
    mine_ref,
    latent_ref,
    scale_ref,
    own_ref,
    out_weight_ref,
    sem,
):
    arrival = pltpu.make_async_copy(out_weight_hbm, out_weight_ref, sem)
    arrival.start()
    everyone, slots, window, channels = partial_ref.shape
    group, share, model = mixed_ref.shape
    seqs = everyone // group
    patches = seqs * slots
    rows = patches * window
    own_rows = group * share
    frame_dev = own_rows // patches
    cols = out_weight_ref.shape[0]
    chunk = min(patches, STEP_ROWS // window)

    total = partial_ref[:seqs].astype(jnp.float32)
    for other in range(1, group):
        total = total + partial_ref[other * seqs : (other + 1) * seqs].astype(jnp.float32)
    latent_ref[...] = total.reshape(patches, window, channels)
    latents = total.reshape(rows, channels).astype(jnp.bfloat16)
    own = dot(select_ref[...], latents).astype(jnp.bfloat16)

    def project(index, part):
        return dot(jnp.concatenate([part, part], axis=1), scaled_ref[index])

    def of_window(index):
        flat = project(index, latents).reshape(patches, window, cols)
        flat = flat + offset_ref[index][:, None]
        return flat.reshape(rows, cols).astype(jnp.bfloat16)

    def by_patch(table):
        return jnp.concatenate([table] * frame_dev, axis=0)

    query = (project(0, own) + by_patch(offset_ref[0])).astype(jnp.bfloat16)
    key, value = of_window(1), of_window(2)

    def scale_of(embedded):
        mean = jnp.sum(embedded * embedded, axis=-1, keepdims=True) / model
        return lax.rsqrt(mean + 1e-06)

    def measure(start, embedded):
        embedded = embedded.reshape(chunk, window, model)
        scale = scale_of(embedded + pos_slot_ref[pl.ds(start, chunk)][:, None])
        scale_ref[pl.ds(start, chunk)] = jnp.broadcast_to(scale, (chunk, window, LANES))

    if chunk == patches:
        both = dot(jnp.concatenate([latents, own], axis=0), embed_ref[...])
        measure(0, both[:rows])
        own_embedded = both[rows:]
    else:

        @pl.loop(0, patches // chunk)
        def _(step):
            part = latent_ref[pl.ds(step * chunk, chunk)].reshape(chunk * window, channels)
            measure(step * chunk, dot(part.astype(jnp.bfloat16), embed_ref[...]))

        own_embedded = dot(own, embed_ref[...])

    own_embedded = own_embedded + by_patch(pos_all_ref[...])
    row_scale = scale_of(own_embedded) * (HS**-0.5)
    column_scale = jnp.transpose(scale_ref[...].reshape(rows, LANES))[:1]
    factor = row_scale * column_scale
    bias = bias_ref[...]
    heads = []
    for head in range(cols // HS):
        at = slice(head * HS, (head + 1) * HS)
        scores = lax.dot_general(
            query[:, at], key[:, at], (((1,), (1,)), ((), ())), preferred_element_type=jnp.float32
        )
        scores = scores * factor + bias
        expo = jnp.exp(scores - jnp.max(scores, axis=-1, keepdims=True))
        probs = expo * (column_scale / jnp.sum(expo, axis=-1, keepdims=True))
        heads.append(dot(probs.astype(jnp.bfloat16), value[:, at]).astype(jnp.bfloat16))
    for other in range(group):
        own_ref[other] = own_embedded[other * share : (other + 1) * share]
    mine_ref[...] = own_ref[lax.axis_index(GROUP)]
    arrival.wait()
    mixed = dot(jnp.concatenate(heads, axis=1), out_weight_ref[...])
    for other in range(group):
        mixed_ref[other] = mixed[other * share : (other + 1) * share].astype(jnp.bfloat16)


def sum_kernel(mine_ref, mixed_ref, out_ref):
    total = mine_ref[...]
    for member in range(mixed_ref.shape[0]):
        total = total + mixed_ref[member].astype(jnp.float32)
    out_ref[...] = total.astype(jnp.bfloat16)


def on_device(
    gen_hidden,
    gen_out_weight,
    patch_order,
    frame_block,
    embed_weight,
    pos_table,
    norm_gain,
    qkv_weight,
    out_weight,
):
    slots, frames, depth = gen_hidden.shape
    channels, model = embed_weight.shape
    cols = qkv_weight.shape[2]
    out_weight = pltpu.with_memory_space_constraint(out_weight, pltpu.HBM)
    seqs = lax.axis_size("seq")
    group = lax.axis_size(GROUP)
    patches = seqs * slots
    frame_dev = frames // seqs
    window = frame_dev + 2 * REACH
    rows = window * patches
    own_rows = frame_dev * patches
    share = own_rows // group
    f32, bf16 = jnp.float32, jnp.bfloat16
    array = jax.ShapeDtypeStruct
    grant = (16 if rows <= STEP_ROWS else 40) * MIB

    windows = pl.pallas_call(
        functools.partial(latent_kernel, frame_dev),
        out_shape=pltpu.VMEM((group * seqs, slots, window, channels), bf16),
        in_specs=[HBM] * 2,
        out_specs=VMEM,
        scratch_shapes=[
            pltpu.VMEM((slots, frames, depth), bf16),
            pltpu.VMEM((depth, channels), bf16),
            pltpu.VMEM((slots, frames + 2 * REACH, channels), f32),
            pltpu.SemaphoreType.DMA((2,)),
        ],
        compiler_params=pltpu.CompilerParams(vmem_limit_bytes=12 * MIB),
        cost_estimate=pl.CostEstimate(
            flops=20_000_000_000, bytes_accessed=40_000_000, transcendentals=0
        ),
        name="partial_latents",
    )(
        pltpu.with_memory_space_constraint(gen_hidden, pltpu.HBM),
        pltpu.with_memory_space_constraint(gen_out_weight, pltpu.HBM),
    )
    moved = lax.all_to_all(
        windows,
        SCATTERED,
        split_axis=0,
        concat_axis=0,
        tiled=True,
    )

    products = pl.pallas_call(
        functools.partial(weights_kernel, frame_dev, window),
        out_shape=(
            array((3, 2 * channels, cols), bf16),
            array((3, patches, cols), f32),
            array((patches, model), f32),
            array((patches, model), f32),
            array((own_rows, rows), bf16),
            array((own_rows, rows), f32),
            array((channels, model), bf16),
        ),
        in_specs=[SMEM] * 2 + [VMEM] * 2 + [HBM] * 2,
        out_specs=(VMEM,) * 7,
        scratch_shapes=[
            pltpu.VMEM((3, patches, cols), f32),
            pltpu.VMEM((3, model, cols), bf16),
            pltpu.SemaphoreType.DMA((3 * (cols // min(cols, WIDTH)),)),
            pltpu.SemaphoreType.DMA(()),
        ],
        compiler_params=pltpu.CompilerParams(vmem_limit_bytes=24 * MIB),
        cost_estimate=pl.CostEstimate(
            flops=2 * (channels + patches) * model * 3 * cols,
            bytes_accessed=2 * model * 3 * cols,
            transcendentals=0,
        ),
        name="weight_products",
    )(
        patch_order,
        frame_block,
        pos_table,
        norm_gain.reshape(model // LANES, LANES),
        pltpu.with_memory_space_constraint(embed_weight, pltpu.HBM),
        pltpu.with_memory_space_constraint(jnp.transpose(qkv_weight, (1, 0, 2)), pltpu.HBM),
    )

    mixed, mine = pl.pallas_call(
        attend_kernel,
        out_shape=(array((group, share, model), bf16), array((share, model), f32)),
        in_specs=[VMEM] * 8 + [HBM],
        out_specs=(VMEM, VMEM),
        scratch_shapes=[
            pltpu.VMEM((patches, window, channels), f32),
            pltpu.VMEM((patches, window, LANES), f32),
            pltpu.VMEM((group, share, model), f32),
            pltpu.VMEM((cols, model), bf16),
            pltpu.SemaphoreType.DMA(()),
        ],
        compiler_params=pltpu.CompilerParams(vmem_limit_bytes=grant),
        name="attend",
    )(
        moved,
        *products,
        out_weight,
    )
    mixed = lax.all_to_all(mixed, GROUP, split_axis=0, concat_axis=0, tiled=True)
    return pl.pallas_call(
        sum_kernel,
        out_shape=array((share, model), bf16),
        in_specs=[VMEM] * 2,
        out_specs=VMEM,
        compiler_params=pltpu.CompilerParams(vmem_limit_bytes=8 * MIB),
        name="final_sum",
    )(mine, mixed)


def solution(mesh):
    in_specs = (
        P("seq", None, ("mp", "role")),
        P(("mp", "role"), None),
        P(),
        P(),
        P(),
        P(),
        P(),
        P(None, None, ("mp", "role")),
        P(("mp", "role"), None),
    )
    out_specs = P(("seq", "mp", "role"), None)
    return jax.shard_map(
        on_device, mesh=mesh, in_specs=in_specs, out_specs=out_specs, check_vma=False
    )
```

```python
import functools

import jax
import jax.numpy as jnp
from jax import lax
from jax.experimental import pallas as pl
from jax.experimental.pallas import tpu as pltpu
from jax.sharding import PartitionSpec as P

HS = 128
MOSTB = 4
REACH = MOSTB - 1
GROUP = ("mp", "role")
SCATTERED = ("role", "mp", "seq")
LANES = 128
STEP_ROWS = 256
WIDTH = 256
AHEAD = 3
STRIP = 256
MIB = 1024 * 1024
VMEM = pl.BlockSpec(memory_space=pltpu.VMEM)
SMEM = pl.BlockSpec(memory_space=pltpu.SMEM)
HBM = pl.BlockSpec(memory_space=pltpu.HBM)


def dot(a, b):
    return jnp.dot(a, b, preferred_element_type=jnp.float32)


def latent_kernel(
    frame_dev, hidden_hbm, weight_hbm, out_ref, hidden_ref, weight_ref, padded_ref, sems
):
    copies = [
        pltpu.make_async_copy(hidden_hbm, hidden_ref, sems.at[0]),
        pltpu.make_async_copy(weight_hbm, weight_ref, sems.at[1]),
    ]
    for copy in copies:
        copy.start()
    slots, frames, depth = hidden_ref.shape
    everyone, _, window, channels = out_ref.shape
    seqs = frames // frame_dev
    padded_ref[...] = jnp.zeros_like(padded_ref)
    for copy in copies:
        copy.wait()
    for slot in range(slots):
        padded_ref[slot, REACH : REACH + frames] = dot(hidden_ref[slot], weight_ref[...])
    for to in range(seqs):
        piece = padded_ref[:, to * frame_dev : to * frame_dev + window]
        for at in range(to, everyone, seqs):
            out_ref[at] = piece.astype(out_ref.dtype)


def weights_kernel(
    frame_dev,
    window,
    order_ref,
    block_ref,
    pos_ref,
    gain_ref,
    embed_hbm,
    weight_hbm,
    scaled_ref,
    offset_ref,
    pos_slot_ref,
    pos_all_ref,
    select_ref,
    bias_ref,
    embed_ref,
    natural_ref,
    weight_ref,
    sems,
    embed_sem,
):
    channels, model = embed_ref.shape
    patches = pos_ref.shape[0]
    frames = block_ref.shape[0]
    own_rows, rows = bias_ref.shape
    device = lax.axis_index("seq")

    cols = weight_ref.shape[2]
    width = min(cols, WIDTH)
    parts = [(index, at) for index in range(3) for at in range(0, cols, width)]

    def arrival(part):
        index, at = parts[part]
        place = (index, slice(None), pl.ds(at, width))
        return pltpu.make_async_copy(weight_hbm.at[place], weight_ref.at[place], sems.at[part])

    embed_arrival = pltpu.make_async_copy(embed_hbm, embed_ref, embed_sem)
    embed_arrival.start()
    for part in range(AHEAD):
        arrival(part).start()

    pos = pos_ref[...].astype(jnp.float32)
    pos_all_ref[...] = pos

    column = lax.broadcasted_iota(jnp.int32, (1, rows), 1)
    column_slot, column_frame = column // window, column % window

    def patch_at(slot, found):
        return jnp.where(column_slot == slot, order_ref[slot], found)

    column_patch = jnp.zeros((1, rows), jnp.int32)
    if patches <= 16:
        for slot in range(patches):
            column_patch = patch_at(slot, column_patch)
    else:
        column_patch = lax.fori_loop(0, patches, patch_at, column_patch)

    row = lax.broadcasted_iota(jnp.int32, (own_rows, rows), 0)
    hit = jnp.logical_and(column_patch == row % patches, column_frame == row // patches + REACH)
    select_ref[...] = jnp.where(hit, 1.0, 0.0).astype(jnp.bfloat16)

    def block_of(frame):
        inside = jnp.logical_and(frame >= 0, frame < frames)
        return jnp.where(inside, block_ref[jnp.clip(frame, 0, frames - 1)], -1)

    column_block = jnp.full((1, rows), -1, jnp.int32)
    for frame in range(window):
        found = block_of(device * frame_dev - REACH + frame)
        column_block = jnp.where(column_frame == frame, found, column_block)
    row_frame = row // patches
    row_block = jnp.full((own_rows, rows), -2, jnp.int32)
    for frame in range(frame_dev):
        row_block = jnp.where(row_frame == frame, block_of(device * frame_dev + frame), row_block)
    bias_ref[...] = jnp.where(row_block == column_block, 0.0, -1e30)

    gain = jnp.concatenate(
        [gain_ref[at : at + 1, :].astype(jnp.float32) for at in range(model // LANES)], axis=1
    )
    embed_arrival.wait()
    left = jnp.concatenate([embed_ref[...].astype(jnp.float32) * gain, pos * gain], axis=0)
    left = left.astype(jnp.bfloat16)
    for part, (index, at) in enumerate(parts):
        arrival(part).wait()
        if part + AHEAD < len(parts):
            arrival(part + AHEAD).start()
        here = slice(at, at + width)
        both = dot(left, weight_ref[index, :, here])
        scaled = both[:channels]
        high = scaled.astype(jnp.bfloat16)
        scaled_ref[index, :channels, here] = high
        scaled_ref[index, channels:, here] = (scaled - high.astype(jnp.float32)).astype(jnp.bfloat16)
        natural_ref[index, :, here] = both[channels:]

    offset_ref[0] = natural_ref[0]

    def place(slot):
        at = pl.ds(order_ref[slot], 1)
        pos_slot_ref[pl.ds(slot, 1), :] = pos_all_ref[at, :]
        for index in range(1, 3):
            offset_ref[index, pl.ds(slot, 1), :] = natural_ref[index, at, :]

    if patches <= 16:
        for slot in range(patches):
            place(slot)
    else:
        pl.loop(0, patches)(place)


def attend_kernel(
    partial_ref,
    scaled_ref,
    offset_ref,
    pos_slot_ref,
    pos_all_ref,
    select_ref,
    bias_ref,
    embed_ref,
    out_weight_hbm,
    mixed_ref,
    mine_ref,
    latent_ref,
    scale_ref,
    own_ref,
    out_weight_ref,
    sem,
):
    arrival = pltpu.make_async_copy(out_weight_hbm, out_weight_ref, sem)
    arrival.start()
    everyone, slots, window, channels = partial_ref.shape
    group, share, model = mixed_ref.shape
    seqs = everyone // group
    patches = seqs * slots
    rows = patches * window
    own_rows = group * share
    frame_dev = own_rows // patches
    cols = out_weight_ref.shape[0]
    chunk = min(patches, STEP_ROWS // window)

    total = partial_ref[:seqs].astype(jnp.float32)
    for other in range(1, group):
        total = total + partial_ref[other * seqs : (other + 1) * seqs].astype(jnp.float32)
    latent_ref[...] = total.reshape(patches, window, channels)
    latents = total.reshape(rows, channels).astype(jnp.bfloat16)
    own = dot(select_ref[...], latents).astype(jnp.bfloat16)

    def project(index, part):
        return dot(jnp.concatenate([part, part], axis=1), scaled_ref[index])

    def of_window(index):
        flat = project(index, latents).reshape(patches, window, cols)
        flat = flat + offset_ref[index][:, None]
        return flat.reshape(rows, cols).astype(jnp.bfloat16)

    def by_patch(table):
        return jnp.concatenate([table] * frame_dev, axis=0)

    query = (project(0, own) + by_patch(offset_ref[0])).astype(jnp.bfloat16)
    key, value = of_window(1), of_window(2)

    def embedded_strips(lhs, table):
        squares = jnp.zeros((lhs.shape[0], LANES), jnp.float32)
        for at in range(0, model, STRIP):
            strip = dot(lhs, embed_ref[:, at : at + STRIP]) + table(slice(at, at + STRIP))
            for lane in range(0, STRIP, LANES):
                part = strip[:, lane : lane + LANES]
                squares = squares + part * part
            yield at, strip
        mean = jnp.sum(squares, axis=-1, keepdims=True) / model
        yield None, lax.rsqrt(mean + 1e-06)

    def pos_of_window(start, at):
        part = pos_slot_ref[pl.ds(start, chunk), at][:, None]
        return jnp.broadcast_to(part, (chunk, window, STRIP)).reshape(chunk * window, STRIP)

    def pos_of_own(at):
        return by_patch(pos_all_ref[:, at])

    def keep_window(start, scale):
        scale = jnp.broadcast_to(scale, (chunk * window, LANES)).reshape(chunk, window, LANES)
        scale_ref[pl.ds(start, chunk)] = scale

    def keep_own(at, strip):
        for other in range(group):
            own_ref[other, :, at : at + STRIP] = strip[other * share : (other + 1) * share]

    if chunk == patches:
        lhs = jnp.concatenate([latents, own], axis=0)

        def pos_of_both(at):
            return jnp.concatenate([pos_of_window(0, at), pos_of_own(at)], axis=0)

        for at, strip in embedded_strips(lhs, pos_of_both):
            if at is None:
                keep_window(0, strip[:rows])
                row_scale = strip[rows:]
            else:
                keep_own(at, strip[rows:])
    else:

        @pl.loop(0, patches // chunk)
        def _(step):
            start = step * chunk
            part = latent_ref[pl.ds(start, chunk)].reshape(chunk * window, channels)
            strips = embedded_strips(
                part.astype(jnp.bfloat16), functools.partial(pos_of_window, start)
            )
            for at, strip in strips:
                if at is None:
                    keep_window(start, strip)

        for at, strip in embedded_strips(own, pos_of_own):
            if at is None:
                row_scale = strip
            else:
                keep_own(at, strip)

    row_scale = row_scale * (HS**-0.5)
    column_scale = jnp.transpose(scale_ref[...].reshape(rows, LANES))[:1]
    factor = row_scale * column_scale
    bias = bias_ref[...]
    heads = []
    for head in range(cols // HS):
        at = slice(head * HS, (head + 1) * HS)
        scores = lax.dot_general(
            query[:, at], key[:, at], (((1,), (1,)), ((), ())), preferred_element_type=jnp.float32
        )
        scores = scores * factor + bias
        expo = jnp.exp(scores - jnp.max(scores, axis=-1, keepdims=True))
        probs = expo * (column_scale / jnp.sum(expo, axis=-1, keepdims=True))
        heads.append(dot(probs.astype(jnp.bfloat16), value[:, at]).astype(jnp.bfloat16))
    mine_ref[...] = own_ref[lax.axis_index(GROUP)]
    heads = jnp.concatenate(heads, axis=1)
    arrival.wait()
    for at in range(0, model, STRIP):
        here = slice(at, at + STRIP)
        mixed = dot(heads, out_weight_ref[:, here]).astype(jnp.bfloat16)
        for other in range(group):
            mixed_ref[other, :, here] = mixed[other * share : (other + 1) * share]


def sum_kernel(mine_ref, mixed_ref, out_ref):
    total = mine_ref[...]
    for member in range(mixed_ref.shape[0]):
        total = total + mixed_ref[member].astype(jnp.float32)
    out_ref[...] = total.astype(jnp.bfloat16)


def on_device(
    gen_hidden,
    gen_out_weight,
    patch_order,
    frame_block,
    embed_weight,
    pos_table,
    norm_gain,
    qkv_weight,
    out_weight,
):
    slots, frames, depth = gen_hidden.shape
    channels, model = embed_weight.shape
    cols = qkv_weight.shape[2]
    out_weight = pltpu.with_memory_space_constraint(out_weight, pltpu.HBM)
    seqs = lax.axis_size("seq")
    group = lax.axis_size(GROUP)
    patches = seqs * slots
    frame_dev = frames // seqs
    window = frame_dev + 2 * REACH
    rows = window * patches
    own_rows = frame_dev * patches
    share = own_rows // group
    f32, bf16 = jnp.float32, jnp.bfloat16
    array = jax.ShapeDtypeStruct
    grant = (16 if rows <= STEP_ROWS else 40) * MIB

    windows = pl.pallas_call(
        functools.partial(latent_kernel, frame_dev),
        out_shape=pltpu.VMEM((group * seqs, slots, window, channels), bf16),
        in_specs=[HBM] * 2,
        out_specs=VMEM,
        scratch_shapes=[
            pltpu.VMEM((slots, frames, depth), bf16),
            pltpu.VMEM((depth, channels), bf16),
            pltpu.VMEM((slots, frames + 2 * REACH, channels), f32),
            pltpu.SemaphoreType.DMA((2,)),
        ],
        compiler_params=pltpu.CompilerParams(vmem_limit_bytes=12 * MIB),
        cost_estimate=pl.CostEstimate(
            flops=20_000_000_000, bytes_accessed=40_000_000, transcendentals=0
        ),
        name="partial_latents",
    )(
        pltpu.with_memory_space_constraint(gen_hidden, pltpu.HBM),
        pltpu.with_memory_space_constraint(gen_out_weight, pltpu.HBM),
    )
    moved = lax.all_to_all(
        windows,
        SCATTERED,
        split_axis=0,
        concat_axis=0,
        tiled=True,
    )

    products = pl.pallas_call(
        functools.partial(weights_kernel, frame_dev, window),
        out_shape=(
            array((3, 2 * channels, cols), bf16),
            array((3, patches, cols), f32),
            array((patches, model), f32),
            array((patches, model), f32),
            array((own_rows, rows), bf16),
            array((own_rows, rows), f32),
            array((channels, model), bf16),
        ),
        in_specs=[SMEM] * 2 + [VMEM] * 2 + [HBM] * 2,
        out_specs=(VMEM,) * 7,
        scratch_shapes=[
            pltpu.VMEM((3, patches, cols), f32),
            pltpu.VMEM((3, model, cols), bf16),
            pltpu.SemaphoreType.DMA((3 * (cols // min(cols, WIDTH)),)),
            pltpu.SemaphoreType.DMA(()),
        ],
        compiler_params=pltpu.CompilerParams(vmem_limit_bytes=24 * MIB),
        cost_estimate=pl.CostEstimate(
            flops=2 * (channels + patches) * model * 3 * cols,
            bytes_accessed=2 * model * 3 * cols,
            transcendentals=0,
        ),
        name="weight_products",
    )(
        patch_order,
        frame_block,
        pos_table,
        norm_gain.reshape(model // LANES, LANES),
        pltpu.with_memory_space_constraint(embed_weight, pltpu.HBM),
        pltpu.with_memory_space_constraint(jnp.transpose(qkv_weight, (1, 0, 2)), pltpu.HBM),
    )

    mixed, mine = pl.pallas_call(
        attend_kernel,
        out_shape=(array((group, share, model), bf16), array((share, model), f32)),
        in_specs=[VMEM] * 8 + [HBM],
        out_specs=(VMEM, VMEM),
        scratch_shapes=[
            pltpu.VMEM((patches, window, channels), f32),
            pltpu.VMEM((patches, window, LANES), f32),
            pltpu.VMEM((group, share, model), f32),
            pltpu.VMEM((cols, model), bf16),
            pltpu.SemaphoreType.DMA(()),
        ],
        compiler_params=pltpu.CompilerParams(vmem_limit_bytes=grant),
        name="attend",
    )(
        moved,
        *products,
        out_weight,
    )
    mixed = lax.all_to_all(mixed, GROUP, split_axis=0, concat_axis=0, tiled=True)
    return pl.pallas_call(
        sum_kernel,
        out_shape=array((share, model), bf16),
        in_specs=[VMEM] * 2,
        out_specs=VMEM,
        compiler_params=pltpu.CompilerParams(vmem_limit_bytes=8 * MIB),
        name="final_sum",
    )(mine, mixed)


def solution(mesh):
    in_specs = (
        P("seq", None, ("mp", "role")),
        P(("mp", "role"), None),
        P(),
        P(),
        P(),
        P(),
        P(),
        P(None, None, ("mp", "role")),
        P(("mp", "role"), None),
    )
    out_specs = P(("seq", "mp", "role"), None)
    return jax.shard_map(
        on_device, mesh=mesh, in_specs=in_specs, out_specs=out_specs, check_vma=False
    )
```

```python
import functools

import jax
import jax.numpy as jnp
from jax import lax
from jax.experimental import pallas as pl
from jax.experimental.pallas import tpu as pltpu
from jax.sharding import PartitionSpec as P

HS = 128
MOSTB = 4
REACH = MOSTB - 1
GROUP = ("mp", "role")
SCATTERED = ("role", "mp", "seq")
LANES = 128
STEP_ROWS = 256
DEPTH = 1024
AHEAD = 4
STRIP = 256
MIB = 1024 * 1024
VMEM = pl.BlockSpec(memory_space=pltpu.VMEM)
SMEM = pl.BlockSpec(memory_space=pltpu.SMEM)
HBM = pl.BlockSpec(memory_space=pltpu.HBM)


def dot(a, b):
    return jnp.dot(a, b, preferred_element_type=jnp.float32)


def latent_kernel(
    frame_dev, hidden_hbm, weight_hbm, out_ref, hidden_ref, weight_ref, padded_ref, sems
):
    copies = [
        pltpu.make_async_copy(hidden_hbm, hidden_ref, sems.at[0]),
        pltpu.make_async_copy(weight_hbm, weight_ref, sems.at[1]),
    ]
    for copy in copies:
        copy.start()
    slots, frames, depth = hidden_ref.shape
    everyone, _, window, channels = out_ref.shape
    seqs = frames // frame_dev
    padded_ref[...] = jnp.zeros_like(padded_ref)
    for copy in copies:
        copy.wait()
    for slot in range(slots):
        padded_ref[slot, REACH : REACH + frames] = dot(hidden_ref[slot], weight_ref[...])
    for to in range(seqs):
        piece = padded_ref[:, to * frame_dev : to * frame_dev + window]
        for at in range(to, everyone, seqs):
            out_ref[at] = piece.astype(out_ref.dtype)


def weights_kernel(
    frame_dev,
    window,
    order_ref,
    block_ref,
    embed_ref,
    pos_ref,
    gain_ref,
    weight_hbm,
    scaled_ref,
    offset_ref,
    pos_slot_ref,
    pos_mine_ref,
    select_ref,
    select_mine_ref,
    bias_ref,
    natural_ref,
    pos_all_ref,
    weight_ref,
    sems,
):
    channels, model = embed_ref.shape
    patches = pos_ref.shape[0]
    frames = block_ref.shape[0]
    own_rows, rows = bias_ref.shape
    share = select_mine_ref.shape[0]
    device = lax.axis_index("seq")
    member = lax.axis_index(GROUP)

    deep = min(model, DEPTH)
    parts = [(index, at) for index in range(3) for at in range(0, model, deep)]

    def arrival(part):
        index, at = parts[part]
        place = (index, pl.ds(at, deep))
        return pltpu.make_async_copy(weight_hbm.at[place], weight_ref.at[place], sems.at[part])

    for part in range(AHEAD):
        arrival(part).start()

    pos = pos_ref[...].astype(jnp.float32)
    pos_all_ref[...] = pos

    column = lax.broadcasted_iota(jnp.int32, (1, rows), 1)
    column_slot, column_frame = column // window, column % window

    def patch_at(slot, found):
        return jnp.where(column_slot == slot, order_ref[slot], found)

    column_patch = jnp.zeros((1, rows), jnp.int32)
    if patches <= 16:
        for slot in range(patches):
            column_patch = patch_at(slot, column_patch)
    else:
        column_patch = lax.fori_loop(0, patches, patch_at, column_patch)

    def select(count, first):
        row = lax.broadcasted_iota(jnp.int32, (count, rows), 0) + first
        hit = jnp.logical_and(
            column_patch == row % patches, column_frame == row // patches + REACH
        )
        return jnp.where(hit, 1.0, 0.0).astype(jnp.bfloat16)

    select_ref[...] = select(own_rows, 0)
    select_mine_ref[...] = select(share, member * share)
    for frame in range(frame_dev * patches // share):
        row = frame * share

        @pl.when(member == frame)
        def _():
            for at in range(share):
                mine = (row + at) % patches
                pos_mine_ref[at : at + 1, :] = pos_all_ref[mine : mine + 1, :]

    def block_of(frame):
        inside = jnp.logical_and(frame >= 0, frame < frames)
        return jnp.where(inside, block_ref[jnp.clip(frame, 0, frames - 1)], -1)

    column_block = jnp.full((1, rows), -1, jnp.int32)
    for frame in range(window):
        found = block_of(device * frame_dev - REACH + frame)
        column_block = jnp.where(column_frame == frame, found, column_block)
    row_frame = lax.broadcasted_iota(jnp.int32, (own_rows, rows), 0) // patches
    row_block = jnp.full((own_rows, rows), -2, jnp.int32)
    for frame in range(frame_dev):
        row_block = jnp.where(row_frame == frame, block_of(device * frame_dev + frame), row_block)
    bias_ref[...] = jnp.where(row_block == column_block, 0.0, -1e30)

    gain = jnp.concatenate(
        [gain_ref[at : at + 1, :].astype(jnp.float32) for at in range(model // LANES)], axis=1
    )
    left = jnp.concatenate([embed_ref[...].astype(jnp.float32) * gain, pos * gain], axis=0)
    left = left.astype(jnp.bfloat16)
    for part, (index, at) in enumerate(parts):
        arrival(part).wait()
        if part + AHEAD < len(parts):
            arrival(part + AHEAD).start()
        here = slice(at, at + deep)
        product = dot(left[:, here], weight_ref[index, here])
        both = product if at == 0 else both + product
        if at + deep == model:
            scaled = both[:channels]
            high = scaled.astype(jnp.bfloat16)
            scaled_ref[index, :channels] = high
            scaled_ref[index, channels:] = (scaled - high.astype(jnp.float32)).astype(jnp.bfloat16)
            natural_ref[index] = both[channels:]

    def place(slot):
        at = pl.ds(order_ref[slot], 1)
        pos_slot_ref[pl.ds(slot, 1), :] = pos_all_ref[at, :]
        for index in range(3):
            offset_ref[index, pl.ds(slot, 1), :] = natural_ref[index, at, :]

    if patches <= 16:
        for slot in range(patches):
            place(slot)
    else:
        pl.loop(0, patches)(place)


def attend_kernel(
    partial_ref,
    embed_ref,
    scaled_ref,
    offset_ref,
    pos_slot_ref,
    pos_mine_ref,
    select_ref,
    select_mine_ref,
    bias_ref,
    out_weight_hbm,
    mixed_ref,
    mine_ref,
    latent_ref,
    scale_ref,
    out_weight_ref,
    sem,
):
    arrival = pltpu.make_async_copy(out_weight_hbm, out_weight_ref, sem)
    arrival.start()
    everyone, slots, window, channels = partial_ref.shape
    group = mixed_ref.shape[0]
    seqs = everyone // group
    patches = seqs * slots
    rows = patches * window
    share, model = mine_ref.shape
    cols = out_weight_ref.shape[0]

    total = partial_ref[:seqs].astype(jnp.float32)
    for other in range(1, group):
        total = total + partial_ref[other * seqs : (other + 1) * seqs].astype(jnp.float32)
    latent_ref[...] = total.reshape(patches, window, channels)
    chunk = min(patches, STEP_ROWS // window)

    def measure(step):
        here = pl.ds(step * chunk, chunk)
        part = latent_ref[here].reshape(chunk * window, channels).astype(jnp.bfloat16)
        squares = jnp.zeros((chunk, window, LANES), jnp.float32)
        for at in range(0, model, STRIP):
            strip = dot(part, embed_ref[:, at : at + STRIP]).reshape(chunk, window, STRIP)
            strip = strip + pos_slot_ref[here, at : at + STRIP][:, None]
            for lane in range(0, STRIP, LANES):
                piece = strip[:, :, lane : lane + LANES]
                squares = squares + piece * piece
        mean = jnp.sum(squares, axis=-1, keepdims=True) / model
        scale_ref[here] = jnp.broadcast_to(lax.rsqrt(mean + 1e-06), (chunk, window, LANES))

    if chunk == patches:
        measure(0)
    else:
        pl.loop(0, patches // chunk)(measure)

    latents = latent_ref[...].reshape(rows, channels).astype(jnp.bfloat16)
    twice = jnp.concatenate([latents, latents], axis=1)
    scale = scale_ref[...].reshape(rows, LANES)[:, :1]

    def project(index):
        flat = dot(twice, scaled_ref[index]).reshape(patches, window, cols)
        flat = (flat + offset_ref[index][:, None]).reshape(rows, cols)
        return (flat * scale).astype(jnp.bfloat16)

    query = dot(select_ref[...], project(0)).astype(jnp.bfloat16)
    key, value = project(1), project(2)
    bias = bias_ref[...]
    heads = []
    for head in range(cols // HS):
        at = slice(head * HS, (head + 1) * HS)
        scores = lax.dot_general(
            query[:, at], key[:, at], (((1,), (1,)), ((), ())), preferred_element_type=jnp.float32
        )
        scores = scores * (HS**-0.5) + bias
        expo = jnp.exp(scores - jnp.max(scores, axis=-1, keepdims=True))
        probs = (expo / jnp.sum(expo, axis=-1, keepdims=True)).astype(jnp.bfloat16)
        heads.append(dot(probs, value[:, at]).astype(jnp.bfloat16))
    mine = dot(select_mine_ref[...], latents).astype(jnp.bfloat16)
    mine_ref[...] = dot(mine, embed_ref[...]) + pos_mine_ref[...]
    arrival.wait()
    mixed = dot(jnp.concatenate(heads, axis=1), out_weight_ref[...])
    for other in range(group):
        mixed_ref[other] = mixed[other * share : (other + 1) * share].astype(jnp.bfloat16)


def sum_kernel(mine_ref, mixed_ref, out_ref):
    total = mine_ref[...]
    for member in range(mixed_ref.shape[0]):
        total = total + mixed_ref[member].astype(jnp.float32)
    out_ref[...] = total.astype(jnp.bfloat16)


def on_device(
    gen_hidden,
    gen_out_weight,
    patch_order,
    frame_block,
    embed_weight,
    pos_table,
    norm_gain,
    qkv_weight,
    out_weight,
):
    slots, frames, depth = gen_hidden.shape
    channels, model = embed_weight.shape
    cols = qkv_weight.shape[2]
    out_weight = pltpu.with_memory_space_constraint(out_weight, pltpu.HBM)
    seqs = lax.axis_size("seq")
    group = lax.axis_size(GROUP)
    patches = seqs * slots
    frame_dev = frames // seqs
    window = frame_dev + 2 * REACH
    rows = window * patches
    own_rows = frame_dev * patches
    share = own_rows // group
    f32, bf16 = jnp.float32, jnp.bfloat16
    array = jax.ShapeDtypeStruct
    grant = (16 if rows <= STEP_ROWS else 40) * MIB

    windows = pl.pallas_call(
        functools.partial(latent_kernel, frame_dev),
        out_shape=pltpu.VMEM((group * seqs, slots, window, channels), bf16),
        in_specs=[HBM] * 2,
        out_specs=VMEM,
        scratch_shapes=[
            pltpu.VMEM((slots, frames, depth), bf16),
            pltpu.VMEM((depth, channels), bf16),
            pltpu.VMEM((slots, frames + 2 * REACH, channels), f32),
            pltpu.SemaphoreType.DMA((2,)),
        ],
        compiler_params=pltpu.CompilerParams(vmem_limit_bytes=12 * MIB),
        cost_estimate=pl.CostEstimate(
            flops=20_000_000_000, bytes_accessed=40_000_000, transcendentals=0
        ),
        name="partial_latents",
    )(
        pltpu.with_memory_space_constraint(gen_hidden, pltpu.HBM),
        pltpu.with_memory_space_constraint(gen_out_weight, pltpu.HBM),
    )
    moved = lax.all_to_all(
        windows,
        SCATTERED,
        split_axis=0,
        concat_axis=0,
        tiled=True,
    )

    products = pl.pallas_call(
        functools.partial(weights_kernel, frame_dev, window),
        out_shape=(
            array((3, 2 * channels, cols), bf16),
            array((3, patches, cols), f32),
            array((patches, model), f32),
            array((share, model), f32),
            array((own_rows, rows), bf16),
            array((share, rows), bf16),
            array((own_rows, rows), f32),
        ),
        in_specs=[SMEM] * 2 + [VMEM] * 3 + [HBM],
        out_specs=(VMEM,) * 7,
        scratch_shapes=[
            pltpu.VMEM((3, patches, cols), f32),
            pltpu.VMEM((patches, model), f32),
            pltpu.VMEM((3, model, cols), bf16),
            pltpu.SemaphoreType.DMA((3 * (model // min(model, DEPTH)),)),
        ],
        compiler_params=pltpu.CompilerParams(vmem_limit_bytes=24 * MIB),
        cost_estimate=pl.CostEstimate(
            flops=2 * (channels + patches) * model * 3 * cols,
            bytes_accessed=2 * model * 3 * cols,
            transcendentals=0,
        ),
        name="weight_products",
    )(
        patch_order,
        frame_block,
        embed_weight,
        pos_table,
        norm_gain.reshape(model // LANES, LANES),
        pltpu.with_memory_space_constraint(jnp.transpose(qkv_weight, (1, 0, 2)), pltpu.HBM),
    )

    mixed, mine = pl.pallas_call(
        attend_kernel,
        out_shape=(array((group, share, model), bf16), array((share, model), f32)),
        in_specs=[VMEM] * 9 + [HBM],
        out_specs=(VMEM, VMEM),
        scratch_shapes=[
            pltpu.VMEM((patches, window, channels), f32),
            pltpu.VMEM((patches, window, LANES), f32),
            pltpu.VMEM((cols, model), bf16),
            pltpu.SemaphoreType.DMA(()),
        ],
        compiler_params=pltpu.CompilerParams(vmem_limit_bytes=grant),
        name="attend",
    )(
        moved,
        embed_weight,
        *products,
        out_weight,
    )
    mixed = lax.all_to_all(mixed, GROUP, split_axis=0, concat_axis=0, tiled=True)
    return pl.pallas_call(
        sum_kernel,
        out_shape=array((share, model), bf16),
        in_specs=[VMEM] * 2,
        out_specs=VMEM,
        compiler_params=pltpu.CompilerParams(vmem_limit_bytes=8 * MIB),
        name="final_sum",
    )(mine, mixed)


def solution(mesh):
    in_specs = (
        P("seq", None, ("mp", "role")),
        P(("mp", "role"), None),
        P(),
        P(),
        P(),
        P(),
        P(),
        P(None, None, ("mp", "role")),
        P(("mp", "role"), None),
    )
    out_specs = P(("seq", "mp", "role"), None)
    return jax.shard_map(
        on_device, mesh=mesh, in_specs=in_specs, out_specs=out_specs, check_vma=False
    )
```

```python
import functools

import jax
import jax.numpy as jnp
from jax import lax
from jax.experimental import pallas as pl
from jax.experimental.pallas import tpu as pltpu
from jax.sharding import PartitionSpec as P

HS = 128
MOSTB = 4
REACH = MOSTB - 1
GROUP = ("mp", "role")
SCATTERED = ("role", "mp", "seq")
LANES = 128
STEP_ROWS = 256
DEPTH = 1024
AHEAD = 4
STRIP = 512
MIB = 1024 * 1024
VMEM = pl.BlockSpec(memory_space=pltpu.VMEM)
SMEM = pl.BlockSpec(memory_space=pltpu.SMEM)
HBM = pl.BlockSpec(memory_space=pltpu.HBM)


def dot(a, b):
    return jnp.dot(a, b, preferred_element_type=jnp.float32)


def latent_kernel(
    frame_dev, hidden_hbm, weight_hbm, out_ref, hidden_ref, weight_ref, padded_ref, sems
):
    copies = [
        pltpu.make_async_copy(hidden_hbm, hidden_ref, sems.at[0]),
        pltpu.make_async_copy(weight_hbm, weight_ref, sems.at[1]),
    ]
    for copy in copies:
        copy.start()
    slots, frames, depth = hidden_ref.shape
    everyone, _, window, channels = out_ref.shape
    seqs = frames // frame_dev
    padded_ref[...] = jnp.zeros_like(padded_ref)
    for copy in copies:
        copy.wait()
    for slot in range(slots):
        padded_ref[slot, REACH : REACH + frames] = dot(hidden_ref[slot], weight_ref[...])
    for to in range(seqs):
        piece = padded_ref[:, to * frame_dev : to * frame_dev + window]
        for at in range(to, everyone, seqs):
            out_ref[at] = piece.astype(out_ref.dtype)


def weights_kernel(
    frame_dev,
    window,
    order_ref,
    block_ref,
    embed_ref,
    pos_ref,
    gain_ref,
    weight_hbm,
    out_weight_hbm,
    scaled_ref,
    offset_ref,
    gram_ref,
    cross_ref,
    level_ref,
    pos_mine_ref,
    select_ref,
    select_mine_ref,
    bias_ref,
    first_ref,
    natural_ref,
    natural_cross_ref,
    natural_level_ref,
    pos_all_ref,
    weight_ref,
    sems,
    first_sem,
):
    channels, model = embed_ref.shape
    patches = pos_ref.shape[0]
    frames = block_ref.shape[0]
    own_rows, rows = bias_ref.shape
    share = select_mine_ref.shape[0]
    device = lax.axis_index("seq")
    member = lax.axis_index(GROUP)

    deep = min(model, DEPTH)
    parts = [(index, at) for index in range(3) for at in range(0, model, deep)]

    def arrival(part):
        index, at = parts[part]
        place = (index, pl.ds(at, deep))
        return pltpu.make_async_copy(weight_hbm.at[place], weight_ref.at[place], sems.at[part])

    first = pltpu.make_async_copy(
        out_weight_hbm.at[pl.ds(0, first_ref.shape[0])], first_ref, first_sem
    )
    for part in range(AHEAD):
        arrival(part).start()

    pos = pos_ref[...].astype(jnp.float32)
    pos_all_ref[...] = pos

    column = lax.broadcasted_iota(jnp.int32, (1, rows), 1)
    column_slot, column_frame = column // window, column % window

    def patch_at(slot, found):
        return jnp.where(column_slot == slot, order_ref[slot], found)

    column_patch = jnp.zeros((1, rows), jnp.int32)
    if patches <= 16:
        for slot in range(patches):
            column_patch = patch_at(slot, column_patch)
    else:
        column_patch = lax.fori_loop(0, patches, patch_at, column_patch)

    def select(count, first):
        row = lax.broadcasted_iota(jnp.int32, (count, rows), 0) + first
        hit = jnp.logical_and(
            column_patch == row % patches, column_frame == row // patches + REACH
        )
        return jnp.where(hit, 1.0, 0.0).astype(jnp.bfloat16)

    select_ref[...] = select(own_rows, 0)
    select_mine_ref[...] = select(share, member * share)
    for frame in range(frame_dev * patches // share):
        row = frame * share

        @pl.when(member == frame)
        def _():
            for at in range(share):
                mine = (row + at) % patches
                pos_mine_ref[at : at + 1, :] = pos_all_ref[mine : mine + 1, :]

    def block_of(frame):
        inside = jnp.logical_and(frame >= 0, frame < frames)
        return jnp.where(inside, block_ref[jnp.clip(frame, 0, frames - 1)], -1)

    column_block = jnp.full((1, rows), -1, jnp.int32)
    for frame in range(window):
        found = block_of(device * frame_dev - REACH + frame)
        column_block = jnp.where(column_frame == frame, found, column_block)
    row_frame = lax.broadcasted_iota(jnp.int32, (own_rows, rows), 0) // patches
    row_block = jnp.full((own_rows, rows), -2, jnp.int32)
    for frame in range(frame_dev):
        row_block = jnp.where(row_frame == frame, block_of(device * frame_dev + frame), row_block)
    bias_ref[...] = jnp.where(row_block == column_block, 0.0, -1e30)

    gain = jnp.concatenate(
        [gain_ref[at : at + 1, :].astype(jnp.float32) for at in range(model // LANES)], axis=1
    )
    left = jnp.concatenate([embed_ref[...].astype(jnp.float32) * gain, pos * gain], axis=0)
    left = left.astype(jnp.bfloat16)
    def keep(ref, scaled):
        high = scaled.astype(jnp.bfloat16)
        ref[:channels] = high
        ref[channels:] = (scaled - high.astype(jnp.float32)).astype(jnp.bfloat16)

    plain = jnp.concatenate([embed_ref[...], pos_ref[...]], axis=0)
    both = lax.dot_general(
        plain, embed_ref[...], (((1,), (1,)), ((), ())), preferred_element_type=jnp.float32
    )
    keep(gram_ref, both[:channels])
    natural_cross_ref[...] = 2.0 * both[channels:]
    level = jnp.sum(pos * pos, axis=-1, keepdims=True) / channels
    natural_level_ref[...] = jnp.broadcast_to(level, (patches, channels))

    for part, (index, at) in enumerate(parts):
        arrival(part).wait()
        if part + AHEAD < len(parts):
            arrival(part + AHEAD).start()
        if part + AHEAD == len(parts) - 1:
            first.start()
        here = slice(at, at + deep)
        product = dot(left[:, here], weight_ref[index, here])
        both = product if at == 0 else both + product
        if at + deep == model:
            keep(scaled_ref.at[index], both[:channels])
            natural_ref[index] = both[channels:]

    def place(slot):
        to, at = pl.ds(slot, 1), pl.ds(order_ref[slot], 1)
        cross_ref[to, :] = natural_cross_ref[at, :]
        level_ref[to, :] = natural_level_ref[at, :]
        for index in range(3):
            offset_ref[index, to, :] = natural_ref[index, at, :]

    if patches <= 16:
        for slot in range(patches):
            place(slot)
    else:
        pl.loop(0, patches)(place)
    first.wait()


def attend_kernel(
    partial_ref,
    embed_ref,
    scaled_ref,
    offset_ref,
    gram_ref,
    cross_ref,
    level_ref,
    pos_mine_ref,
    select_ref,
    select_mine_ref,
    bias_ref,
    first_ref,
    out_weight_hbm,
    mixed_ref,
    mine_ref,
    second_ref,
    sem,
):
    half = first_ref.shape[0]
    arrival = pltpu.make_async_copy(out_weight_hbm.at[pl.ds(half, half)], second_ref, sem)
    arrival.start()
    everyone, slots, window, channels = partial_ref.shape
    group, share, model = mixed_ref.shape
    seqs = everyone // group
    patches = seqs * slots
    rows = patches * window
    cols = out_weight_hbm.shape[0]

    total = partial_ref[:seqs].astype(jnp.float32)
    for other in range(1, group):
        total = total + partial_ref[other * seqs : (other + 1) * seqs].astype(jnp.float32)
    latents = total.reshape(rows, channels).astype(jnp.bfloat16)
    twice = jnp.concatenate([latents, latents], axis=1)
    slope = dot(twice, gram_ref[...]).reshape(patches, window, channels)
    slope = slope + cross_ref[...][:, None]
    squares = slope * latents.astype(jnp.float32).reshape(patches, window, channels)
    squares = (squares + level_ref[...][:, None]).reshape(rows, channels)
    mean = jnp.maximum(jnp.sum(squares, axis=-1, keepdims=True), 0.0) / model
    scale = lax.rsqrt(mean + 1e-06)

    def project(index):
        flat = dot(twice, scaled_ref[index]).reshape(patches, window, cols)
        flat = (flat + offset_ref[index][:, None]).reshape(rows, cols)
        return (flat * scale).astype(jnp.bfloat16)

    query = dot(select_ref[...], project(0)).astype(jnp.bfloat16)
    key, value = project(1), project(2)
    bias = bias_ref[...]
    heads = []
    for head in range(cols // HS):
        at = slice(head * HS, (head + 1) * HS)
        scores = lax.dot_general(
            query[:, at], key[:, at], (((1,), (1,)), ((), ())), preferred_element_type=jnp.float32
        )
        scores = scores * (HS**-0.5) + bias
        expo = jnp.exp(scores - jnp.max(scores, axis=-1, keepdims=True))
        probs = (expo / jnp.sum(expo, axis=-1, keepdims=True)).astype(jnp.bfloat16)
        heads.append(dot(probs, value[:, at]).astype(jnp.bfloat16))
    mine = dot(select_mine_ref[...], latents).astype(jnp.bfloat16)
    mine_ref[...] = dot(mine, embed_ref[...]) + pos_mine_ref[...]
    heads = jnp.concatenate(heads, axis=1)
    arrival.wait()
    for at in range(0, model, STRIP):
        here = slice(at, at + STRIP)
        mixed = dot(heads[:, :half], first_ref[:, here]) + dot(heads[:, half:], second_ref[:, here])
        mixed = mixed.astype(jnp.bfloat16)
        for other in range(group):
            mixed_ref[other, :, here] = mixed[other * share : (other + 1) * share]


def sum_kernel(mine_ref, mixed_ref, out_ref):
    total = mine_ref[...]
    for member in range(mixed_ref.shape[0]):
        total = total + mixed_ref[member].astype(jnp.float32)
    out_ref[...] = total.astype(jnp.bfloat16)


def on_device(
    gen_hidden,
    gen_out_weight,
    patch_order,
    frame_block,
    embed_weight,
    pos_table,
    norm_gain,
    qkv_weight,
    out_weight,
):
    slots, frames, depth = gen_hidden.shape
    channels, model = embed_weight.shape
    cols = qkv_weight.shape[2]
    out_weight = pltpu.with_memory_space_constraint(out_weight, pltpu.HBM)
    seqs = lax.axis_size("seq")
    group = lax.axis_size(GROUP)
    patches = seqs * slots
    frame_dev = frames // seqs
    window = frame_dev + 2 * REACH
    rows = window * patches
    own_rows = frame_dev * patches
    share = own_rows // group
    f32, bf16 = jnp.float32, jnp.bfloat16
    array = jax.ShapeDtypeStruct
    grant = (16 if rows <= STEP_ROWS else 40) * MIB

    windows = pl.pallas_call(
        functools.partial(latent_kernel, frame_dev),
        out_shape=pltpu.VMEM((group * seqs, slots, window, channels), bf16),
        in_specs=[HBM] * 2,
        out_specs=VMEM,
        scratch_shapes=[
            pltpu.VMEM((slots, frames, depth), bf16),
            pltpu.VMEM((depth, channels), bf16),
            pltpu.VMEM((slots, frames + 2 * REACH, channels), f32),
            pltpu.SemaphoreType.DMA((2,)),
        ],
        compiler_params=pltpu.CompilerParams(vmem_limit_bytes=12 * MIB),
        cost_estimate=pl.CostEstimate(
            flops=20_000_000_000, bytes_accessed=40_000_000, transcendentals=0
        ),
        name="partial_latents",
    )(
        pltpu.with_memory_space_constraint(gen_hidden, pltpu.HBM),
        pltpu.with_memory_space_constraint(gen_out_weight, pltpu.HBM),
    )
    moved = lax.all_to_all(
        windows,
        SCATTERED,
        split_axis=0,
        concat_axis=0,
        tiled=True,
    )

    products = pl.pallas_call(
        functools.partial(weights_kernel, frame_dev, window),
        out_shape=(
            array((3, 2 * channels, cols), bf16),
            array((3, patches, cols), f32),
            array((2 * channels, channels), bf16),
            array((patches, channels), f32),
            array((patches, channels), f32),
            array((share, model), f32),
            array((own_rows, rows), bf16),
            array((share, rows), bf16),
            array((own_rows, rows), f32),
            array((cols // 2, model), bf16),
        ),
        in_specs=[SMEM] * 2 + [VMEM] * 3 + [HBM] * 2,
        out_specs=(VMEM,) * 10,
        scratch_shapes=[
            pltpu.VMEM((3, patches, cols), f32),
            pltpu.VMEM((patches, channels), f32),
            pltpu.VMEM((patches, channels), f32),
            pltpu.VMEM((patches, model), f32),
            pltpu.VMEM((3, model, cols), bf16),
            pltpu.SemaphoreType.DMA((3 * (model // min(model, DEPTH)),)),
            pltpu.SemaphoreType.DMA(()),
        ],
        compiler_params=pltpu.CompilerParams(vmem_limit_bytes=24 * MIB),
        cost_estimate=pl.CostEstimate(
            flops=2 * (channels + patches) * model * 3 * cols,
            bytes_accessed=2 * model * 3 * cols,
            transcendentals=0,
        ),
        name="weight_products",
    )(
        patch_order,
        frame_block,
        embed_weight,
        pos_table,
        norm_gain.reshape(model // LANES, LANES),
        pltpu.with_memory_space_constraint(jnp.transpose(qkv_weight, (1, 0, 2)), pltpu.HBM),
        out_weight,
    )

    mixed, mine = pl.pallas_call(
        attend_kernel,
        out_shape=(array((group, share, model), bf16), array((share, model), f32)),
        in_specs=[VMEM] * 12 + [HBM],
        out_specs=(VMEM, VMEM),
        scratch_shapes=[
            pltpu.VMEM((cols - cols // 2, model), bf16),
            pltpu.SemaphoreType.DMA(()),
        ],
        compiler_params=pltpu.CompilerParams(vmem_limit_bytes=grant),
        name="attend",
    )(
        moved,
        embed_weight,
        *products,
        out_weight,
    )
    mixed = lax.all_to_all(mixed, GROUP, split_axis=0, concat_axis=0, tiled=True)
    return pl.pallas_call(
        sum_kernel,
        out_shape=array((share, model), bf16),
        in_specs=[VMEM] * 2,
        out_specs=VMEM,
        compiler_params=pltpu.CompilerParams(vmem_limit_bytes=8 * MIB),
        name="final_sum",
    )(mine, mixed)


def solution(mesh):
    in_specs = (
        P("seq", None, ("mp", "role")),
        P(("mp", "role"), None),
        P(),
        P(),
        P(),
        P(),
        P(),
        P(None, None, ("mp", "role")),
        P(("mp", "role"), None),
    )
    out_specs = P(("seq", "mp", "role"), None)
    return jax.shard_map(
        on_device, mesh=mesh, in_specs=in_specs, out_specs=out_specs, check_vma=False
    )
```

```python
import functools

import jax
import jax.numpy as jnp
from jax import lax
from jax.experimental import pallas as pl
from jax.experimental.pallas import tpu as pltpu
from jax.sharding import PartitionSpec as P

HS = 128
MOSTB = 4
REACH = MOSTB - 1
GROUP = ("mp", "role")
SCATTERED = ("role", "mp", "seq")
LANES = 128
STEP_ROWS = 256
DEPTH = 1024
AHEAD = 4
STRIP = 512
MIB = 1024 * 1024
VMEM = pl.BlockSpec(memory_space=pltpu.VMEM)
SMEM = pl.BlockSpec(memory_space=pltpu.SMEM)
HBM = pl.BlockSpec(memory_space=pltpu.HBM)


def dot(a, b):
    return jnp.dot(a, b, preferred_element_type=jnp.float32)


def latent_kernel(
    frame_dev,
    hidden_hbm,
    weight_hbm,
    out_hbm,
    hidden_ref,
    weight_ref,
    padded_ref,
    out_ref,
    in_sems,
    out_sems,
):
    slots, frames, depth = hidden_ref.shape
    everyone, _, window, channels = out_ref.shape
    seqs = frames // frame_dev
    arrivals = [pltpu.make_async_copy(hidden_hbm, hidden_ref, in_sems.at[0])]
    for index, at in enumerate(range(0, depth, LANES)):
        piece = pl.ds(at, LANES)
        arrivals.append(
            pltpu.make_async_copy(
                weight_hbm.at[piece], weight_ref.at[piece], in_sems.at[index + 1]
            )
        )
    for copy in arrivals:
        copy.start()
    padded_ref[...] = jnp.zeros_like(padded_ref)
    for copy in arrivals:
        copy.wait()
    for slot in range(slots):
        padded_ref[slot, REACH : REACH + frames] = dot(hidden_ref[slot], weight_ref[...])
    pieces = [
        padded_ref[:, to * frame_dev : to * frame_dev + window].astype(out_ref.dtype)
        for to in range(seqs)
    ]
    leaving = []
    for index, first in enumerate(range(0, everyone, seqs)):
        for to in range(seqs):
            out_ref[first + to] = pieces[to]
        part = pl.ds(first, seqs)
        leaving.append(
            pltpu.make_async_copy(out_ref.at[part], out_hbm.at[part], out_sems.at[index])
        )
        leaving[-1].start()
    for copy in leaving:
        copy.wait()


def weights_kernel(
    frame_dev,
    window,
    order_ref,
    block_ref,
    embed_ref,
    pos_ref,
    gain_ref,
    weight_hbm,
    out_weight_hbm,
    scaled_ref,
    offset_ref,
    gram_ref,
    cross_ref,
    level_ref,
    natural_cross_ref,
    natural_level_ref,
    pos_mine_ref,
    select_ref,
    select_mine_ref,
    bias_ref,
    first_ref,
    natural_ref,
    pos_all_ref,
    weight_ref,
    sems,
    first_sem,
):
    channels, model = embed_ref.shape
    patches = pos_ref.shape[0]
    frames = block_ref.shape[0]
    own_rows, rows = bias_ref.shape
    share = select_mine_ref.shape[0]
    device = lax.axis_index("seq")
    member = lax.axis_index(GROUP)

    deep = min(model, DEPTH)
    parts = [(index, at) for index in range(3) for at in range(0, model, deep)]

    def arrival(part):
        index, at = parts[part]
        place = (index, pl.ds(at, deep))
        return pltpu.make_async_copy(weight_hbm.at[place], weight_ref.at[place], sems.at[part])

    first = pltpu.make_async_copy(
        out_weight_hbm.at[pl.ds(0, first_ref.shape[0])], first_ref, first_sem
    )
    for part in range(AHEAD):
        arrival(part).start()

    pos = pos_ref[...].astype(jnp.float32)
    pos_all_ref[...] = pos

    column = lax.broadcasted_iota(jnp.int32, (1, rows), 1)
    column_slot, column_frame = column // window, column % window

    def patch_at(slot, found):
        return jnp.where(column_slot == slot, order_ref[slot], found)

    column_patch = jnp.zeros((1, rows), jnp.int32)
    if patches <= 16:
        for slot in range(patches):
            column_patch = patch_at(slot, column_patch)
    else:
        column_patch = lax.fori_loop(0, patches, patch_at, column_patch)

    def select(count, first):
        row = lax.broadcasted_iota(jnp.int32, (count, rows), 0) + first
        hit = jnp.logical_and(
            column_patch == row % patches, column_frame == row // patches + REACH
        )
        return jnp.where(hit, 1.0, 0.0).astype(jnp.bfloat16)

    select_ref[...] = select(own_rows, 0)
    select_mine_ref[...] = select(share, member * share)
    for frame in range(frame_dev * patches // share):
        row = frame * share

        @pl.when(member == frame)
        def _():
            for at in range(share):
                mine = (row + at) % patches
                pos_mine_ref[at : at + 1, :] = pos_all_ref[mine : mine + 1, :]

    def block_of(frame):
        inside = jnp.logical_and(frame >= 0, frame < frames)
        return jnp.where(inside, block_ref[jnp.clip(frame, 0, frames - 1)], -1)

    column_block = jnp.full((1, rows), -1, jnp.int32)
    for frame in range(window):
        found = block_of(device * frame_dev - REACH + frame)
        column_block = jnp.where(column_frame == frame, found, column_block)
    row_frame = lax.broadcasted_iota(jnp.int32, (own_rows, rows), 0) // patches
    row_block = jnp.full((own_rows, rows), -2, jnp.int32)
    for frame in range(frame_dev):
        row_block = jnp.where(row_frame == frame, block_of(device * frame_dev + frame), row_block)
    bias_ref[...] = jnp.where(row_block == column_block, 0.0, -1e30)

    gain = jnp.concatenate(
        [gain_ref[at : at + 1, :].astype(jnp.float32) for at in range(model // LANES)], axis=1
    )
    left = jnp.concatenate([embed_ref[...].astype(jnp.float32) * gain, pos * gain], axis=0)
    left = left.astype(jnp.bfloat16)
    def keep(ref, scaled):
        high = scaled.astype(jnp.bfloat16)
        ref[:channels] = high
        ref[channels:] = (scaled - high.astype(jnp.float32)).astype(jnp.bfloat16)

    plain = jnp.concatenate([embed_ref[...], pos_ref[...]], axis=0)
    both = lax.dot_general(
        plain, embed_ref[...], (((1,), (1,)), ((), ())), preferred_element_type=jnp.float32
    )
    keep(gram_ref, both[:channels])
    natural_cross_ref[...] = 2.0 * both[channels:]
    level = jnp.sum(pos * pos, axis=-1, keepdims=True) / channels
    natural_level_ref[...] = jnp.broadcast_to(level, (patches, channels))

    for part, (index, at) in enumerate(parts):
        arrival(part).wait()
        if part + AHEAD < len(parts):
            arrival(part + AHEAD).start()
        if part + AHEAD == len(parts) - 1:
            first.start()
        here = slice(at, at + deep)
        product = dot(left[:, here], weight_ref[index, here])
        both = product if at == 0 else both + product
        if at + deep == model:
            keep(scaled_ref.at[index], both[:channels])
            natural_ref[index] = both[channels:]

    offset_ref[0] = natural_ref[0]

    def place(slot):
        to, at = pl.ds(slot, 1), pl.ds(order_ref[slot], 1)
        cross_ref[to, :] = natural_cross_ref[at, :]
        level_ref[to, :] = natural_level_ref[at, :]
        for index in range(1, 3):
            offset_ref[index, to, :] = natural_ref[index, at, :]

    if patches <= 16:
        for slot in range(patches):
            place(slot)
    else:
        pl.loop(0, patches)(place)
    first.wait()


def attend_kernel(
    partial_ref,
    embed_ref,
    scaled_ref,
    offset_ref,
    gram_ref,
    cross_ref,
    level_ref,
    natural_cross_ref,
    natural_level_ref,
    pos_mine_ref,
    select_ref,
    select_mine_ref,
    bias_ref,
    first_ref,
    out_weight_hbm,
    mixed_ref,
    mine_ref,
    second_ref,
    sem,
):
    half = first_ref.shape[0]
    arrival = pltpu.make_async_copy(out_weight_hbm.at[pl.ds(half, half)], second_ref, sem)
    arrival.start()
    everyone, slots, window, channels = partial_ref.shape
    group, share, model = mixed_ref.shape
    seqs = everyone // group
    patches = seqs * slots
    rows = patches * window
    cols = out_weight_hbm.shape[0]

    total = partial_ref[:seqs].astype(jnp.float32)
    for other in range(1, group):
        total = total + partial_ref[other * seqs : (other + 1) * seqs].astype(jnp.float32)
    latents = total.reshape(rows, channels).astype(jnp.bfloat16)
    own = dot(select_ref[...], latents).astype(jnp.bfloat16)

    def apply(part, table):
        return dot(jnp.concatenate([part, part], axis=1), table)

    def by_row(table):
        wide = jnp.broadcast_to(table[:, None], (patches, window, table.shape[1]))
        return wide.reshape(rows, table.shape[1])

    def by_patch(table):
        return jnp.concatenate([table] * (group * share // patches), axis=0)

    def scale_of(part, cross, level):
        slope = apply(part, gram_ref[...]) + cross
        squares = slope * part.astype(jnp.float32) + level
        mean = jnp.maximum(jnp.sum(squares, axis=-1, keepdims=True), 0.0) / model
        return lax.rsqrt(mean + 1e-06)

    scale = scale_of(latents, by_row(cross_ref[...]), by_row(level_ref[...]))
    own_scale = scale_of(own, by_patch(natural_cross_ref[...]), by_patch(natural_level_ref[...]))
    own_scale = own_scale * (HS**-0.5)

    def project(index):
        flat = apply(latents, scaled_ref[index]) + by_row(offset_ref[index])
        return (flat * scale).astype(jnp.bfloat16)

    query = (apply(own, scaled_ref[0]) + by_patch(offset_ref[0])).astype(jnp.bfloat16)
    key, value = project(1), project(2)
    bias = bias_ref[...]
    heads = []
    for head in range(cols // HS):
        at = slice(head * HS, (head + 1) * HS)
        scores = lax.dot_general(
            query[:, at], key[:, at], (((1,), (1,)), ((), ())), preferred_element_type=jnp.float32
        )
        scores = scores * own_scale + bias
        expo = jnp.exp(scores - jnp.max(scores, axis=-1, keepdims=True))
        probs = (expo / jnp.sum(expo, axis=-1, keepdims=True)).astype(jnp.bfloat16)
        heads.append(dot(probs, value[:, at]).astype(jnp.bfloat16))
    mine = dot(select_mine_ref[...], latents).astype(jnp.bfloat16)
    mine_ref[...] = dot(mine, embed_ref[...]) + pos_mine_ref[...]
    heads = jnp.concatenate(heads, axis=1)
    arrival.wait()
    for at in range(0, model, STRIP):
        here = slice(at, at + STRIP)
        mixed = dot(heads[:, :half], first_ref[:, here]) + dot(heads[:, half:], second_ref[:, here])
        mixed = mixed.astype(jnp.bfloat16)
        for other in range(group):
            mixed_ref[other, :, here] = mixed[other * share : (other + 1) * share]


def sum_kernel(mine_ref, mixed_ref, out_ref):
    total = mine_ref[...]
    for member in range(mixed_ref.shape[0]):
        total = total + mixed_ref[member].astype(jnp.float32)
    out_ref[...] = total.astype(jnp.bfloat16)


def on_device(
    gen_hidden,
    gen_out_weight,
    patch_order,
    frame_block,
    embed_weight,
    pos_table,
    norm_gain,
    qkv_weight,
    out_weight,
):
    slots, frames, depth = gen_hidden.shape
    channels, model = embed_weight.shape
    cols = qkv_weight.shape[2]
    out_weight = pltpu.with_memory_space_constraint(out_weight, pltpu.HBM)
    seqs = lax.axis_size("seq")
    group = lax.axis_size(GROUP)
    patches = seqs * slots
    frame_dev = frames // seqs
    window = frame_dev + 2 * REACH
    rows = window * patches
    own_rows = frame_dev * patches
    share = own_rows // group
    f32, bf16 = jnp.float32, jnp.bfloat16
    array = jax.ShapeDtypeStruct
    grant = (16 if rows <= STEP_ROWS else 40) * MIB

    windows = pl.pallas_call(
        functools.partial(latent_kernel, frame_dev),
        out_shape=array((group * seqs, slots, window, channels), bf16),
        in_specs=[HBM] * 2,
        out_specs=HBM,
        scratch_shapes=[
            pltpu.VMEM((slots, frames, depth), bf16),
            pltpu.VMEM((depth, channels), bf16),
            pltpu.VMEM((slots, frames + 2 * REACH, channels), f32),
            pltpu.VMEM((group * seqs, slots, window, channels), bf16),
            pltpu.SemaphoreType.DMA((1 + depth // LANES,)),
            pltpu.SemaphoreType.DMA((group,)),
        ],
        compiler_params=pltpu.CompilerParams(vmem_limit_bytes=12 * MIB),
        cost_estimate=pl.CostEstimate(
            flops=20_000_000_000, bytes_accessed=40_000_000, transcendentals=0
        ),
        name="partial_latents",
    )(
        pltpu.with_memory_space_constraint(gen_hidden, pltpu.HBM),
        pltpu.with_memory_space_constraint(gen_out_weight, pltpu.HBM),
    )
    moved = lax.all_to_all(
        windows,
        SCATTERED,
        split_axis=0,
        concat_axis=0,
        tiled=True,
    )

    products = pl.pallas_call(
        functools.partial(weights_kernel, frame_dev, window),
        out_shape=(
            array((3, 2 * channels, cols), bf16),
            array((3, patches, cols), f32),
            array((2 * channels, channels), bf16),
            array((patches, channels), f32),
            array((patches, channels), f32),
            array((patches, channels), f32),
            array((patches, channels), f32),
            array((share, model), f32),
            array((own_rows, rows), bf16),
            array((share, rows), bf16),
            array((own_rows, rows), f32),
            array((cols // 2, model), bf16),
        ),
        in_specs=[SMEM] * 2 + [VMEM] * 3 + [HBM] * 2,
        out_specs=(VMEM,) * 12,
        scratch_shapes=[
            pltpu.VMEM((3, patches, cols), f32),
            pltpu.VMEM((patches, model), f32),
            pltpu.VMEM((3, model, cols), bf16),
            pltpu.SemaphoreType.DMA((3 * (model // min(model, DEPTH)),)),
            pltpu.SemaphoreType.DMA(()),
        ],
        compiler_params=pltpu.CompilerParams(vmem_limit_bytes=24 * MIB),
        cost_estimate=pl.CostEstimate(
            flops=2 * (channels + patches) * model * 3 * cols,
            bytes_accessed=2 * model * 3 * cols,
            transcendentals=0,
        ),
        name="weight_products",
    )(
        patch_order,
        frame_block,
        embed_weight,
        pos_table,
        norm_gain.reshape(model // LANES, LANES),
        pltpu.with_memory_space_constraint(jnp.transpose(qkv_weight, (1, 0, 2)), pltpu.HBM),
        out_weight,
    )

    mixed, mine = pl.pallas_call(
        attend_kernel,
        out_shape=(array((group, share, model), bf16), array((share, model), f32)),
        in_specs=[VMEM] * 14 + [HBM],
        out_specs=(VMEM, VMEM),
        scratch_shapes=[
            pltpu.VMEM((cols - cols // 2, model), bf16),
            pltpu.SemaphoreType.DMA(()),
        ],
        compiler_params=pltpu.CompilerParams(vmem_limit_bytes=grant),
        name="attend",
    )(
        moved,
        embed_weight,
        *products,
        out_weight,
    )
    mixed = lax.all_to_all(mixed, GROUP, split_axis=0, concat_axis=0, tiled=True)
    return pl.pallas_call(
        sum_kernel,
        out_shape=array((share, model), bf16),
        in_specs=[VMEM] * 2,
        out_specs=VMEM,
        compiler_params=pltpu.CompilerParams(vmem_limit_bytes=8 * MIB),
        name="final_sum",
    )(mine, mixed)


def solution(mesh):
    in_specs = (
        P("seq", None, ("mp", "role")),
        P(("mp", "role"), None),
        P(),
        P(),
        P(),
        P(),
        P(),
        P(None, None, ("mp", "role")),
        P(("mp", "role"), None),
    )
    out_specs = P(("seq", "mp", "role"), None)
    return jax.shard_map(
        on_device, mesh=mesh, in_specs=in_specs, out_specs=out_specs, check_vma=False
    )
```

```python
import functools

import jax
import jax.numpy as jnp
from jax import lax
from jax.experimental import pallas as pl
from jax.experimental.pallas import tpu as pltpu
from jax.sharding import PartitionSpec as P

HS = 128
MOSTB = 4
REACH = MOSTB - 1
GROUP = ("mp", "role")
SCATTERED = ("mp", "seq")
LANES = 128
STEP_ROWS = 256
DEPTH = 1024
AHEAD = 4
STRIP = 512
MIB = 1024 * 1024
VMEM = pl.BlockSpec(memory_space=pltpu.VMEM)
SMEM = pl.BlockSpec(memory_space=pltpu.SMEM)
HBM = pl.BlockSpec(memory_space=pltpu.HBM)


def dot(a, b):
    return jnp.dot(a, b, preferred_element_type=jnp.float32)


def latent_kernel(
    frame_dev,
    hidden_hbm,
    weight_hbm,
    out_hbm,
    hidden_ref,
    weight_ref,
    padded_ref,
    out_ref,
    in_sems,
    out_sems,
):
    slots, frames, depth = hidden_ref.shape
    everyone, _, window, channels = out_ref.shape
    seqs = frames // frame_dev
    arrivals = [pltpu.make_async_copy(hidden_hbm, hidden_ref, in_sems.at[0])]
    for index, at in enumerate(range(0, depth, LANES)):
        piece = pl.ds(at, LANES)
        arrivals.append(
            pltpu.make_async_copy(
                weight_hbm.at[piece], weight_ref.at[piece], in_sems.at[index + 1]
            )
        )
    for copy in arrivals:
        copy.start()
    padded_ref[...] = jnp.zeros_like(padded_ref)
    for copy in arrivals:
        copy.wait()
    for slot in range(slots):
        padded_ref[slot, REACH : REACH + frames] = dot(hidden_ref[slot], weight_ref[...])
    pieces = [
        padded_ref[:, to * frame_dev : to * frame_dev + window].astype(out_ref.dtype)
        for to in range(seqs)
    ]
    leaving = []
    for index, first in enumerate(range(0, everyone, seqs)):
        for to in range(seqs):
            out_ref[first + to] = pieces[to]
        part = pl.ds(first, seqs)
        leaving.append(
            pltpu.make_async_copy(out_ref.at[part], out_hbm.at[part], out_sems.at[index])
        )
        leaving[-1].start()
    for copy in leaving:
        copy.wait()


def weights_kernel(
    frame_dev,
    window,
    order_ref,
    block_ref,
    embed_ref,
    pos_ref,
    gain_ref,
    weight_hbm,
    out_weight_hbm,
    scaled_ref,
    offset_ref,
    gram_ref,
    cross_ref,
    level_ref,
    natural_cross_ref,
    natural_level_ref,
    pos_mine_ref,
    select_ref,
    select_mine_ref,
    bias_ref,
    first_ref,
    natural_ref,
    pos_all_ref,
    weight_ref,
    sems,
    first_sem,
):
    channels, model = embed_ref.shape
    patches = pos_ref.shape[0]
    frames = block_ref.shape[0]
    own_rows, rows = bias_ref.shape
    share = select_mine_ref.shape[0]
    device = lax.axis_index("seq")
    member = lax.axis_index(GROUP)

    deep = min(model, DEPTH)
    parts = [(index, at) for index in range(3) for at in range(0, model, deep)]

    def arrival(part):
        index, at = parts[part]
        place = (index, pl.ds(at, deep))
        return pltpu.make_async_copy(weight_hbm.at[place], weight_ref.at[place], sems.at[part])

    first = pltpu.make_async_copy(
        out_weight_hbm.at[pl.ds(0, first_ref.shape[0])], first_ref, first_sem
    )
    for part in range(AHEAD):
        arrival(part).start()

    pos = pos_ref[...].astype(jnp.float32)
    pos_all_ref[...] = pos

    column = lax.broadcasted_iota(jnp.int32, (1, rows), 1)
    column_slot, column_frame = column // window, column % window

    def patch_at(slot, found):
        return jnp.where(column_slot == slot, order_ref[slot], found)

    column_patch = jnp.zeros((1, rows), jnp.int32)
    if patches <= 16:
        for slot in range(patches):
            column_patch = patch_at(slot, column_patch)
    else:
        column_patch = lax.fori_loop(0, patches, patch_at, column_patch)

    def select(count, first):
        row = lax.broadcasted_iota(jnp.int32, (count, rows), 0) + first
        hit = jnp.logical_and(
            column_patch == row % patches, column_frame == row // patches + REACH
        )
        return jnp.where(hit, 1.0, 0.0).astype(jnp.bfloat16)

    select_ref[...] = select(own_rows, 0)
    select_mine_ref[...] = select(share, member * share)
    for frame in range(frame_dev * patches // share):
        row = frame * share

        @pl.when(member == frame)
        def _():
            for at in range(share):
                mine = (row + at) % patches
                pos_mine_ref[at : at + 1, :] = pos_all_ref[mine : mine + 1, :]

    def block_of(frame):
        inside = jnp.logical_and(frame >= 0, frame < frames)
        return jnp.where(inside, block_ref[jnp.clip(frame, 0, frames - 1)], -1)

    column_block = jnp.full((1, rows), -1, jnp.int32)
    for frame in range(window):
        found = block_of(device * frame_dev - REACH + frame)
        column_block = jnp.where(column_frame == frame, found, column_block)
    row_frame = lax.broadcasted_iota(jnp.int32, (own_rows, rows), 0) // patches
    row_block = jnp.full((own_rows, rows), -2, jnp.int32)
    for frame in range(frame_dev):
        row_block = jnp.where(row_frame == frame, block_of(device * frame_dev + frame), row_block)
    bias_ref[...] = jnp.where(row_block == column_block, 0.0, -1e30)

    gain = jnp.concatenate(
        [gain_ref[at : at + 1, :].astype(jnp.float32) for at in range(model // LANES)], axis=1
    )
    left = jnp.concatenate([embed_ref[...].astype(jnp.float32) * gain, pos * gain], axis=0)
    left = left.astype(jnp.bfloat16)
    def keep(ref, scaled):
        high = scaled.astype(jnp.bfloat16)
        ref[:channels] = high
        ref[channels:] = (scaled - high.astype(jnp.float32)).astype(jnp.bfloat16)

    plain = jnp.concatenate([embed_ref[...], pos_ref[...]], axis=0)
    both = lax.dot_general(
        plain, embed_ref[...], (((1,), (1,)), ((), ())), preferred_element_type=jnp.float32
    )
    keep(gram_ref, both[:channels])
    natural_cross_ref[...] = 2.0 * both[channels:]
    level = jnp.sum(pos * pos, axis=-1, keepdims=True) / channels
    natural_level_ref[...] = jnp.broadcast_to(level, (patches, channels))

    for part, (index, at) in enumerate(parts):
        arrival(part).wait()
        if part + AHEAD < len(parts):
            arrival(part + AHEAD).start()
        if part + AHEAD == len(parts) - 1:
            first.start()
        here = slice(at, at + deep)
        product = dot(left[:, here], weight_ref[index, here])
        both = product if at == 0 else both + product
        if at + deep == model:
            keep(scaled_ref.at[index], both[:channels])
            natural_ref[index] = both[channels:]

    offset_ref[0] = natural_ref[0]

    def place(slot):
        to, at = pl.ds(slot, 1), pl.ds(order_ref[slot], 1)
        cross_ref[to, :] = natural_cross_ref[at, :]
        level_ref[to, :] = natural_level_ref[at, :]
        for index in range(1, 3):
            offset_ref[index, to, :] = natural_ref[index, at, :]

    if patches <= 16:
        for slot in range(patches):
            place(slot)
    else:
        pl.loop(0, patches)(place)
    first.wait()


def attend_kernel(
    roles,
    *refs,
):
    attend(refs[:roles], *refs[roles:])


def attend(
    partial_refs,
    embed_ref,
    scaled_ref,
    offset_ref,
    gram_ref,
    cross_ref,
    level_ref,
    natural_cross_ref,
    natural_level_ref,
    pos_mine_ref,
    select_ref,
    select_mine_ref,
    bias_ref,
    first_ref,
    out_weight_hbm,
    mixed_ref,
    mine_ref,
    second_ref,
    sem,
):
    half = first_ref.shape[0]
    arrival = pltpu.make_async_copy(out_weight_hbm.at[pl.ds(half, half)], second_ref, sem)
    arrival.start()
    senders, slots, window, channels = partial_refs[0].shape
    group, share, model = mixed_ref.shape
    seqs = senders * len(partial_refs) // group
    patches = seqs * slots
    rows = patches * window
    cols = out_weight_hbm.shape[0]

    totals = []
    for partial_ref in partial_refs:
        total = partial_ref[:seqs].astype(jnp.float32)
        for first in range(seqs, senders, seqs):
            total = total + partial_ref[first : first + seqs].astype(jnp.float32)
        totals.append(total)
    total = functools.reduce(jnp.add, totals)
    latents = total.reshape(rows, channels).astype(jnp.bfloat16)
    own = dot(select_ref[...], latents).astype(jnp.bfloat16)

    def apply(part, table):
        return dot(jnp.concatenate([part, part], axis=1), table)

    def by_row(table):
        wide = jnp.broadcast_to(table[:, None], (patches, window, table.shape[1]))
        return wide.reshape(rows, table.shape[1])

    def by_patch(table):
        return jnp.concatenate([table] * (group * share // patches), axis=0)

    def scale_of(part, cross, level):
        slope = apply(part, gram_ref[...]) + cross
        squares = slope * part.astype(jnp.float32) + level
        mean = jnp.maximum(jnp.sum(squares, axis=-1, keepdims=True), 0.0) / model
        return lax.rsqrt(mean + 1e-06)

    scale = scale_of(latents, by_row(cross_ref[...]), by_row(level_ref[...]))
    own_scale = scale_of(own, by_patch(natural_cross_ref[...]), by_patch(natural_level_ref[...]))
    own_scale = own_scale * (HS**-0.5)

    def project(index):
        flat = apply(latents, scaled_ref[index]) + by_row(offset_ref[index])
        return (flat * scale).astype(jnp.bfloat16)

    query = (apply(own, scaled_ref[0]) + by_patch(offset_ref[0])).astype(jnp.bfloat16)
    key, value = project(1), project(2)
    bias = bias_ref[...]
    heads = []
    for head in range(cols // HS):
        at = slice(head * HS, (head + 1) * HS)
        scores = lax.dot_general(
            query[:, at], key[:, at], (((1,), (1,)), ((), ())), preferred_element_type=jnp.float32
        )
        scores = scores * own_scale + bias
        expo = jnp.exp(scores - jnp.max(scores, axis=-1, keepdims=True))
        probs = (expo / jnp.sum(expo, axis=-1, keepdims=True)).astype(jnp.bfloat16)
        heads.append(dot(probs, value[:, at]).astype(jnp.bfloat16))
    mine = dot(select_mine_ref[...], latents).astype(jnp.bfloat16)
    mine_ref[...] = dot(mine, embed_ref[...]) + pos_mine_ref[...]
    heads = jnp.concatenate(heads, axis=1)
    arrival.wait()
    for at in range(0, model, STRIP):
        here = slice(at, at + STRIP)
        mixed = dot(heads[:, :half], first_ref[:, here]) + dot(heads[:, half:], second_ref[:, here])
        mixed = mixed.astype(jnp.bfloat16)
        for other in range(group):
            mixed_ref[other, :, here] = mixed[other * share : (other + 1) * share]


def sum_kernel(mine_ref, mixed_ref, out_ref):
    total = mine_ref[...]
    for member in range(mixed_ref.shape[0]):
        total = total + mixed_ref[member].astype(jnp.float32)
    out_ref[...] = total.astype(jnp.bfloat16)


def on_device(
    gen_hidden,
    gen_out_weight,
    patch_order,
    frame_block,
    embed_weight,
    pos_table,
    norm_gain,
    qkv_weight,
    out_weight,
):
    slots, frames, depth = gen_hidden.shape
    channels, model = embed_weight.shape
    cols = qkv_weight.shape[2]
    out_weight = pltpu.with_memory_space_constraint(out_weight, pltpu.HBM)
    seqs = lax.axis_size("seq")
    group = lax.axis_size(GROUP)
    roles = lax.axis_size("role")
    senders = lax.axis_size(SCATTERED)
    patches = seqs * slots
    frame_dev = frames // seqs
    window = frame_dev + 2 * REACH
    rows = window * patches
    own_rows = frame_dev * patches
    share = own_rows // group
    f32, bf16 = jnp.float32, jnp.bfloat16
    array = jax.ShapeDtypeStruct
    grant = (16 if rows <= STEP_ROWS else 40) * MIB

    windows = pl.pallas_call(
        functools.partial(latent_kernel, frame_dev),
        out_shape=array((senders, slots, window, channels), bf16),
        in_specs=[HBM] * 2,
        out_specs=HBM,
        scratch_shapes=[
            pltpu.VMEM((slots, frames, depth), bf16),
            pltpu.VMEM((depth, channels), bf16),
            pltpu.VMEM((slots, frames + 2 * REACH, channels), f32),
            pltpu.VMEM((senders, slots, window, channels), bf16),
            pltpu.SemaphoreType.DMA((1 + depth // LANES,)),
            pltpu.SemaphoreType.DMA((senders // seqs,)),
        ],
        compiler_params=pltpu.CompilerParams(vmem_limit_bytes=12 * MIB),
        cost_estimate=pl.CostEstimate(
            flops=20_000_000_000, bytes_accessed=40_000_000, transcendentals=0
        ),
        name="partial_latents",
    )(
        pltpu.with_memory_space_constraint(gen_hidden, pltpu.HBM),
        pltpu.with_memory_space_constraint(gen_out_weight, pltpu.HBM),
    )
    moved = lax.all_to_all(
        windows,
        SCATTERED,
        split_axis=0,
        concat_axis=0,
        tiled=True,
    )
    others = [
        lax.ppermute(moved, "role", [(i, (i + step) % roles) for i in range(roles)])
        for step in range(1, roles)
    ]

    products = pl.pallas_call(
        functools.partial(weights_kernel, frame_dev, window),
        out_shape=(
            array((3, 2 * channels, cols), bf16),
            array((3, patches, cols), f32),
            array((2 * channels, channels), bf16),
            array((patches, channels), f32),
            array((patches, channels), f32),
            array((patches, channels), f32),
            array((patches, channels), f32),
            array((share, model), f32),
            array((own_rows, rows), bf16),
            array((share, rows), bf16),
            array((own_rows, rows), f32),
            array((cols // 2, model), bf16),
        ),
        in_specs=[SMEM] * 2 + [VMEM] * 3 + [HBM] * 2,
        out_specs=(VMEM,) * 12,
        scratch_shapes=[
            pltpu.VMEM((3, patches, cols), f32),
            pltpu.VMEM((patches, model), f32),
            pltpu.VMEM((3, model, cols), bf16),
            pltpu.SemaphoreType.DMA((3 * (model // min(model, DEPTH)),)),
            pltpu.SemaphoreType.DMA(()),
        ],
        compiler_params=pltpu.CompilerParams(vmem_limit_bytes=24 * MIB),
        cost_estimate=pl.CostEstimate(
            flops=2 * (channels + patches) * model * 3 * cols,
            bytes_accessed=2 * model * 3 * cols,
            transcendentals=0,
        ),
        name="weight_products",
    )(
        patch_order,
        frame_block,
        embed_weight,
        pos_table,
        norm_gain.reshape(model // LANES, LANES),
        pltpu.with_memory_space_constraint(jnp.transpose(qkv_weight, (1, 0, 2)), pltpu.HBM),
        out_weight,
    )

    mixed, mine = pl.pallas_call(
        functools.partial(attend_kernel, roles),
        out_shape=(array((group, share, model), bf16), array((share, model), f32)),
        in_specs=[VMEM] * (13 + roles) + [HBM],
        out_specs=(VMEM, VMEM),
        scratch_shapes=[
            pltpu.VMEM((cols - cols // 2, model), bf16),
            pltpu.SemaphoreType.DMA(()),
        ],
        compiler_params=pltpu.CompilerParams(vmem_limit_bytes=grant),
        name="attend",
    )(
        moved,
        *others,
        embed_weight,
        *products,
        out_weight,
    )
    mixed = lax.all_to_all(mixed, GROUP, split_axis=0, concat_axis=0, tiled=True)
    return pl.pallas_call(
        sum_kernel,
        out_shape=array((share, model), bf16),
        in_specs=[VMEM] * 2,
        out_specs=VMEM,
        compiler_params=pltpu.CompilerParams(vmem_limit_bytes=8 * MIB),
        name="final_sum",
    )(mine, mixed)


def solution(mesh):
    in_specs = (
        P("seq", None, ("mp", "role")),
        P(("mp", "role"), None),
        P(),
        P(),
        P(),
        P(),
        P(),
        P(None, None, ("mp", "role")),
        P(("mp", "role"), None),
    )
    out_specs = P(("seq", "mp", "role"), None)
    return jax.shard_map(
        on_device, mesh=mesh, in_specs=in_specs, out_specs=out_specs, check_vma=False
    )
```

```python
import functools

import jax
import jax.numpy as jnp
from jax import lax
from jax.experimental import pallas as pl
from jax.experimental.pallas import tpu as pltpu
from jax.sharding import PartitionSpec as P

HS = 128
MOSTB = 4
REACH = MOSTB - 1
GROUP = ("mp", "role")
SCATTERED = ("role", "mp", "seq")
LANES = 128
STEP_ROWS = 256
DEPTH = 1024
AHEAD = 4
STRIP = 512
MIB = 1024 * 1024
VMEM = pl.BlockSpec(memory_space=pltpu.VMEM)
SMEM = pl.BlockSpec(memory_space=pltpu.SMEM)
HBM = pl.BlockSpec(memory_space=pltpu.HBM)


def dot(a, b):
    return jnp.dot(a, b, preferred_element_type=jnp.float32)


def latent_kernel(
    frame_dev,
    hidden_hbm,
    weight_hbm,
    out_hbm,
    hidden_ref,
    weight_ref,
    padded_ref,
    out_ref,
    in_sems,
    out_sems,
):
    slots, frames, depth = hidden_ref.shape
    everyone, _, window, channels = out_ref.shape
    seqs = frames // frame_dev
    arrivals = [pltpu.make_async_copy(hidden_hbm, hidden_ref, in_sems.at[0])]
    for index, at in enumerate(range(0, depth, LANES)):
        piece = pl.ds(at, LANES)
        arrivals.append(
            pltpu.make_async_copy(
                weight_hbm.at[piece], weight_ref.at[piece], in_sems.at[index + 1]
            )
        )
    for copy in arrivals:
        copy.start()
    padded_ref[...] = jnp.zeros_like(padded_ref)
    for copy in arrivals:
        copy.wait()
    for slot in range(slots):
        padded_ref[slot, REACH : REACH + frames] = dot(hidden_ref[slot], weight_ref[...])
    pieces = [
        padded_ref[:, to * frame_dev : to * frame_dev + window].astype(out_ref.dtype)
        for to in range(seqs)
    ]
    leaving = []
    for index, first in enumerate(range(0, everyone, seqs)):
        for to in range(seqs):
            out_ref[first + to] = pieces[to]
        part = pl.ds(first, seqs)
        leaving.append(
            pltpu.make_async_copy(out_ref.at[part], out_hbm.at[part], out_sems.at[index])
        )
        leaving[-1].start()
    for copy in leaving:
        copy.wait()


def weights_kernel(
    frame_dev,
    window,
    order_ref,
    block_ref,
    embed_ref,
    pos_ref,
    gain_ref,
    weight_hbm,
    out_weight_hbm,
    scaled_ref,
    offset_ref,
    gram_ref,
    cross_ref,
    level_ref,
    natural_cross_ref,
    natural_level_ref,
    pos_mine_ref,
    select_ref,
    select_mine_ref,
    bias_ref,
    first_ref,
    natural_ref,
    pos_all_ref,
    weight_ref,
    sems,
    first_sem,
):
    channels, model = embed_ref.shape
    patches = pos_ref.shape[0]
    frames = block_ref.shape[0]
    own_rows, rows = bias_ref.shape
    share = select_mine_ref.shape[0]
    device = lax.axis_index("seq")
    member = lax.axis_index(GROUP)

    deep = min(model, DEPTH)
    parts = [(index, at) for index in range(3) for at in range(0, model, deep)]

    def arrival(part):
        index, at = parts[part]
        place = (index, pl.ds(at, deep))
        return pltpu.make_async_copy(weight_hbm.at[place], weight_ref.at[place], sems.at[part])

    first = pltpu.make_async_copy(
        out_weight_hbm.at[pl.ds(0, first_ref.shape[0])], first_ref, first_sem
    )
    for part in range(AHEAD):
        arrival(part).start()

    pos = pos_ref[...].astype(jnp.float32)
    pos_all_ref[...] = pos

    column = lax.broadcasted_iota(jnp.int32, (1, rows), 1)
    column_slot, column_frame = column // window, column % window

    def patch_at(slot, found):
        return jnp.where(column_slot == slot, order_ref[slot], found)

    column_patch = jnp.zeros((1, rows), jnp.int32)
    if patches <= 16:
        for slot in range(patches):
            column_patch = patch_at(slot, column_patch)
    else:
        column_patch = lax.fori_loop(0, patches, patch_at, column_patch)

    def select(count, first):
        row = lax.broadcasted_iota(jnp.int32, (count, rows), 0) + first
        hit = jnp.logical_and(
            column_patch == row % patches, column_frame == row // patches + REACH
        )
        return jnp.where(hit, 1.0, 0.0).astype(jnp.bfloat16)

    select_ref[...] = select(own_rows, 0)
    select_mine_ref[...] = select(share, member * share)
    for frame in range(frame_dev * patches // share):
        row = frame * share

        @pl.when(member == frame)
        def _():
            for at in range(share):
                mine = (row + at) % patches
                pos_mine_ref[at : at + 1, :] = pos_all_ref[mine : mine + 1, :]

    def block_of(frame):
        inside = jnp.logical_and(frame >= 0, frame < frames)
        return jnp.where(inside, block_ref[jnp.clip(frame, 0, frames - 1)], -1)

    column_block = jnp.full((1, rows), -1, jnp.int32)
    for frame in range(window):
        found = block_of(device * frame_dev - REACH + frame)
        column_block = jnp.where(column_frame == frame, found, column_block)
    row_frame = lax.broadcasted_iota(jnp.int32, (own_rows, rows), 0) // patches
    row_block = jnp.full((own_rows, rows), -2, jnp.int32)
    for frame in range(frame_dev):
        row_block = jnp.where(row_frame == frame, block_of(device * frame_dev + frame), row_block)
    bias_ref[...] = jnp.where(row_block == column_block, 0.0, -1e30)

    gain = jnp.concatenate(
        [gain_ref[at : at + 1, :].astype(jnp.float32) for at in range(model // LANES)], axis=1
    )
    left = jnp.concatenate([embed_ref[...].astype(jnp.float32) * gain, pos * gain], axis=0)
    left = left.astype(jnp.bfloat16)
    def keep(ref, scaled):
        high = scaled.astype(jnp.bfloat16)
        ref[:channels] = high
        ref[channels:] = (scaled - high.astype(jnp.float32)).astype(jnp.bfloat16)

    plain = jnp.concatenate([embed_ref[...], pos_ref[...]], axis=0)
    both = lax.dot_general(
        plain, embed_ref[...], (((1,), (1,)), ((), ())), preferred_element_type=jnp.float32
    )
    keep(gram_ref, both[:channels])
    natural_cross_ref[...] = 2.0 * both[channels:]
    level = jnp.sum(pos * pos, axis=-1, keepdims=True) / channels
    natural_level_ref[...] = jnp.broadcast_to(level, (patches, channels))

    for part, (index, at) in enumerate(parts):
        arrival(part).wait()
        if part + AHEAD < len(parts):
            arrival(part + AHEAD).start()
        if part + AHEAD == len(parts) - 1:
            first.start()
        here = slice(at, at + deep)
        product = dot(left[:, here], weight_ref[index, here])
        both = product if at == 0 else both + product
        if at + deep == model:
            keep(scaled_ref.at[index], both[:channels])
            natural_ref[index] = both[channels:]

    offset_ref[0] = natural_ref[0]

    def place(slot):
        to, at = pl.ds(slot, 1), pl.ds(order_ref[slot], 1)
        cross_ref[to, :] = natural_cross_ref[at, :]
        level_ref[to, :] = natural_level_ref[at, :]
        for index in range(1, 3):
            offset_ref[index, to, :] = natural_ref[index, at, :]

    if patches <= 16:
        for slot in range(patches):
            place(slot)
    else:
        pl.loop(0, patches)(place)
    first.wait()


def attend_kernel(
    partial_ref,
    embed_ref,
    scaled_ref,
    offset_ref,
    gram_ref,
    cross_ref,
    level_ref,
    natural_cross_ref,
    natural_level_ref,
    pos_mine_ref,
    select_ref,
    select_mine_ref,
    bias_ref,
    first_ref,
    out_weight_hbm,
    keep_ref,
    mine_ref,
    *rest,
):
    *send_refs, second_ref, sem = rest
    half = first_ref.shape[0]
    arrival = pltpu.make_async_copy(out_weight_hbm.at[pl.ds(half, half)], second_ref, sem)
    arrival.start()
    everyone, slots, window, channels = partial_ref.shape
    mps, share, model = keep_ref.shape
    roles = 1 + len(send_refs)
    group = mps * roles
    seqs = everyone // group
    patches = seqs * slots
    rows = patches * window
    cols = out_weight_hbm.shape[0]

    total = partial_ref[:seqs].astype(jnp.float32)
    for other in range(1, group):
        total = total + partial_ref[other * seqs : (other + 1) * seqs].astype(jnp.float32)
    latents = total.reshape(rows, channels).astype(jnp.bfloat16)
    own = dot(select_ref[...], latents).astype(jnp.bfloat16)

    def apply(part, table):
        return dot(jnp.concatenate([part, part], axis=1), table)

    def by_row(table):
        wide = jnp.broadcast_to(table[:, None], (patches, window, table.shape[1]))
        return wide.reshape(rows, table.shape[1])

    def by_patch(table):
        return jnp.concatenate([table] * (group * share // patches), axis=0)

    def scale_of(part, cross, level):
        slope = apply(part, gram_ref[...]) + cross
        squares = slope * part.astype(jnp.float32) + level
        mean = jnp.maximum(jnp.sum(squares, axis=-1, keepdims=True), 0.0) / model
        return lax.rsqrt(mean + 1e-06)

    scale = scale_of(latents, by_row(cross_ref[...]), by_row(level_ref[...]))
    own_scale = scale_of(own, by_patch(natural_cross_ref[...]), by_patch(natural_level_ref[...]))
    own_scale = own_scale * (HS**-0.5)

    def project(index):
        flat = apply(latents, scaled_ref[index]) + by_row(offset_ref[index])
        return (flat * scale).astype(jnp.bfloat16)

    query = (apply(own, scaled_ref[0]) + by_patch(offset_ref[0])).astype(jnp.bfloat16)
    key, value = project(1), project(2)
    bias = bias_ref[...]
    heads = []
    for head in range(cols // HS):
        at = slice(head * HS, (head + 1) * HS)
        scores = lax.dot_general(
            query[:, at], key[:, at], (((1,), (1,)), ((), ())), preferred_element_type=jnp.float32
        )
        scores = scores * own_scale + bias
        expo = jnp.exp(scores - jnp.max(scores, axis=-1, keepdims=True))
        probs = (expo / jnp.sum(expo, axis=-1, keepdims=True)).astype(jnp.bfloat16)
        heads.append(dot(probs, value[:, at]).astype(jnp.bfloat16))
    mine = dot(select_mine_ref[...], latents).astype(jnp.bfloat16)
    mine_ref[...] = dot(mine, embed_ref[...]) + pos_mine_ref[...]
    heads = jnp.concatenate(heads, axis=1)
    arrival.wait()
    role = lax.axis_index("role")
    for at in range(0, model, STRIP):
        here = slice(at, at + STRIP)
        mixed = dot(heads[:, :half], first_ref[:, here]) + dot(heads[:, half:], second_ref[:, here])
        for mp in range(mps):
            parts = [
                mixed[index * share : (index + 1) * share]
                for index in range(mp * roles, (mp + 1) * roles)
            ]

            def of_role(step):
                wanted, found = (role + step) % roles, parts[0]
                for index in range(1, roles):
                    found = jnp.where(wanted == index, parts[index], found)
                return found

            keep_ref[mp, :, here] = of_role(0)
            for step, send_ref in enumerate(send_refs):
                send_ref[mp, :, here] = of_role(step + 1).astype(jnp.bfloat16)


def add_kernel(roles, mine_ref, keep_ref, *refs):
    others, (total_ref, *send_refs) = refs[: roles - 1], refs[roles - 1 :]
    mps = keep_ref.shape[0]
    mp = lax.axis_index("mp")

    def total(step):
        at = (mp + step) % mps
        rows = keep_ref[at]
        for other in others:
            rows = rows + other[at].astype(jnp.float32)
        return rows

    total_ref[...] = mine_ref[...] + total(0)
    for step, send_ref in enumerate(send_refs):
        send_ref[...] = total(step + 1).astype(jnp.bfloat16)


def sum_kernel(total_ref, *refs):
    *others, out_ref = refs
    total = total_ref[...]
    for other in others:
        total = total + other[...].astype(jnp.float32)
    out_ref[...] = total.astype(jnp.bfloat16)


def around(block, axis, step):
    size = lax.axis_size(axis)
    return lax.ppermute(block, axis, [(i, (i + step) % size) for i in range(size)])


def on_device(
    gen_hidden,
    gen_out_weight,
    patch_order,
    frame_block,
    embed_weight,
    pos_table,
    norm_gain,
    qkv_weight,
    out_weight,
):
    slots, frames, depth = gen_hidden.shape
    channels, model = embed_weight.shape
    cols = qkv_weight.shape[2]
    out_weight = pltpu.with_memory_space_constraint(out_weight, pltpu.HBM)
    seqs = lax.axis_size("seq")
    group = lax.axis_size(GROUP)
    mps, roles = lax.axis_size("mp"), lax.axis_size("role")
    patches = seqs * slots
    frame_dev = frames // seqs
    window = frame_dev + 2 * REACH
    rows = window * patches
    own_rows = frame_dev * patches
    share = own_rows // group
    f32, bf16 = jnp.float32, jnp.bfloat16
    array = jax.ShapeDtypeStruct
    grant = (16 if rows <= STEP_ROWS else 40) * MIB

    windows = pl.pallas_call(
        functools.partial(latent_kernel, frame_dev),
        out_shape=array((group * seqs, slots, window, channels), bf16),
        in_specs=[HBM] * 2,
        out_specs=HBM,
        scratch_shapes=[
            pltpu.VMEM((slots, frames, depth), bf16),
            pltpu.VMEM((depth, channels), bf16),
            pltpu.VMEM((slots, frames + 2 * REACH, channels), f32),
            pltpu.VMEM((group * seqs, slots, window, channels), bf16),
            pltpu.SemaphoreType.DMA((1 + depth // LANES,)),
            pltpu.SemaphoreType.DMA((group,)),
        ],
        compiler_params=pltpu.CompilerParams(vmem_limit_bytes=12 * MIB),
        cost_estimate=pl.CostEstimate(
            flops=20_000_000_000, bytes_accessed=40_000_000, transcendentals=0
        ),
        name="partial_latents",
    )(
        pltpu.with_memory_space_constraint(gen_hidden, pltpu.HBM),
        pltpu.with_memory_space_constraint(gen_out_weight, pltpu.HBM),
    )
    moved = lax.all_to_all(
        windows,
        SCATTERED,
        split_axis=0,
        concat_axis=0,
        tiled=True,
    )

    products = pl.pallas_call(
        functools.partial(weights_kernel, frame_dev, window),
        out_shape=(
            array((3, 2 * channels, cols), bf16),
            array((3, patches, cols), f32),
            array((2 * channels, channels), bf16),
            array((patches, channels), f32),
            array((patches, channels), f32),
            array((patches, channels), f32),
            array((patches, channels), f32),
            array((share, model), f32),
            array((own_rows, rows), bf16),
            array((share, rows), bf16),
            array((own_rows, rows), f32),
            array((cols // 2, model), bf16),
        ),
        in_specs=[SMEM] * 2 + [VMEM] * 3 + [HBM] * 2,
        out_specs=(VMEM,) * 12,
        scratch_shapes=[
            pltpu.VMEM((3, patches, cols), f32),
            pltpu.VMEM((patches, model), f32),
            pltpu.VMEM((3, model, cols), bf16),
            pltpu.SemaphoreType.DMA((3 * (model // min(model, DEPTH)),)),
            pltpu.SemaphoreType.DMA(()),
        ],
        compiler_params=pltpu.CompilerParams(vmem_limit_bytes=24 * MIB),
        cost_estimate=pl.CostEstimate(
            flops=2 * (channels + patches) * model * 3 * cols,
            bytes_accessed=2 * model * 3 * cols,
            transcendentals=0,
        ),
        name="weight_products",
    )(
        patch_order,
        frame_block,
        embed_weight,
        pos_table,
        norm_gain.reshape(model // LANES, LANES),
        pltpu.with_memory_space_constraint(jnp.transpose(qkv_weight, (1, 0, 2)), pltpu.HBM),
        out_weight,
    )

    keep, mine, *sent = pl.pallas_call(
        attend_kernel,
        out_shape=(
            array((mps, share, model), f32),
            array((share, model), f32),
            *[array((mps, share, model), bf16)] * (roles - 1),
        ),
        in_specs=[VMEM] * 14 + [HBM],
        out_specs=(VMEM,) * (1 + roles),
        scratch_shapes=[
            pltpu.VMEM((cols - cols // 2, model), bf16),
            pltpu.SemaphoreType.DMA(()),
        ],
        compiler_params=pltpu.CompilerParams(vmem_limit_bytes=grant),
        name="attend",
    )(
        moved,
        embed_weight,
        *products,
        out_weight,
    )
    small = pltpu.CompilerParams(vmem_limit_bytes=8 * MIB)
    sent = [around(block, "role", step + 1) for step, block in enumerate(sent)]
    total, *sent = pl.pallas_call(
        functools.partial(add_kernel, roles),
        out_shape=(array((share, model), f32), *[array((share, model), bf16)] * (mps - 1)),
        in_specs=[VMEM] * (1 + roles),
        out_specs=(VMEM,) * mps,
        compiler_params=small,
        name="sum_over_role",
    )(mine, keep, *sent)
    sent = [around(block, "mp", step + 1) for step, block in enumerate(sent)]
    return pl.pallas_call(
        sum_kernel,
        out_shape=array((share, model), bf16),
        in_specs=[VMEM] * mps,
        out_specs=VMEM,
        compiler_params=small,
        name="sum_over_mp",
    )(total, *sent)


def solution(mesh):
    in_specs = (
        P("seq", None, ("mp", "role")),
        P(("mp", "role"), None),
        P(),
        P(),
        P(),
        P(),
        P(),
        P(None, None, ("mp", "role")),
        P(("mp", "role"), None),
    )
    out_specs = P(("seq", "mp", "role"), None)
    return jax.shard_map(
        on_device, mesh=mesh, in_specs=in_specs, out_specs=out_specs, check_vma=False
    )
```

```python
import functools

import jax
import jax.numpy as jnp
from jax import lax
from jax.experimental import pallas as pl
from jax.experimental.pallas import tpu as pltpu
from jax.sharding import PartitionSpec as P

HS = 128
MOSTB = 4
REACH = MOSTB - 1
GROUP = ("mp", "role")
SCATTERED = ("role", "mp", "seq")
LANES = 128
STEP_ROWS = 256
DEPTH = 1024
AHEAD = 4
STRIP = 512
MIB = 1024 * 1024
VMEM = pl.BlockSpec(memory_space=pltpu.VMEM)
SMEM = pl.BlockSpec(memory_space=pltpu.SMEM)
HBM = pl.BlockSpec(memory_space=pltpu.HBM)


def dot(a, b):
    return jnp.dot(a, b, preferred_element_type=jnp.float32)


def latent_kernel(
    frame_dev,
    hidden_hbm,
    weight_hbm,
    out_hbm,
    hidden_ref,
    weight_ref,
    padded_ref,
    out_ref,
    in_sems,
    out_sems,
):
    slots, frames, depth = hidden_ref.shape
    everyone, _, window, channels = out_ref.shape
    seqs = frames // frame_dev
    arrivals = [pltpu.make_async_copy(hidden_hbm, hidden_ref, in_sems.at[0])]
    for index, at in enumerate(range(0, depth, LANES)):
        piece = pl.ds(at, LANES)
        arrivals.append(
            pltpu.make_async_copy(
                weight_hbm.at[piece], weight_ref.at[piece], in_sems.at[index + 1]
            )
        )
    for copy in arrivals:
        copy.start()
    padded_ref[...] = jnp.zeros_like(padded_ref)
    for copy in arrivals:
        copy.wait()
    for slot in range(slots):
        padded_ref[slot, REACH : REACH + frames] = dot(hidden_ref[slot], weight_ref[...])
    pieces = [
        padded_ref[:, to * frame_dev : to * frame_dev + window].astype(out_ref.dtype)
        for to in range(seqs)
    ]
    leaving = []
    for index, first in enumerate(range(0, everyone, seqs)):
        for to in range(seqs):
            out_ref[first + to] = pieces[to]
        part = pl.ds(first, seqs)
        leaving.append(
            pltpu.make_async_copy(out_ref.at[part], out_hbm.at[part], out_sems.at[index])
        )
        leaving[-1].start()
    for copy in leaving:
        copy.wait()


def weights_kernel(
    frame_dev,
    window,
    mps,
    roles,
    order_ref,
    block_ref,
    embed_ref,
    pos_ref,
    gain_ref,
    weight_hbm,
    out_weight_hbm,
    scaled_ref,
    offset_ref,
    gram_ref,
    cross_ref,
    level_ref,
    own_offset_ref,
    own_cross_ref,
    own_level_ref,
    pos_mine_ref,
    select_ref,
    bias_ref,
    first_ref,
    natural_ref,
    natural_cross_ref,
    natural_level_ref,
    pos_all_ref,
    weight_ref,
    sems,
    first_sem,
):
    channels, model = embed_ref.shape
    patches = pos_ref.shape[0]
    frames = block_ref.shape[0]
    own_rows, rows = bias_ref.shape
    share = pos_mine_ref.shape[0]
    device = lax.axis_index("seq")
    mp, role = lax.axis_index("mp"), lax.axis_index("role")
    firsts = [
        (((mp + along) % mps) * roles + (role + across) % roles) * share
        for along in range(mps)
        for across in range(roles)
    ]

    deep = min(model, DEPTH)
    parts = [(index, at) for index in range(3) for at in range(0, model, deep)]

    def arrival(part):
        index, at = parts[part]
        place = (index, pl.ds(at, deep))
        return pltpu.make_async_copy(weight_hbm.at[place], weight_ref.at[place], sems.at[part])

    first = pltpu.make_async_copy(
        out_weight_hbm.at[pl.ds(0, first_ref.shape[0])], first_ref, first_sem
    )
    for part in range(AHEAD):
        arrival(part).start()

    pos = pos_ref[...].astype(jnp.float32)
    pos_all_ref[...] = pos

    column = lax.broadcasted_iota(jnp.int32, (1, rows), 1)
    column_slot, column_frame = column // window, column % window

    def patch_at(slot, found):
        return jnp.where(column_slot == slot, order_ref[slot], found)

    column_patch = jnp.zeros((1, rows), jnp.int32)
    if patches <= 16:
        for slot in range(patches):
            column_patch = patch_at(slot, column_patch)
    else:
        column_patch = lax.fori_loop(0, patches, patch_at, column_patch)

    row = lax.broadcasted_iota(jnp.int32, (own_rows, rows), 0)
    natural = jnp.zeros((own_rows, rows), jnp.int32)
    for index, first_row in enumerate(firsts):
        natural = jnp.where(row // share == index, first_row + row % share, natural)
    row_patch, row_frame = natural % patches, natural // patches
    hit = jnp.logical_and(column_patch == row_patch, column_frame == row_frame + REACH)
    select_ref[...] = jnp.where(hit, 1.0, 0.0).astype(jnp.bfloat16)

    def block_of(frame):
        inside = jnp.logical_and(frame >= 0, frame < frames)
        return jnp.where(inside, block_ref[jnp.clip(frame, 0, frames - 1)], -1)

    column_block = jnp.full((1, rows), -1, jnp.int32)
    for frame in range(window):
        found = block_of(device * frame_dev - REACH + frame)
        column_block = jnp.where(column_frame == frame, found, column_block)
    row_block = jnp.full((own_rows, rows), -2, jnp.int32)
    for frame in range(frame_dev):
        row_block = jnp.where(row_frame == frame, block_of(device * frame_dev + frame), row_block)
    bias_ref[...] = jnp.where(row_block == column_block, 0.0, -1e30)

    gain = jnp.concatenate(
        [gain_ref[at : at + 1, :].astype(jnp.float32) for at in range(model // LANES)], axis=1
    )
    left = jnp.concatenate([embed_ref[...].astype(jnp.float32) * gain, pos * gain], axis=0)
    left = left.astype(jnp.bfloat16)
    def keep(ref, scaled):
        high = scaled.astype(jnp.bfloat16)
        ref[:channels] = high
        ref[channels:] = (scaled - high.astype(jnp.float32)).astype(jnp.bfloat16)

    plain = jnp.concatenate([embed_ref[...], pos_ref[...]], axis=0)
    both = lax.dot_general(
        plain, embed_ref[...], (((1,), (1,)), ((), ())), preferred_element_type=jnp.float32
    )
    keep(gram_ref, both[:channels])
    natural_cross_ref[...] = 2.0 * both[channels:]
    level = jnp.sum(pos * pos, axis=-1, keepdims=True) / channels
    natural_level_ref[...] = jnp.broadcast_to(level, (patches, channels))

    for part, (index, at) in enumerate(parts):
        arrival(part).wait()
        if part + AHEAD < len(parts):
            arrival(part + AHEAD).start()
        if part + AHEAD == len(parts) - 1:
            first.start()
        here = slice(at, at + deep)
        product = dot(left[:, here], weight_ref[index, here])
        both = product if at == 0 else both + product
        if at + deep == model:
            keep(scaled_ref.at[index], both[:channels])
            natural_ref[index] = both[channels:]

    def place(slot):
        to, at = pl.ds(slot, 1), pl.ds(order_ref[slot], 1)
        cross_ref[to, :] = natural_cross_ref[at, :]
        level_ref[to, :] = natural_level_ref[at, :]
        for index in range(1, 3):
            offset_ref[index - 1, to, :] = natural_ref[index, at, :]

    def place_own(index, within):
        to = pl.ds(index * share + within, 1)
        at = pl.ds((firsts[index] + within) % patches, 1)
        own_offset_ref[to, :] = natural_ref[0, at, :]
        own_cross_ref[to, :] = natural_cross_ref[at, :]
        own_level_ref[to, :] = natural_level_ref[at, :]
        if index == 0:
            pos_mine_ref[to, :] = pos_all_ref[at, :]

    if patches <= 16:
        for slot in range(patches):
            place(slot)
    else:
        pl.loop(0, patches)(place)
    for index in range(len(firsts)):
        if share <= 16:
            for within in range(share):
                place_own(index, within)
        else:
            pl.loop(0, share)(functools.partial(place_own, index))
    first.wait()


def attend_kernel(
    partial_ref,
    scaled_ref,
    offset_ref,
    gram_ref,
    cross_ref,
    level_ref,
    own_offset_ref,
    own_cross_ref,
    own_level_ref,
    select_ref,
    bias_ref,
    first_ref,
    out_weight_hbm,
    mine_ref,
    keep_ref,
    *rest,
):
    *send_refs, second_ref, sem = rest
    half = first_ref.shape[0]
    arrival = pltpu.make_async_copy(out_weight_hbm.at[pl.ds(half, half)], second_ref, sem)
    arrival.start()
    everyone, slots, window, channels = partial_ref.shape
    share, model = keep_ref.shape
    group = 1 + len(send_refs)
    seqs = everyone // group
    patches = seqs * slots
    rows = patches * window
    cols = out_weight_hbm.shape[0]

    total = partial_ref[:seqs].astype(jnp.float32)
    for other in range(1, group):
        total = total + partial_ref[other * seqs : (other + 1) * seqs].astype(jnp.float32)
    latents = total.reshape(rows, channels).astype(jnp.bfloat16)
    own = dot(select_ref[...], latents).astype(jnp.bfloat16)
    mine_ref[...] = own[:share]

    def apply(part, table):
        return dot(jnp.concatenate([part, part], axis=1), table)

    def by_row(table):
        wide = jnp.broadcast_to(table[:, None], (patches, window, table.shape[1]))
        return wide.reshape(rows, table.shape[1])

    def scale_of(part, cross, level):
        slope = apply(part, gram_ref[...]) + cross
        squares = slope * part.astype(jnp.float32) + level
        mean = jnp.maximum(jnp.sum(squares, axis=-1, keepdims=True), 0.0) / model
        return lax.rsqrt(mean + 1e-06)

    scale = scale_of(latents, by_row(cross_ref[...]), by_row(level_ref[...]))
    own_scale = scale_of(own, own_cross_ref[...], own_level_ref[...]) * (HS**-0.5)

    def project(index):
        flat = apply(latents, scaled_ref[index]) + by_row(offset_ref[index - 1])
        return (flat * scale).astype(jnp.bfloat16)

    query = (apply(own, scaled_ref[0]) + own_offset_ref[...]).astype(jnp.bfloat16)
    key, value = project(1), project(2)
    bias = bias_ref[...]
    heads = []
    for head in range(cols // HS):
        at = slice(head * HS, (head + 1) * HS)
        scores = lax.dot_general(
            query[:, at], key[:, at], (((1,), (1,)), ((), ())), preferred_element_type=jnp.float32
        )
        scores = scores * own_scale + bias
        expo = jnp.exp(scores - jnp.max(scores, axis=-1, keepdims=True))
        probs = (expo / jnp.sum(expo, axis=-1, keepdims=True)).astype(jnp.bfloat16)
        heads.append(dot(probs, value[:, at]).astype(jnp.bfloat16))
    heads = jnp.concatenate(heads, axis=1)
    arrival.wait()
    for at in range(0, model, STRIP):
        here = slice(at, at + STRIP)
        mixed = dot(heads[:, :half], first_ref[:, here]) + dot(heads[:, half:], second_ref[:, here])
        keep_ref[:, here] = mixed[:share]
        for index, send_ref in enumerate(send_refs):
            part = mixed[(index + 1) * share : (index + 2) * share]
            send_ref[:, here] = part.astype(jnp.bfloat16)


def residual_kernel(mine_ref, embed_ref, pos_ref, out_ref):
    out_ref[...] = dot(mine_ref[...], embed_ref[...]) + pos_ref[...]


def sum_kernel(residual_ref, keep_ref, *refs):
    *others, out_ref = refs
    total = residual_ref[...] + keep_ref[...]
    for other in others:
        total = total + other[...].astype(jnp.float32)
    out_ref[...] = total.astype(jnp.bfloat16)


def to_member(block, along, across):
    mps, roles = lax.axis_size("mp"), lax.axis_size("role")
    route = [
        (mp * roles + role, ((mp + along) % mps) * roles + (role + across) % roles)
        for mp in range(mps)
        for role in range(roles)
    ]
    return lax.ppermute(block, GROUP, route)


def on_device(
    gen_hidden,
    gen_out_weight,
    patch_order,
    frame_block,
    embed_weight,
    pos_table,
    norm_gain,
    qkv_weight,
    out_weight,
):
    slots, frames, depth = gen_hidden.shape
    channels, model = embed_weight.shape
    cols = qkv_weight.shape[2]
    out_weight = pltpu.with_memory_space_constraint(out_weight, pltpu.HBM)
    seqs = lax.axis_size("seq")
    group = lax.axis_size(GROUP)
    mps, roles = lax.axis_size("mp"), lax.axis_size("role")
    patches = seqs * slots
    frame_dev = frames // seqs
    window = frame_dev + 2 * REACH
    rows = window * patches
    own_rows = frame_dev * patches
    share = own_rows // group
    f32, bf16 = jnp.float32, jnp.bfloat16
    array = jax.ShapeDtypeStruct
    grant = (16 if rows <= STEP_ROWS else 40) * MIB

    windows = pl.pallas_call(
        functools.partial(latent_kernel, frame_dev),
        out_shape=array((group * seqs, slots, window, channels), bf16),
        in_specs=[HBM] * 2,
        out_specs=HBM,
        scratch_shapes=[
            pltpu.VMEM((slots, frames, depth), bf16),
            pltpu.VMEM((depth, channels), bf16),
            pltpu.VMEM((slots, frames + 2 * REACH, channels), f32),
            pltpu.VMEM((group * seqs, slots, window, channels), bf16),
            pltpu.SemaphoreType.DMA((1 + depth // LANES,)),
            pltpu.SemaphoreType.DMA((group,)),
        ],
        compiler_params=pltpu.CompilerParams(vmem_limit_bytes=12 * MIB),
        cost_estimate=pl.CostEstimate(
            flops=20_000_000_000, bytes_accessed=40_000_000, transcendentals=0
        ),
        name="partial_latents",
    )(
        pltpu.with_memory_space_constraint(gen_hidden, pltpu.HBM),
        pltpu.with_memory_space_constraint(gen_out_weight, pltpu.HBM),
    )
    moved = lax.all_to_all(
        windows,
        SCATTERED,
        split_axis=0,
        concat_axis=0,
        tiled=True,
    )

    *products, pos_mine, select, bias, first = pl.pallas_call(
        functools.partial(weights_kernel, frame_dev, window, mps, roles),
        out_shape=(
            array((3, 2 * channels, cols), bf16),
            array((2, patches, cols), f32),
            array((2 * channels, channels), bf16),
            array((patches, channels), f32),
            array((patches, channels), f32),
            array((own_rows, cols), f32),
            array((own_rows, channels), f32),
            array((own_rows, channels), f32),
            array((share, model), f32),
            array((own_rows, rows), bf16),
            array((own_rows, rows), f32),
            array((cols // 2, model), bf16),
        ),
        in_specs=[SMEM] * 2 + [VMEM] * 3 + [HBM] * 2,
        out_specs=(VMEM,) * 12,
        scratch_shapes=[
            pltpu.VMEM((3, patches, cols), f32),
            pltpu.VMEM((patches, channels), f32),
            pltpu.VMEM((patches, channels), f32),
            pltpu.VMEM((patches, model), f32),
            pltpu.VMEM((3, model, cols), bf16),
            pltpu.SemaphoreType.DMA((3 * (model // min(model, DEPTH)),)),
            pltpu.SemaphoreType.DMA(()),
        ],
        compiler_params=pltpu.CompilerParams(vmem_limit_bytes=24 * MIB),
        cost_estimate=pl.CostEstimate(
            flops=2 * (channels + patches) * model * 3 * cols,
            bytes_accessed=2 * model * 3 * cols,
            transcendentals=0,
        ),
        name="weight_products",
    )(
        patch_order,
        frame_block,
        embed_weight,
        pos_table,
        norm_gain.reshape(model // LANES, LANES),
        pltpu.with_memory_space_constraint(jnp.transpose(qkv_weight, (1, 0, 2)), pltpu.HBM),
        out_weight,
    )

    mine, keep, *sent = pl.pallas_call(
        attend_kernel,
        out_shape=(
            array((share, channels), bf16),
            array((share, model), f32),
            *[array((share, model), bf16)] * (group - 1),
        ),
        in_specs=[VMEM] * 12 + [HBM],
        out_specs=(VMEM,) * (1 + group),
        scratch_shapes=[
            pltpu.VMEM((cols - cols // 2, model), bf16),
            pltpu.SemaphoreType.DMA(()),
        ],
        compiler_params=pltpu.CompilerParams(vmem_limit_bytes=grant),
        name="attend",
    )(
        moved,
        *products,
        select,
        bias,
        first,
        out_weight,
    )
    small = pltpu.CompilerParams(vmem_limit_bytes=8 * MIB)
    places = [(along, across) for along in range(mps) for across in range(roles)][1:]
    routed = list(zip(places, sent))
    routed.sort(key=lambda item: item[0][0] == 0)
    received = [to_member(block, *place) for place, block in routed]
    residual = pl.pallas_call(
        residual_kernel,
        out_shape=array((share, model), f32),
        in_specs=[VMEM] * 3,
        out_specs=VMEM,
        compiler_params=small,
        cost_estimate=pl.CostEstimate(
            flops=2 * share * channels * model,
            bytes_accessed=2 * channels * model,
            transcendentals=0,
        ),
        name="residual",
    )(mine, embed_weight, pos_mine)
    return pl.pallas_call(
        sum_kernel,
        out_shape=array((share, model), bf16),
        in_specs=[VMEM] * (1 + group),
        out_specs=VMEM,
        compiler_params=small,
        name="final_sum",
    )(residual, keep, *received)


def solution(mesh):
    in_specs = (
        P("seq", None, ("mp", "role")),
        P(("mp", "role"), None),
        P(),
        P(),
        P(),
        P(),
        P(),
        P(None, None, ("mp", "role")),
        P(("mp", "role"), None),
    )
    out_specs = P(("seq", "mp", "role"), None)
    return jax.shard_map(
        on_device, mesh=mesh, in_specs=in_specs, out_specs=out_specs, check_vma=False
    )
```

```python
import functools

import jax
import jax.numpy as jnp
from jax import lax
from jax.experimental import pallas as pl
from jax.experimental.pallas import tpu as pltpu
from jax.sharding import PartitionSpec as P

HS = 128
MOSTB = 4
REACH = MOSTB - 1
GROUP = ("mp", "role")
SCATTERED = ("role", "mp", "seq")
LANES = 128
STEP_ROWS = 256
DEPTH = 1024
AHEAD = 4
STRIP = 512
MIB = 1024 * 1024
VMEM = pl.BlockSpec(memory_space=pltpu.VMEM)
SMEM = pl.BlockSpec(memory_space=pltpu.SMEM)
HBM = pl.BlockSpec(memory_space=pltpu.HBM)


def dot(a, b):
    return jnp.dot(a, b, preferred_element_type=jnp.float32)


def latent_kernel(
    frame_dev,
    hidden_hbm,
    weight_hbm,
    out_hbm,
    hidden_ref,
    weight_ref,
    padded_ref,
    out_ref,
    in_sems,
    out_sems,
):
    slots, frames, depth = hidden_ref.shape
    everyone, _, window, channels = out_ref.shape
    seqs = frames // frame_dev
    arrivals = [pltpu.make_async_copy(hidden_hbm, hidden_ref, in_sems.at[0])]
    for index, at in enumerate(range(0, depth, LANES)):
        piece = pl.ds(at, LANES)
        arrivals.append(
            pltpu.make_async_copy(
                weight_hbm.at[piece], weight_ref.at[piece], in_sems.at[index + 1]
            )
        )
    for copy in arrivals:
        copy.start()
    padded_ref[...] = jnp.zeros_like(padded_ref)
    for copy in arrivals:
        copy.wait()
    for slot in range(slots):
        padded_ref[slot, REACH : REACH + frames] = dot(hidden_ref[slot], weight_ref[...])
    pieces = [
        padded_ref[:, to * frame_dev : to * frame_dev + window].astype(out_ref.dtype)
        for to in range(seqs)
    ]
    leaving = []
    for index, first in enumerate(range(0, everyone, seqs)):
        for to in range(seqs):
            out_ref[first + to] = pieces[to]
        part = pl.ds(first, seqs)
        leaving.append(
            pltpu.make_async_copy(out_ref.at[part], out_hbm.at[part], out_sems.at[index])
        )
        leaving[-1].start()
    for copy in leaving:
        copy.wait()


def weights_kernel(
    frame_dev,
    window,
    mps,
    roles,
    order_ref,
    block_ref,
    embed_ref,
    pos_ref,
    gain_ref,
    weight_hbm,
    out_weight_hbm,
    scaled_ref,
    offset_ref,
    gram_ref,
    cross_ref,
    level_ref,
    own_offset_ref,
    own_cross_ref,
    own_level_ref,
    pos_mine_ref,
    select_ref,
    bias_ref,
    first_ref,
    natural_ref,
    natural_cross_ref,
    natural_level_ref,
    pos_all_ref,
    weight_ref,
    sems,
    first_sem,
):
    channels, model = embed_ref.shape
    patches = pos_ref.shape[0]
    frames = block_ref.shape[0]
    own_rows, rows = bias_ref.shape
    share = pos_mine_ref.shape[0]
    device = lax.axis_index("seq")
    mp, role = lax.axis_index("mp"), lax.axis_index("role")
    firsts = [
        (((mp + along) % mps) * roles + (role + across) % roles) * share
        for along in range(mps)
        for across in range(roles)
    ]

    deep = min(model, DEPTH)
    parts = [(index, at) for index in range(3) for at in range(0, model, deep)]

    def arrival(part):
        index, at = parts[part]
        place = (index, pl.ds(at, deep))
        return pltpu.make_async_copy(weight_hbm.at[place], weight_ref.at[place], sems.at[part])

    first = pltpu.make_async_copy(
        out_weight_hbm.at[pl.ds(0, first_ref.shape[0])], first_ref, first_sem
    )
    for part in range(AHEAD):
        arrival(part).start()

    pos = pos_ref[...].astype(jnp.float32)
    pos_all_ref[...] = pos

    column = lax.broadcasted_iota(jnp.int32, (1, rows), 1)
    column_slot, column_frame = column // window, column % window

    def patch_at(slot, found):
        return jnp.where(column_slot == slot, order_ref[slot], found)

    column_patch = jnp.zeros((1, rows), jnp.int32)
    if patches <= 16:
        for slot in range(patches):
            column_patch = patch_at(slot, column_patch)
    else:
        column_patch = lax.fori_loop(0, patches, patch_at, column_patch)

    row = lax.broadcasted_iota(jnp.int32, (own_rows, rows), 0)
    natural = jnp.zeros((own_rows, rows), jnp.int32)
    for index, first_row in enumerate(firsts):
        natural = jnp.where(row // share == index, first_row + row % share, natural)
    row_patch, row_frame = natural % patches, natural // patches
    hit = jnp.logical_and(column_patch == row_patch, column_frame == row_frame + REACH)
    select_ref[...] = jnp.where(hit, 1.0, 0.0).astype(jnp.bfloat16)

    def block_of(frame):
        inside = jnp.logical_and(frame >= 0, frame < frames)
        return jnp.where(inside, block_ref[jnp.clip(frame, 0, frames - 1)], -1)

    column_block = jnp.full((1, rows), -1, jnp.int32)
    for frame in range(window):
        found = block_of(device * frame_dev - REACH + frame)
        column_block = jnp.where(column_frame == frame, found, column_block)
    row_block = jnp.full((own_rows, rows), -2, jnp.int32)
    for frame in range(frame_dev):
        row_block = jnp.where(row_frame == frame, block_of(device * frame_dev + frame), row_block)
    bias_ref[...] = jnp.where(row_block == column_block, 0.0, -1e30)

    gain = jnp.concatenate(
        [gain_ref[at : at + 1, :].astype(jnp.float32) for at in range(model // LANES)], axis=1
    )
    left = jnp.concatenate([embed_ref[...].astype(jnp.float32) * gain, pos * gain], axis=0)
    left = left.astype(jnp.bfloat16)
    def keep(ref, scaled):
        high = scaled.astype(jnp.bfloat16)
        ref[:channels] = high
        ref[channels:] = (scaled - high.astype(jnp.float32)).astype(jnp.bfloat16)

    plain = jnp.concatenate([embed_ref[...], pos_ref[...]], axis=0)
    both = lax.dot_general(
        plain, embed_ref[...], (((1,), (1,)), ((), ())), preferred_element_type=jnp.float32
    )
    keep(gram_ref, both[:channels])
    natural_cross_ref[...] = 2.0 * both[channels:]
    level = jnp.sum(pos * pos, axis=-1, keepdims=True) / channels
    natural_level_ref[...] = jnp.broadcast_to(level, (patches, channels))

    def each(count, place):
        if count <= 16:
            for at in range(count):
                place(at)
        else:
            pl.loop(0, count)(place)

    def own_row(index, within):
        to = pl.ds(index * share + within, 1)
        return to, pl.ds((firsts[index] + within) % patches, 1)

    def place_slot(slot):
        to, at = pl.ds(slot, 1), pl.ds(order_ref[slot], 1)
        cross_ref[to, :] = natural_cross_ref[at, :]
        level_ref[to, :] = natural_level_ref[at, :]

    def place_own(index, within):
        to, at = own_row(index, within)
        own_cross_ref[to, :] = natural_cross_ref[at, :]
        own_level_ref[to, :] = natural_level_ref[at, :]
        if index == 0:
            pos_mine_ref[to, :] = pos_all_ref[at, :]

    def place_query(index, within):
        to, at = own_row(index, within)
        own_offset_ref[to, :] = natural_ref[0, at, :]

    def place_pair(index, slot):
        offset_ref[index - 1, pl.ds(slot, 1), :] = natural_ref[index, pl.ds(order_ref[slot], 1), :]

    each(patches, place_slot)
    for index in range(len(firsts)):
        each(share, functools.partial(place_own, index))

    for part, (index, at) in enumerate(parts):
        arrival(part).wait()
        if part + AHEAD < len(parts):
            arrival(part + AHEAD).start()
        if part + AHEAD == len(parts) - 1:
            first.start()
        here = slice(at, at + deep)
        product = dot(left[:, here], weight_ref[index, here])
        both = product if at == 0 else both + product
        if at + deep == model:
            keep(scaled_ref.at[index], both[:channels])
            natural_ref[index] = both[channels:]
            if index == 0:
                for member in range(len(firsts)):
                    each(share, functools.partial(place_query, member))
            else:
                each(patches, functools.partial(place_pair, index))
    first.wait()


def attend_kernel(
    partial_ref,
    scaled_ref,
    offset_ref,
    gram_ref,
    cross_ref,
    level_ref,
    own_offset_ref,
    own_cross_ref,
    own_level_ref,
    select_ref,
    bias_ref,
    first_ref,
    out_weight_hbm,
    mine_ref,
    keep_ref,
    *rest,
):
    *send_refs, second_ref, sem = rest
    half = first_ref.shape[0]
    arrival = pltpu.make_async_copy(out_weight_hbm.at[pl.ds(half, half)], second_ref, sem)
    arrival.start()
    everyone, slots, window, channels = partial_ref.shape
    share, model = keep_ref.shape
    group = 1 + len(send_refs)
    seqs = everyone // group
    patches = seqs * slots
    rows = patches * window
    cols = out_weight_hbm.shape[0]

    total = partial_ref[:seqs].astype(jnp.float32)
    for other in range(1, group):
        total = total + partial_ref[other * seqs : (other + 1) * seqs].astype(jnp.float32)
    latents = total.reshape(rows, channels).astype(jnp.bfloat16)
    own = dot(select_ref[...], latents).astype(jnp.bfloat16)

    def apply(part, table):
        return dot(jnp.concatenate([part, part], axis=1), table)

    def by_row(table):
        wide = jnp.broadcast_to(table[:, None], (patches, window, table.shape[1]))
        return wide.reshape(rows, table.shape[1])

    def scale_of(part, cross, level):
        slope = apply(part, gram_ref[...]) + cross
        squares = slope * part.astype(jnp.float32) + level
        mean = jnp.maximum(jnp.sum(squares, axis=-1, keepdims=True), 0.0) / model
        return lax.rsqrt(mean + 1e-06)

    scale = scale_of(latents, by_row(cross_ref[...]), by_row(level_ref[...]))
    own_scale = scale_of(own, own_cross_ref[...], own_level_ref[...]) * (HS**-0.5)

    def project(index):
        flat = apply(latents, scaled_ref[index]) + by_row(offset_ref[index - 1])
        return (flat * scale).astype(jnp.bfloat16)

    query = (apply(own, scaled_ref[0]) + own_offset_ref[...]).astype(jnp.bfloat16)
    key, value = project(1), project(2)
    bias = bias_ref[...]
    heads = []
    for head in range(cols // HS):
        at = slice(head * HS, (head + 1) * HS)
        scores = lax.dot_general(
            query[:, at], key[:, at], (((1,), (1,)), ((), ())), preferred_element_type=jnp.float32
        )
        scores = scores * own_scale + bias
        expo = jnp.exp(scores - jnp.max(scores, axis=-1, keepdims=True))
        probs = (expo / jnp.sum(expo, axis=-1, keepdims=True)).astype(jnp.bfloat16)
        heads.append(dot(probs, value[:, at]).astype(jnp.bfloat16))
    heads = jnp.concatenate(heads, axis=1)
    arrival.wait()
    for at in range(0, model, STRIP):
        here = slice(at, at + STRIP)
        mixed = dot(heads[:, :half], first_ref[:, here]) + dot(heads[:, half:], second_ref[:, here])
        keep_ref[:, here] = mixed[:share]
        for index, send_ref in enumerate(send_refs):
            part = mixed[(index + 1) * share : (index + 2) * share]
            send_ref[:, here] = part.astype(jnp.bfloat16)
    mine_ref[...] = own[:share]


def residual_kernel(mine_ref, embed_ref, pos_ref, out_ref):
    out_ref[...] = dot(mine_ref[...], embed_ref[...]) + pos_ref[...]


def sum_kernel(residual_ref, keep_ref, *refs):
    *others, out_ref = refs
    total = residual_ref[...] + keep_ref[...]
    for other in others:
        total = total + other[...].astype(jnp.float32)
    out_ref[...] = total.astype(jnp.bfloat16)


def to_member(block, along, across):
    mps, roles = lax.axis_size("mp"), lax.axis_size("role")
    route = [
        (mp * roles + role, ((mp + along) % mps) * roles + (role + across) % roles)
        for mp in range(mps)
        for role in range(roles)
    ]
    return lax.ppermute(block, GROUP, route)


def on_device(
    gen_hidden,
    gen_out_weight,
    patch_order,
    frame_block,
    embed_weight,
    pos_table,
    norm_gain,
    qkv_weight,
    out_weight,
):
    slots, frames, depth = gen_hidden.shape
    channels, model = embed_weight.shape
    cols = qkv_weight.shape[2]
    out_weight = pltpu.with_memory_space_constraint(out_weight, pltpu.HBM)
    seqs = lax.axis_size("seq")
    group = lax.axis_size(GROUP)
    mps, roles = lax.axis_size("mp"), lax.axis_size("role")
    patches = seqs * slots
    frame_dev = frames // seqs
    window = frame_dev + 2 * REACH
    rows = window * patches
    own_rows = frame_dev * patches
    share = own_rows // group
    f32, bf16 = jnp.float32, jnp.bfloat16
    array = jax.ShapeDtypeStruct
    grant = (16 if rows <= STEP_ROWS else 40) * MIB

    windows = pl.pallas_call(
        functools.partial(latent_kernel, frame_dev),
        out_shape=array((group * seqs, slots, window, channels), bf16),
        in_specs=[HBM] * 2,
        out_specs=HBM,
        scratch_shapes=[
            pltpu.VMEM((slots, frames, depth), bf16),
            pltpu.VMEM((depth, channels), bf16),
            pltpu.VMEM((slots, frames + 2 * REACH, channels), f32),
            pltpu.VMEM((group * seqs, slots, window, channels), bf16),
            pltpu.SemaphoreType.DMA((1 + depth // LANES,)),
            pltpu.SemaphoreType.DMA((group,)),
        ],
        compiler_params=pltpu.CompilerParams(vmem_limit_bytes=12 * MIB),
        cost_estimate=pl.CostEstimate(
            flops=20_000_000_000, bytes_accessed=40_000_000, transcendentals=0
        ),
        name="partial_latents",
    )(
        pltpu.with_memory_space_constraint(gen_hidden, pltpu.HBM),
        pltpu.with_memory_space_constraint(gen_out_weight, pltpu.HBM),
    )
    moved = lax.all_to_all(
        windows,
        SCATTERED,
        split_axis=0,
        concat_axis=0,
        tiled=True,
    )

    *products, pos_mine, select, bias, first = pl.pallas_call(
        functools.partial(weights_kernel, frame_dev, window, mps, roles),
        out_shape=(
            array((3, 2 * channels, cols), bf16),
            array((2, patches, cols), f32),
            array((2 * channels, channels), bf16),
            array((patches, channels), f32),
            array((patches, channels), f32),
            array((own_rows, cols), f32),
            array((own_rows, channels), f32),
            array((own_rows, channels), f32),
            array((share, model), f32),
            array((own_rows, rows), bf16),
            array((own_rows, rows), f32),
            array((cols // 2, model), bf16),
        ),
        in_specs=[SMEM] * 2 + [VMEM] * 3 + [HBM] * 2,
        out_specs=(VMEM,) * 12,
        scratch_shapes=[
            pltpu.VMEM((3, patches, cols), f32),
            pltpu.VMEM((patches, channels), f32),
            pltpu.VMEM((patches, channels), f32),
            pltpu.VMEM((patches, model), f32),
            pltpu.VMEM((3, model, cols), bf16),
            pltpu.SemaphoreType.DMA((3 * (model // min(model, DEPTH)),)),
            pltpu.SemaphoreType.DMA(()),
        ],
        compiler_params=pltpu.CompilerParams(vmem_limit_bytes=24 * MIB),
        cost_estimate=pl.CostEstimate(
            flops=2 * (channels + patches) * model * 3 * cols,
            bytes_accessed=2 * model * 3 * cols,
            transcendentals=0,
        ),
        name="weight_products",
    )(
        patch_order,
        frame_block,
        embed_weight,
        pos_table,
        norm_gain.reshape(model // LANES, LANES),
        pltpu.with_memory_space_constraint(jnp.transpose(qkv_weight, (1, 0, 2)), pltpu.HBM),
        out_weight,
    )

    mine, keep, *sent = pl.pallas_call(
        attend_kernel,
        out_shape=(
            array((share, channels), bf16),
            array((share, model), f32),
            *[array((share, model), bf16)] * (group - 1),
        ),
        in_specs=[VMEM] * 12 + [HBM],
        out_specs=(VMEM,) * (1 + group),
        scratch_shapes=[
            pltpu.VMEM((cols - cols // 2, model), bf16),
            pltpu.SemaphoreType.DMA(()),
        ],
        compiler_params=pltpu.CompilerParams(vmem_limit_bytes=grant),
        name="attend",
    )(
        moved,
        *products,
        select,
        bias,
        first,
        out_weight,
    )
    small = pltpu.CompilerParams(vmem_limit_bytes=8 * MIB)
    places = [(along, across) for along in range(mps) for across in range(roles)][1:]
    routed = list(zip(places, sent))
    routed.sort(key=lambda item: item[0][0] == 0)
    received = [to_member(block, *place) for place, block in routed]
    residual = pl.pallas_call(
        residual_kernel,
        out_shape=array((share, model), f32),
        in_specs=[VMEM] * 3,
        out_specs=VMEM,
        compiler_params=small,
        cost_estimate=pl.CostEstimate(
            flops=2 * share * channels * model,
            bytes_accessed=2 * channels * model,
            transcendentals=0,
        ),
        name="residual",
    )(mine, embed_weight, pos_mine)
    return pl.pallas_call(
        sum_kernel,
        out_shape=array((share, model), bf16),
        in_specs=[VMEM] * (1 + group),
        out_specs=VMEM,
        compiler_params=small,
        name="final_sum",
    )(residual, keep, *received)


def solution(mesh):
    in_specs = (
        P("seq", None, ("mp", "role")),
        P(("mp", "role"), None),
        P(),
        P(),
        P(),
        P(),
        P(),
        P(None, None, ("mp", "role")),
        P(("mp", "role"), None),
    )
    out_specs = P(("seq", "mp", "role"), None)
    return jax.shard_map(
        on_device, mesh=mesh, in_specs=in_specs, out_specs=out_specs, check_vma=False
    )
```

```python
import functools

import jax
import jax.numpy as jnp
from jax import lax
from jax.experimental import pallas as pl
from jax.experimental.pallas import tpu as pltpu
from jax.sharding import PartitionSpec as P

HS = 128
MOSTB = 4
REACH = MOSTB - 1
GROUP = ("mp", "role")
SCATTERED = ("role", "mp", "seq")
LANES = 128
STEP_ROWS = 256
DEPTH = 1024
AHEAD = 9
STRIP = 512
MIB = 1024 * 1024
VMEM = pl.BlockSpec(memory_space=pltpu.VMEM)
SMEM = pl.BlockSpec(memory_space=pltpu.SMEM)
HBM = pl.BlockSpec(memory_space=pltpu.HBM)


def dot(a, b):
    return jnp.dot(a, b, preferred_element_type=jnp.float32)


def latent_kernel(
    frame_dev,
    hidden_hbm,
    weight_hbm,
    out_hbm,
    hidden_ref,
    weight_ref,
    padded_ref,
    out_ref,
    in_sems,
    out_sems,
):
    slots, frames, depth = hidden_ref.shape
    everyone, _, window, channels = out_ref.shape
    seqs = frames // frame_dev
    arrivals = [pltpu.make_async_copy(hidden_hbm, hidden_ref, in_sems.at[0])]
    for index, at in enumerate(range(0, depth, LANES)):
        piece = pl.ds(at, LANES)
        arrivals.append(
            pltpu.make_async_copy(
                weight_hbm.at[piece], weight_ref.at[piece], in_sems.at[index + 1]
            )
        )
    for copy in arrivals:
        copy.start()
    padded_ref[...] = jnp.zeros_like(padded_ref)
    for copy in arrivals:
        copy.wait()
    for slot in range(slots):
        padded_ref[slot, REACH : REACH + frames] = dot(hidden_ref[slot], weight_ref[...])
    pieces = [
        padded_ref[:, to * frame_dev : to * frame_dev + window].astype(out_ref.dtype)
        for to in range(seqs)
    ]
    leaving = []
    for index, first in enumerate(range(0, everyone, seqs)):
        for to in range(seqs):
            out_ref[first + to] = pieces[to]
        part = pl.ds(first, seqs)
        leaving.append(
            pltpu.make_async_copy(out_ref.at[part], out_hbm.at[part], out_sems.at[index])
        )
        leaving[-1].start()
    for copy in leaving:
        copy.wait()


def weights_kernel(
    frame_dev,
    window,
    order_ref,
    block_ref,
    embed_ref,
    pos_ref,
    gain_ref,
    weight_hbm,
    out_weight_hbm,
    scaled_ref,
    offset_ref,
    gram_ref,
    cross_ref,
    level_ref,
    natural_cross_ref,
    natural_level_ref,
    pos_mine_ref,
    select_ref,
    select_mine_ref,
    bias_ref,
    first_ref,
    natural_ref,
    pos_all_ref,
    weight_ref,
    sems,
    first_sem,
):
    channels, model = embed_ref.shape
    patches = pos_ref.shape[0]
    frames = block_ref.shape[0]
    own_rows, rows = bias_ref.shape
    share = select_mine_ref.shape[0]
    device = lax.axis_index("seq")
    member = lax.axis_index(GROUP)

    deep = min(model, DEPTH)
    parts = [(index, at) for index in range(3) for at in range(0, model, deep)]

    def arrival(part):
        index, at = parts[part]
        place = (index, pl.ds(at, deep))
        return pltpu.make_async_copy(weight_hbm.at[place], weight_ref.at[place], sems.at[part])

    first = pltpu.make_async_copy(
        out_weight_hbm.at[pl.ds(0, first_ref.shape[0])], first_ref, first_sem
    )
    for part in range(min(AHEAD, len(parts))):
        arrival(part).start()
    first.start()

    pos = pos_ref[...].astype(jnp.float32)
    pos_all_ref[...] = pos

    column = lax.broadcasted_iota(jnp.int32, (1, rows), 1)
    column_slot, column_frame = column // window, column % window

    def patch_at(slot, found):
        return jnp.where(column_slot == slot, order_ref[slot], found)

    column_patch = jnp.zeros((1, rows), jnp.int32)
    if patches <= 16:
        for slot in range(patches):
            column_patch = patch_at(slot, column_patch)
    else:
        column_patch = lax.fori_loop(0, patches, patch_at, column_patch)

    def select(count, first):
        row = lax.broadcasted_iota(jnp.int32, (count, rows), 0) + first
        hit = jnp.logical_and(
            column_patch == row % patches, column_frame == row // patches + REACH
        )
        return jnp.where(hit, 1.0, 0.0).astype(jnp.bfloat16)

    select_ref[...] = select(own_rows, 0)
    select_mine_ref[...] = select(share, member * share)
    for frame in range(frame_dev * patches // share):
        row = frame * share

        @pl.when(member == frame)
        def _():
            for at in range(share):
                mine = (row + at) % patches
                pos_mine_ref[at : at + 1, :] = pos_all_ref[mine : mine + 1, :]

    def block_of(frame):
        inside = jnp.logical_and(frame >= 0, frame < frames)
        return jnp.where(inside, block_ref[jnp.clip(frame, 0, frames - 1)], -1)

    column_block = jnp.full((1, rows), -1, jnp.int32)
    for frame in range(window):
        found = block_of(device * frame_dev - REACH + frame)
        column_block = jnp.where(column_frame == frame, found, column_block)
    row_frame = lax.broadcasted_iota(jnp.int32, (own_rows, rows), 0) // patches
    row_block = jnp.full((own_rows, rows), -2, jnp.int32)
    for frame in range(frame_dev):
        row_block = jnp.where(row_frame == frame, block_of(device * frame_dev + frame), row_block)
    bias_ref[...] = jnp.where(row_block == column_block, 0.0, -1e30)

    gain = jnp.concatenate(
        [gain_ref[at : at + 1, :].astype(jnp.float32) for at in range(model // LANES)], axis=1
    )
    left = jnp.concatenate([embed_ref[...].astype(jnp.float32) * gain, pos * gain], axis=0)
    left = left.astype(jnp.bfloat16)
    def keep(ref, scaled):
        high = scaled.astype(jnp.bfloat16)
        ref[:channels] = high
        ref[channels:] = (scaled - high.astype(jnp.float32)).astype(jnp.bfloat16)

    plain = jnp.concatenate([embed_ref[...], pos_ref[...]], axis=0)
    both = lax.dot_general(
        plain, embed_ref[...], (((1,), (1,)), ((), ())), preferred_element_type=jnp.float32
    )
    keep(gram_ref, both[:channels])
    natural_cross_ref[...] = 2.0 * both[channels:]
    level = jnp.sum(pos * pos, axis=-1, keepdims=True) / channels
    natural_level_ref[...] = jnp.broadcast_to(level, (patches, channels))

    for part, (index, at) in enumerate(parts):
        arrival(part).wait()
        if part + AHEAD < len(parts):
            arrival(part + AHEAD).start()
        here = slice(at, at + deep)
        product = dot(left[:, here], weight_ref[index, here])
        both = product if at == 0 else both + product
        if at + deep == model:
            keep(scaled_ref.at[index], both[:channels])
            natural_ref[index] = both[channels:]

    offset_ref[0] = natural_ref[0]

    def place(slot):
        to, at = pl.ds(slot, 1), pl.ds(order_ref[slot], 1)
        cross_ref[to, :] = natural_cross_ref[at, :]
        level_ref[to, :] = natural_level_ref[at, :]
        for index in range(1, 3):
            offset_ref[index, to, :] = natural_ref[index, at, :]

    if patches <= 16:
        for slot in range(patches):
            place(slot)
    else:
        pl.loop(0, patches)(place)
    first.wait()


def attend_kernel(
    roles,
    partial_ref,
    scaled_ref,
    offset_ref,
    gram_ref,
    cross_ref,
    level_ref,
    natural_cross_ref,
    natural_level_ref,
    select_ref,
    select_mine_ref,
    bias_ref,
    first_ref,
    out_weight_hbm,
    mine_ref,
    keep_ref,
    *rest,
):
    *send_refs, second_ref, sem = rest
    half = first_ref.shape[0]
    arrival = pltpu.make_async_copy(out_weight_hbm.at[pl.ds(half, half)], second_ref, sem)
    arrival.start()
    everyone, slots, window, channels = partial_ref.shape
    share, model = keep_ref.shape
    group = 1 + len(send_refs)
    mps = group // roles
    seqs = everyone // group
    patches = seqs * slots
    rows = patches * window
    cols = out_weight_hbm.shape[0]

    total = partial_ref[:seqs].astype(jnp.float32)
    for other in range(1, group):
        total = total + partial_ref[other * seqs : (other + 1) * seqs].astype(jnp.float32)
    latents = total.reshape(rows, channels).astype(jnp.bfloat16)
    own = dot(select_ref[...], latents).astype(jnp.bfloat16)

    def apply(part, table):
        return dot(jnp.concatenate([part, part], axis=1), table)

    def by_row(table):
        wide = jnp.broadcast_to(table[:, None], (patches, window, table.shape[1]))
        return wide.reshape(rows, table.shape[1])

    def by_patch(table):
        return jnp.concatenate([table] * (group * share // patches), axis=0)

    def scale_of(part, cross, level):
        slope = apply(part, gram_ref[...]) + cross
        squares = slope * part.astype(jnp.float32) + level
        mean = jnp.maximum(jnp.sum(squares, axis=-1, keepdims=True), 0.0) / model
        return lax.rsqrt(mean + 1e-06)

    scale = scale_of(latents, by_row(cross_ref[...]), by_row(level_ref[...]))
    own_scale = scale_of(own, by_patch(natural_cross_ref[...]), by_patch(natural_level_ref[...]))
    own_scale = own_scale * (HS**-0.5)

    def project(index):
        flat = apply(latents, scaled_ref[index]) + by_row(offset_ref[index])
        return (flat * scale).astype(jnp.bfloat16)

    query = (apply(own, scaled_ref[0]) + by_patch(offset_ref[0])).astype(jnp.bfloat16)
    key, value = project(1), project(2)
    bias = bias_ref[...]
    heads = []
    for head in range(cols // HS):
        at = slice(head * HS, (head + 1) * HS)
        scores = lax.dot_general(
            query[:, at], key[:, at], (((1,), (1,)), ((), ())), preferred_element_type=jnp.float32
        )
        scores = scores * own_scale + bias
        expo = jnp.exp(scores - jnp.max(scores, axis=-1, keepdims=True))
        probs = (expo / jnp.sum(expo, axis=-1, keepdims=True)).astype(jnp.bfloat16)
        heads.append(dot(probs, value[:, at]).astype(jnp.bfloat16))
    mine_ref[...] = dot(select_mine_ref[...], latents).astype(jnp.bfloat16)
    heads = jnp.concatenate(heads, axis=1)
    arrival.wait()
    mp, role = lax.axis_index("mp"), lax.axis_index("role")
    members = [
        ((mp + along) % mps) * roles + (role + across) % roles
        for along in range(mps)
        for across in range(roles)
    ]
    for at in range(0, model, STRIP):
        here = slice(at, at + STRIP)
        mixed = dot(heads[:, :half], first_ref[:, here]) + dot(heads[:, half:], second_ref[:, here])
        parts = [mixed[index * share : (index + 1) * share] for index in range(group)]

        def of_member(member):
            found = parts[0]
            for index in range(1, group):
                found = jnp.where(member == index, parts[index], found)
            return found

        keep_ref[:, here] = of_member(members[0])
        for member, send_ref in zip(members[1:], send_refs):
            send_ref[:, here] = of_member(member).astype(jnp.bfloat16)


def residual_kernel(mine_ref, embed_ref, pos_ref, out_ref):
    out_ref[...] = dot(mine_ref[...], embed_ref[...]) + pos_ref[...]


def sum_kernel(residual_ref, keep_ref, *refs):
    *others, out_ref = refs
    total = residual_ref[...] + keep_ref[...]
    for other in others:
        total = total + other[...].astype(jnp.float32)
    out_ref[...] = total.astype(jnp.bfloat16)


def to_member(block, along, across):
    mps, roles = lax.axis_size("mp"), lax.axis_size("role")
    route = [
        (mp * roles + role, ((mp + along) % mps) * roles + (role + across) % roles)
        for mp in range(mps)
        for role in range(roles)
    ]
    return lax.ppermute(block, GROUP, route)


def on_device(
    gen_hidden,
    gen_out_weight,
    patch_order,
    frame_block,
    embed_weight,
    pos_table,
    norm_gain,
    qkv_weight,
    out_weight,
):
    slots, frames, depth = gen_hidden.shape
    channels, model = embed_weight.shape
    cols = qkv_weight.shape[2]
    out_weight = pltpu.with_memory_space_constraint(out_weight, pltpu.HBM)
    seqs = lax.axis_size("seq")
    group = lax.axis_size(GROUP)
    mps, roles = lax.axis_size("mp"), lax.axis_size("role")
    patches = seqs * slots
    frame_dev = frames // seqs
    window = frame_dev + 2 * REACH
    rows = window * patches
    own_rows = frame_dev * patches
    share = own_rows // group
    f32, bf16 = jnp.float32, jnp.bfloat16
    array = jax.ShapeDtypeStruct
    grant = (16 if rows <= STEP_ROWS else 40) * MIB

    windows = pl.pallas_call(
        functools.partial(latent_kernel, frame_dev),
        out_shape=array((group * seqs, slots, window, channels), bf16),
        in_specs=[HBM] * 2,
        out_specs=HBM,
        scratch_shapes=[
            pltpu.VMEM((slots, frames, depth), bf16),
            pltpu.VMEM((depth, channels), bf16),
            pltpu.VMEM((slots, frames + 2 * REACH, channels), f32),
            pltpu.VMEM((group * seqs, slots, window, channels), bf16),
            pltpu.SemaphoreType.DMA((1 + depth // LANES,)),
            pltpu.SemaphoreType.DMA((group,)),
        ],
        compiler_params=pltpu.CompilerParams(vmem_limit_bytes=12 * MIB),
        cost_estimate=pl.CostEstimate(
            flops=20_000_000_000, bytes_accessed=40_000_000, transcendentals=0
        ),
        name="partial_latents",
    )(
        pltpu.with_memory_space_constraint(gen_hidden, pltpu.HBM),
        pltpu.with_memory_space_constraint(gen_out_weight, pltpu.HBM),
    )
    moved = lax.all_to_all(
        windows,
        SCATTERED,
        split_axis=0,
        concat_axis=0,
        tiled=True,
    )

    *products, pos_mine, select, select_mine, bias, first = pl.pallas_call(
        functools.partial(weights_kernel, frame_dev, window),
        out_shape=(
            array((3, 2 * channels, cols), bf16),
            array((3, patches, cols), f32),
            array((2 * channels, channels), bf16),
            array((patches, channels), f32),
            array((patches, channels), f32),
            array((patches, channels), f32),
            array((patches, channels), f32),
            array((share, model), f32),
            array((own_rows, rows), bf16),
            array((share, rows), bf16),
            array((own_rows, rows), f32),
            array((cols // 2, model), bf16),
        ),
        in_specs=[SMEM] * 2 + [VMEM] * 3 + [HBM] * 2,
        out_specs=(VMEM,) * 12,
        scratch_shapes=[
            pltpu.VMEM((3, patches, cols), f32),
            pltpu.VMEM((patches, model), f32),
            pltpu.VMEM((3, model, cols), bf16),
            pltpu.SemaphoreType.DMA((3 * (model // min(model, DEPTH)),)),
            pltpu.SemaphoreType.DMA(()),
        ],
        compiler_params=pltpu.CompilerParams(vmem_limit_bytes=24 * MIB),
        cost_estimate=pl.CostEstimate(
            flops=2 * (channels + patches) * model * 3 * cols,
            bytes_accessed=2 * model * 3 * cols,
            transcendentals=0,
        ),
        name="weight_products",
    )(
        patch_order,
        frame_block,
        embed_weight,
        pos_table,
        norm_gain.reshape(model // LANES, LANES),
        pltpu.with_memory_space_constraint(jnp.transpose(qkv_weight, (1, 0, 2)), pltpu.HBM),
        out_weight,
    )

    mine, keep, *sent = pl.pallas_call(
        functools.partial(attend_kernel, roles),
        out_shape=(
            array((share, channels), bf16),
            array((share, model), f32),
            *[array((share, model), bf16)] * (group - 1),
        ),
        in_specs=[VMEM] * 12 + [HBM],
        out_specs=(VMEM,) * (1 + group),
        scratch_shapes=[
            pltpu.VMEM((cols - cols // 2, model), bf16),
            pltpu.SemaphoreType.DMA(()),
        ],
        compiler_params=pltpu.CompilerParams(vmem_limit_bytes=grant),
        name="attend",
    )(
        moved,
        *products,
        select,
        select_mine,
        bias,
        first,
        out_weight,
    )
    small = pltpu.CompilerParams(vmem_limit_bytes=8 * MIB)
    places = [(along, across) for along in range(mps) for across in range(roles)][1:]
    routed = list(zip(places, sent))
    routed.sort(key=lambda item: item[0][0] == 0)
    received = [to_member(block, *place) for place, block in routed]
    residual = pl.pallas_call(
        residual_kernel,
        out_shape=array((share, model), f32),
        in_specs=[VMEM] * 3,
        out_specs=VMEM,
        compiler_params=small,
        cost_estimate=pl.CostEstimate(
            flops=2 * share * channels * model,
            bytes_accessed=2 * channels * model,
            transcendentals=0,
        ),
        name="residual",
    )(mine, embed_weight, pos_mine)
    return pl.pallas_call(
        sum_kernel,
        out_shape=array((share, model), bf16),
        in_specs=[VMEM] * (1 + group),
        out_specs=VMEM,
        compiler_params=small,
        name="final_sum",
    )(residual, keep, *received)


def solution(mesh):
    in_specs = (
        P("seq", None, ("mp", "role")),
        P(("mp", "role"), None),
        P(),
        P(),
        P(),
        P(),
        P(),
        P(None, None, ("mp", "role")),
        P(("mp", "role"), None),
    )
    out_specs = P(("seq", "mp", "role"), None)
    return jax.shard_map(
        on_device, mesh=mesh, in_specs=in_specs, out_specs=out_specs, check_vma=False
    )
```

```python
import functools

import jax
import jax.numpy as jnp
from jax import lax
from jax.experimental import pallas as pl
from jax.experimental.pallas import tpu as pltpu
from jax.sharding import PartitionSpec as P

HS = 128
MOSTB = 4
REACH = MOSTB - 1
GROUP = ("mp", "role")
SCATTERED = ("role", "mp", "seq")
LANES = 128
STEP_ROWS = 256
DEPTH = 1024
AHEAD = 9
STRIP = 512
MIB = 1024 * 1024
VMEM = pl.BlockSpec(memory_space=pltpu.VMEM)
SMEM = pl.BlockSpec(memory_space=pltpu.SMEM)
HBM = pl.BlockSpec(memory_space=pltpu.HBM)


def dot(a, b):
    return jnp.dot(a, b, preferred_element_type=jnp.float32)


def latent_kernel(
    frame_dev,
    hidden_hbm,
    weight_hbm,
    out_hbm,
    hidden_ref,
    weight_ref,
    padded_ref,
    out_ref,
    in_sems,
    out_sems,
):
    slots, frames, depth = hidden_ref.shape
    everyone, _, window, channels = out_ref.shape
    seqs = frames // frame_dev
    arrivals = [pltpu.make_async_copy(hidden_hbm, hidden_ref, in_sems.at[0])]
    for index, at in enumerate(range(0, depth, LANES)):
        piece = pl.ds(at, LANES)
        arrivals.append(
            pltpu.make_async_copy(
                weight_hbm.at[piece], weight_ref.at[piece], in_sems.at[index + 1]
            )
        )
    for copy in arrivals:
        copy.start()
    padded_ref[...] = jnp.zeros_like(padded_ref)
    for copy in arrivals:
        copy.wait()
    for slot in range(slots):
        padded_ref[slot, REACH : REACH + frames] = dot(hidden_ref[slot], weight_ref[...])
    pieces = [
        padded_ref[:, to * frame_dev : to * frame_dev + window].astype(out_ref.dtype)
        for to in range(seqs)
    ]
    leaving = []
    for index, first in enumerate(range(0, everyone, seqs)):
        for to in range(seqs):
            out_ref[first + to] = pieces[to]
        part = pl.ds(first, seqs)
        leaving.append(
            pltpu.make_async_copy(out_ref.at[part], out_hbm.at[part], out_sems.at[index])
        )
        leaving[-1].start()
    for copy in leaving:
        copy.wait()


def weights_kernel(
    frame_dev,
    window,
    order_ref,
    block_ref,
    embed_ref,
    pos_ref,
    gain_ref,
    weight_hbm,
    out_weight_hbm,
    scaled_ref,
    offset_ref,
    gram_ref,
    cross_ref,
    level_ref,
    natural_cross_ref,
    natural_level_ref,
    pos_mine_ref,
    select_ref,
    select_mine_ref,
    bias_ref,
    first_ref,
    natural_ref,
    pos_all_ref,
    weight_ref,
    sems,
    first_sem,
):
    channels, model = embed_ref.shape
    patches = pos_ref.shape[0]
    frames = block_ref.shape[0]
    own_rows, rows = bias_ref.shape
    share = select_mine_ref.shape[0]
    device = lax.axis_index("seq")
    member = lax.axis_index(GROUP)

    deep = min(model, DEPTH)
    parts = [(index, at) for index in range(3) for at in range(0, model, deep)]

    def arrival(part):
        index, at = parts[part]
        place = (index, pl.ds(at, deep))
        return pltpu.make_async_copy(weight_hbm.at[place], weight_ref.at[place], sems.at[part])

    first = pltpu.make_async_copy(
        out_weight_hbm.at[pl.ds(0, first_ref.shape[0])], first_ref, first_sem
    )
    for part in range(min(AHEAD, len(parts))):
        arrival(part).start()
    first.start()

    pos = pos_ref[...].astype(jnp.float32)
    pos_all_ref[...] = pos

    column = lax.broadcasted_iota(jnp.int32, (1, rows), 1)
    column_slot, column_frame = column // window, column % window

    def patch_at(slot, found):
        return jnp.where(column_slot == slot, order_ref[slot], found)

    column_patch = jnp.zeros((1, rows), jnp.int32)
    if patches <= 16:
        for slot in range(patches):
            column_patch = patch_at(slot, column_patch)
    else:
        column_patch = lax.fori_loop(0, patches, patch_at, column_patch)

    def select(count, first):
        row = lax.broadcasted_iota(jnp.int32, (count, rows), 0) + first
        hit = jnp.logical_and(
            column_patch == row % patches, column_frame == row // patches + REACH
        )
        return jnp.where(hit, 1.0, 0.0).astype(jnp.bfloat16)

    select_ref[...] = select(own_rows, 0)
    select_mine_ref[...] = select(share, member * share)
    for frame in range(frame_dev * patches // share):
        row = frame * share

        @pl.when(member == frame)
        def _():
            for at in range(share):
                mine = (row + at) % patches
                pos_mine_ref[at : at + 1, :] = pos_all_ref[mine : mine + 1, :]

    def block_of(frame):
        inside = jnp.logical_and(frame >= 0, frame < frames)
        return jnp.where(inside, block_ref[jnp.clip(frame, 0, frames - 1)], -1)

    column_block = jnp.full((1, rows), -1, jnp.int32)
    for frame in range(window):
        found = block_of(device * frame_dev - REACH + frame)
        column_block = jnp.where(column_frame == frame, found, column_block)
    row_frame = lax.broadcasted_iota(jnp.int32, (own_rows, rows), 0) // patches
    row_block = jnp.full((own_rows, rows), -2, jnp.int32)
    for frame in range(frame_dev):
        row_block = jnp.where(row_frame == frame, block_of(device * frame_dev + frame), row_block)
    bias_ref[...] = jnp.where(row_block == column_block, 0.0, -1e30)

    gain = jnp.concatenate(
        [gain_ref[at : at + 1, :].astype(jnp.float32) for at in range(model // LANES)], axis=1
    )
    left = jnp.concatenate([embed_ref[...].astype(jnp.float32) * gain, pos * gain], axis=0)
    left = left.astype(jnp.bfloat16)
    def keep(ref, scaled):
        high = scaled.astype(jnp.bfloat16)
        ref[:channels] = high
        ref[channels:] = (scaled - high.astype(jnp.float32)).astype(jnp.bfloat16)

    plain = jnp.concatenate([embed_ref[...], pos_ref[...]], axis=0)
    both = lax.dot_general(
        plain, embed_ref[...], (((1,), (1,)), ((), ())), preferred_element_type=jnp.float32
    )
    keep(gram_ref, both[:channels])
    natural_cross_ref[...] = 2.0 * both[channels:]
    level = jnp.sum(pos * pos, axis=-1, keepdims=True) / channels
    natural_level_ref[...] = jnp.broadcast_to(level, (patches, channels))

    for part, (index, at) in enumerate(parts):
        arrival(part).wait()
        if part + AHEAD < len(parts):
            arrival(part + AHEAD).start()
        here = slice(at, at + deep)
        product = dot(left[:, here], weight_ref[index, here])
        both = product if at == 0 else both + product
        if at + deep == model:
            keep(scaled_ref.at[index], both[:channels])
            natural_ref[index] = both[channels:]

    offset_ref[0] = natural_ref[0]

    def place(slot):
        to, at = pl.ds(slot, 1), pl.ds(order_ref[slot], 1)
        cross_ref[to, :] = natural_cross_ref[at, :]
        level_ref[to, :] = natural_level_ref[at, :]
        for index in range(1, 3):
            offset_ref[index, to, :] = natural_ref[index, at, :]

    if patches <= 16:
        for slot in range(patches):
            place(slot)
    else:
        pl.loop(0, patches)(place)
    first.wait()


def attend_kernel(
    roles,
    partial_ref,
    scaled_ref,
    offset_ref,
    gram_ref,
    cross_ref,
    level_ref,
    natural_cross_ref,
    natural_level_ref,
    select_ref,
    select_mine_ref,
    bias_ref,
    first_ref,
    out_weight_hbm,
    mine_ref,
    keep_ref,
    *rest,
):
    *send_refs, second_ref, sem = rest
    half = first_ref.shape[0]
    arrival = pltpu.make_async_copy(out_weight_hbm.at[pl.ds(half, half)], second_ref, sem)
    arrival.start()
    everyone, slots, window, channels = partial_ref.shape
    share, model = keep_ref.shape
    group = 1 + len(send_refs)
    mps = group // roles
    seqs = everyone // group
    patches = seqs * slots
    rows = patches * window
    cols = out_weight_hbm.shape[0]

    total = partial_ref[:seqs].astype(jnp.float32)
    for other in range(1, group):
        total = total + partial_ref[other * seqs : (other + 1) * seqs].astype(jnp.float32)
    latents = total.reshape(rows, channels).astype(jnp.bfloat16)
    own = dot(select_ref[...], latents).astype(jnp.bfloat16)

    def apply(part, table):
        return dot(jnp.concatenate([part, part], axis=1), table)

    def by_row(table):
        wide = jnp.broadcast_to(table[:, None], (patches, window, table.shape[1]))
        return wide.reshape(rows, table.shape[1])

    def by_patch(table):
        return jnp.concatenate([table] * (group * share // patches), axis=0)

    def scale_of(part, cross, level):
        slope = apply(part, gram_ref[...]) + cross
        squares = slope * part.astype(jnp.float32) + level
        mean = jnp.maximum(jnp.sum(squares, axis=-1, keepdims=True), 0.0) / model
        return lax.rsqrt(mean + 1e-06)

    scale = scale_of(latents, by_row(cross_ref[...]), by_row(level_ref[...]))
    own_scale = scale_of(own, by_patch(natural_cross_ref[...]), by_patch(natural_level_ref[...]))
    own_scale = own_scale * (HS**-0.5)

    def project(index):
        flat = apply(latents, scaled_ref[index]) + by_row(offset_ref[index])
        return (flat * scale).astype(jnp.bfloat16)

    query = (apply(own, scaled_ref[0]) + by_patch(offset_ref[0])).astype(jnp.bfloat16)
    key, value = project(1), project(2)
    bias = bias_ref[...]
    heads = []
    for head in range(cols // HS):
        at = slice(head * HS, (head + 1) * HS)
        scores = lax.dot_general(
            query[:, at], key[:, at], (((1,), (1,)), ((), ())), preferred_element_type=jnp.float32
        )
        scores = scores * own_scale + bias
        expo = jnp.exp(scores - jnp.max(scores, axis=-1, keepdims=True))
        probs = (expo / jnp.sum(expo, axis=-1, keepdims=True)).astype(jnp.bfloat16)
        heads.append(dot(probs, value[:, at]).astype(jnp.bfloat16))
    mine_ref[...] = dot(select_mine_ref[...], latents).astype(jnp.bfloat16)
    heads = jnp.concatenate(heads, axis=1)
    arrival.wait()
    mp, role = lax.axis_index("mp"), lax.axis_index("role")
    members = [
        ((mp + along) % mps) * roles + (role + across) % roles
        for along in range(mps)
        for across in range(roles)
    ]
    for at in range(0, model, STRIP):
        here = slice(at, at + STRIP)
        mixed = dot(heads[:, :half], first_ref[:, here]) + dot(heads[:, half:], second_ref[:, here])
        parts = [mixed[index * share : (index + 1) * share] for index in range(group)]

        def of_member(member):
            found = parts[0]
            for index in range(1, group):
                found = jnp.where(member == index, parts[index], found)
            return found

        keep_ref[:, here] = of_member(members[0])
        for member, send_ref in zip(members[1:], send_refs):
            send_ref[:, here] = of_member(member).astype(jnp.bfloat16)


def residual_kernel(mine_ref, embed_ref, pos_ref, out_ref):
    out_ref[...] = dot(mine_ref[...], embed_ref[...]) + pos_ref[...]


def sum_kernel(residual_ref, keep_ref, *refs):
    *others, out_ref = refs
    total = residual_ref[...] + keep_ref[...]
    for other in others:
        total = total + other[...].astype(jnp.float32)
    out_ref[...] = total.astype(jnp.bfloat16)


def to_member(block, along, across):
    mps, roles = lax.axis_size("mp"), lax.axis_size("role")
    route = [
        (mp * roles + role, ((mp + along) % mps) * roles + (role + across) % roles)
        for mp in range(mps)
        for role in range(roles)
    ]
    return lax.ppermute(block, GROUP, route)


def on_device(
    gen_hidden,
    gen_out_weight,
    patch_order,
    frame_block,
    embed_weight,
    pos_table,
    norm_gain,
    qkv_weight,
    out_weight,
):
    slots, frames, depth = gen_hidden.shape
    channels, model = embed_weight.shape
    cols = qkv_weight.shape[2]
    out_weight = pltpu.with_memory_space_constraint(out_weight, pltpu.HBM)
    seqs = lax.axis_size("seq")
    group = lax.axis_size(GROUP)
    mps, roles = lax.axis_size("mp"), lax.axis_size("role")
    patches = seqs * slots
    frame_dev = frames // seqs
    window = frame_dev + 2 * REACH
    rows = window * patches
    own_rows = frame_dev * patches
    share = own_rows // group
    f32, bf16 = jnp.float32, jnp.bfloat16
    array = jax.ShapeDtypeStruct
    grant = (16 if rows <= STEP_ROWS else 40) * MIB

    windows = pl.pallas_call(
        functools.partial(latent_kernel, frame_dev),
        out_shape=array((group * seqs, slots, window, channels), bf16),
        in_specs=[HBM] * 2,
        out_specs=HBM,
        scratch_shapes=[
            pltpu.VMEM((slots, frames, depth), bf16),
            pltpu.VMEM((depth, channels), bf16),
            pltpu.VMEM((slots, frames + 2 * REACH, channels), f32),
            pltpu.VMEM((group * seqs, slots, window, channels), bf16),
            pltpu.SemaphoreType.DMA((1 + depth // LANES,)),
            pltpu.SemaphoreType.DMA((group,)),
        ],
        compiler_params=pltpu.CompilerParams(vmem_limit_bytes=12 * MIB),
        cost_estimate=pl.CostEstimate(
            flops=20_000_000_000, bytes_accessed=40_000_000, transcendentals=0
        ),
        name="partial_latents",
    )(
        pltpu.with_memory_space_constraint(gen_hidden, pltpu.HBM),
        pltpu.with_memory_space_constraint(gen_out_weight, pltpu.HBM),
    )
    moved = lax.all_to_all(
        windows,
        SCATTERED,
        split_axis=0,
        concat_axis=0,
        tiled=True,
    )

    *products, pos_mine, select, select_mine, bias, first = pl.pallas_call(
        functools.partial(weights_kernel, frame_dev, window),
        out_shape=(
            array((3, 2 * channels, cols), bf16),
            array((3, patches, cols), f32),
            array((2 * channels, channels), bf16),
            array((patches, channels), f32),
            array((patches, channels), f32),
            array((patches, channels), f32),
            array((patches, channels), f32),
            array((share, model), f32),
            array((own_rows, rows), bf16),
            array((share, rows), bf16),
            array((own_rows, rows), f32),
            array((cols // 2, model), bf16),
        ),
        in_specs=[SMEM] * 2 + [VMEM] * 3 + [HBM] * 2,
        out_specs=(VMEM,) * 12,
        scratch_shapes=[
            pltpu.VMEM((3, patches, cols), f32),
            pltpu.VMEM((patches, model), f32),
            pltpu.VMEM((3, model, cols), bf16),
            pltpu.SemaphoreType.DMA((3 * (model // min(model, DEPTH)),)),
            pltpu.SemaphoreType.DMA(()),
        ],
        compiler_params=pltpu.CompilerParams(vmem_limit_bytes=24 * MIB),
        cost_estimate=pl.CostEstimate(
            flops=2 * (channels + patches) * model * 3 * cols,
            bytes_accessed=2 * model * 3 * cols,
            transcendentals=0,
        ),
        name="weight_products",
    )(
        patch_order,
        frame_block,
        embed_weight,
        pos_table,
        norm_gain.reshape(model // LANES, LANES),
        pltpu.with_memory_space_constraint(jnp.transpose(qkv_weight, (1, 0, 2)), pltpu.HBM),
        out_weight,
    )

    mine, keep, *sent = pl.pallas_call(
        functools.partial(attend_kernel, roles),
        out_shape=(
            array((share, channels), bf16),
            array((share, model), f32),
            *[array((share, model), bf16)] * (group - 1),
        ),
        in_specs=[VMEM] * 12 + [HBM],
        out_specs=(VMEM,) * (1 + group),
        scratch_shapes=[
            pltpu.VMEM((cols - cols // 2, model), bf16),
            pltpu.SemaphoreType.DMA(()),
        ],
        compiler_params=pltpu.CompilerParams(vmem_limit_bytes=grant),
        name="attend",
    )(
        moved,
        *products,
        select,
        select_mine,
        bias,
        first,
        out_weight,
    )
    small = pltpu.CompilerParams(vmem_limit_bytes=8 * MIB)
    places = [(along, across) for along in range(mps) for across in range(roles)][1:]
    received = [to_member(block, *place) for place, block in zip(places, sent)]
    residual = pl.pallas_call(
        residual_kernel,
        out_shape=array((share, model), f32),
        in_specs=[VMEM] * 3,
        out_specs=VMEM,
        compiler_params=small,
        cost_estimate=pl.CostEstimate(
            flops=2 * share * channels * model,
            bytes_accessed=2 * channels * model,
            transcendentals=0,
        ),
        name="residual",
    )(mine, embed_weight, pos_mine)
    return pl.pallas_call(
        sum_kernel,
        out_shape=array((share, model), bf16),
        in_specs=[VMEM] * (1 + group),
        out_specs=VMEM,
        compiler_params=small,
        name="final_sum",
    )(residual, keep, *received)


def solution(mesh):
    in_specs = (
        P("seq", None, ("mp", "role")),
        P(("mp", "role"), None),
        P(),
        P(),
        P(),
        P(),
        P(),
        P(None, None, ("mp", "role")),
        P(("mp", "role"), None),
    )
    out_specs = P(("seq", "mp", "role"), None)
    return jax.shard_map(
        on_device, mesh=mesh, in_specs=in_specs, out_specs=out_specs, check_vma=False
    )
```

```python
import functools

import jax
import jax.numpy as jnp
from jax import lax
from jax.experimental import pallas as pl
from jax.experimental.pallas import tpu as pltpu
from jax.sharding import PartitionSpec as P

HS = 128
MOSTB = 4
REACH = MOSTB - 1
GROUP = ("mp", "role")
SCATTERED = ("role", "mp", "seq")
LANES = 128
STEP_ROWS = 256
DEPTH = 1024
AHEAD = 9
STRIP = 512
MIB = 1024 * 1024
VMEM = pl.BlockSpec(memory_space=pltpu.VMEM)
SMEM = pl.BlockSpec(memory_space=pltpu.SMEM)
HBM = pl.BlockSpec(memory_space=pltpu.HBM)


def dot(a, b):
    return jnp.dot(a, b, preferred_element_type=jnp.float32)


def latent_kernel(
    frame_dev,
    hidden_hbm,
    weight_hbm,
    out_hbm,
    hidden_ref,
    weight_ref,
    padded_ref,
    out_ref,
    in_sems,
    out_sems,
):
    slots, frames, depth = hidden_ref.shape
    everyone, _, window, channels = out_ref.shape
    seqs = frames // frame_dev
    hidden = pltpu.make_async_copy(hidden_hbm, hidden_ref, in_sems.at[0])
    deep = depth // 3 if depth % (3 * LANES) == 0 else depth
    arrivals = []
    for index, at in enumerate(range(0, depth, deep)):
        piece = pl.ds(at, deep)
        arrivals.append(
            pltpu.make_async_copy(
                weight_hbm.at[piece], weight_ref.at[piece], in_sems.at[index + 1]
            )
        )
    hidden.start()
    for copy in arrivals:
        copy.start()
    padded_ref[...] = jnp.zeros_like(padded_ref)
    hidden.wait()
    partial = [jnp.zeros((frames, channels), jnp.float32)] * slots
    for index, copy in enumerate(arrivals):
        copy.wait()
        here = slice(index * deep, (index + 1) * deep)
        for slot in range(slots):
            partial[slot] = partial[slot] + dot(hidden_ref[slot, :, here], weight_ref[here])
    for slot in range(slots):
        padded_ref[slot, REACH : REACH + frames] = partial[slot]
    pieces = [
        padded_ref[:, to * frame_dev : to * frame_dev + window].astype(out_ref.dtype)
        for to in range(seqs)
    ]
    leaving = []
    for index, first in enumerate(range(0, everyone, seqs)):
        for to in range(seqs):
            out_ref[first + to] = pieces[to]
        part = pl.ds(first, seqs)
        leaving.append(
            pltpu.make_async_copy(out_ref.at[part], out_hbm.at[part], out_sems.at[index])
        )
        leaving[-1].start()
    for copy in leaving:
        copy.wait()


def weights_kernel(
    frame_dev,
    window,
    order_ref,
    block_ref,
    embed_ref,
    pos_ref,
    gain_ref,
    weight_hbm,
    out_weight_hbm,
    scaled_ref,
    offset_ref,
    gram_ref,
    cross_ref,
    level_ref,
    natural_cross_ref,
    natural_level_ref,
    pos_mine_ref,
    select_ref,
    select_mine_ref,
    bias_ref,
    first_ref,
    natural_ref,
    pos_all_ref,
    weight_ref,
    sems,
    first_sem,
):
    channels, model = embed_ref.shape
    patches = pos_ref.shape[0]
    frames = block_ref.shape[0]
    own_rows, rows = bias_ref.shape
    share = select_mine_ref.shape[0]
    device = lax.axis_index("seq")
    member = lax.axis_index(GROUP)

    deep = min(model, DEPTH)
    parts = [(index, at) for index in range(3) for at in range(0, model, deep)]

    def arrival(part):
        index, at = parts[part]
        place = (index, pl.ds(at, deep))
        return pltpu.make_async_copy(weight_hbm.at[place], weight_ref.at[place], sems.at[part])

    first = pltpu.make_async_copy(
        out_weight_hbm.at[pl.ds(0, first_ref.shape[0])], first_ref, first_sem
    )
    for part in range(min(AHEAD, len(parts))):
        arrival(part).start()
    first.start()

    pos = pos_ref[...].astype(jnp.float32)
    pos_all_ref[...] = pos

    column = lax.broadcasted_iota(jnp.int32, (1, rows), 1)
    column_slot, column_frame = column // window, column % window

    def patch_at(slot, found):
        return jnp.where(column_slot == slot, order_ref[slot], found)

    column_patch = jnp.zeros((1, rows), jnp.int32)
    if patches <= 16:
        for slot in range(patches):
            column_patch = patch_at(slot, column_patch)
    else:
        column_patch = lax.fori_loop(0, patches, patch_at, column_patch)

    def select(count, first):
        row = lax.broadcasted_iota(jnp.int32, (count, rows), 0) + first
        hit = jnp.logical_and(
            column_patch == row % patches, column_frame == row // patches + REACH
        )
        return jnp.where(hit, 1.0, 0.0).astype(jnp.bfloat16)

    select_ref[...] = select(own_rows, 0)
    select_mine_ref[...] = select(share, member * share)
    for frame in range(frame_dev * patches // share):
        row = frame * share

        @pl.when(member == frame)
        def _():
            for at in range(share):
                mine = (row + at) % patches
                pos_mine_ref[at : at + 1, :] = pos_all_ref[mine : mine + 1, :]

    def block_of(frame):
        inside = jnp.logical_and(frame >= 0, frame < frames)
        return jnp.where(inside, block_ref[jnp.clip(frame, 0, frames - 1)], -1)

    column_block = jnp.full((1, rows), -1, jnp.int32)
    for frame in range(window):
        found = block_of(device * frame_dev - REACH + frame)
        column_block = jnp.where(column_frame == frame, found, column_block)
    row_frame = lax.broadcasted_iota(jnp.int32, (own_rows, rows), 0) // patches
    row_block = jnp.full((own_rows, rows), -2, jnp.int32)
    for frame in range(frame_dev):
        row_block = jnp.where(row_frame == frame, block_of(device * frame_dev + frame), row_block)
    bias_ref[...] = jnp.where(row_block == column_block, 0.0, -1e30)

    gain = jnp.concatenate(
        [gain_ref[at : at + 1, :].astype(jnp.float32) for at in range(model // LANES)], axis=1
    )
    left = jnp.concatenate([embed_ref[...].astype(jnp.float32) * gain, pos * gain], axis=0)
    left = left.astype(jnp.bfloat16)
    def keep(ref, scaled):
        high = scaled.astype(jnp.bfloat16)
        ref[:channels] = high
        ref[channels:] = (scaled - high.astype(jnp.float32)).astype(jnp.bfloat16)

    plain = jnp.concatenate([embed_ref[...], pos_ref[...]], axis=0)
    both = lax.dot_general(
        plain, embed_ref[...], (((1,), (1,)), ((), ())), preferred_element_type=jnp.float32
    )
    keep(gram_ref, both[:channels])
    natural_cross_ref[...] = 2.0 * both[channels:]
    level = jnp.sum(pos * pos, axis=-1, keepdims=True) / channels
    natural_level_ref[...] = jnp.broadcast_to(level, (patches, channels))

    for part, (index, at) in enumerate(parts):
        arrival(part).wait()
        if part + AHEAD < len(parts):
            arrival(part + AHEAD).start()
        here = slice(at, at + deep)
        product = dot(left[:, here], weight_ref[index, here])
        both = product if at == 0 else both + product
        if at + deep == model:
            keep(scaled_ref.at[index], both[:channels])
            natural_ref[index] = both[channels:]

    offset_ref[0] = natural_ref[0]

    def place(slot):
        to, at = pl.ds(slot, 1), pl.ds(order_ref[slot], 1)
        cross_ref[to, :] = natural_cross_ref[at, :]
        level_ref[to, :] = natural_level_ref[at, :]
        for index in range(1, 3):
            offset_ref[index, to, :] = natural_ref[index, at, :]

    if patches <= 16:
        for slot in range(patches):
            place(slot)
    else:
        pl.loop(0, patches)(place)
    first.wait()


def attend_kernel(
    roles,
    partial_ref,
    scaled_ref,
    offset_ref,
    gram_ref,
    cross_ref,
    level_ref,
    natural_cross_ref,
    natural_level_ref,
    select_ref,
    select_mine_ref,
    bias_ref,
    first_ref,
    out_weight_hbm,
    mine_ref,
    keep_ref,
    *rest,
):
    *send_refs, second_ref, sem = rest
    half = first_ref.shape[0]
    arrival = pltpu.make_async_copy(out_weight_hbm.at[pl.ds(half, half)], second_ref, sem)
    arrival.start()
    everyone, slots, window, channels = partial_ref.shape
    share, model = keep_ref.shape
    group = 1 + len(send_refs)
    mps = group // roles
    seqs = everyone // group
    patches = seqs * slots
    rows = patches * window
    cols = out_weight_hbm.shape[0]

    total = partial_ref[:seqs].astype(jnp.float32)
    for other in range(1, group):
        total = total + partial_ref[other * seqs : (other + 1) * seqs].astype(jnp.float32)
    latents = total.reshape(rows, channels).astype(jnp.bfloat16)
    own = dot(select_ref[...], latents).astype(jnp.bfloat16)

    def apply(part, table):
        return dot(jnp.concatenate([part, part], axis=1), table)

    def by_row(table):
        wide = jnp.broadcast_to(table[:, None], (patches, window, table.shape[1]))
        return wide.reshape(rows, table.shape[1])

    def by_patch(table):
        return jnp.concatenate([table] * (group * share // patches), axis=0)

    def scale_of(part, cross, level):
        slope = apply(part, gram_ref[...]) + cross
        squares = slope * part.astype(jnp.float32) + level
        mean = jnp.maximum(jnp.sum(squares, axis=-1, keepdims=True), 0.0) / model
        return lax.rsqrt(mean + 1e-06)

    scale = scale_of(latents, by_row(cross_ref[...]), by_row(level_ref[...]))
    own_scale = scale_of(own, by_patch(natural_cross_ref[...]), by_patch(natural_level_ref[...]))
    own_scale = own_scale * (HS**-0.5)

    def project(index):
        flat = apply(latents, scaled_ref[index]) + by_row(offset_ref[index])
        return (flat * scale).astype(jnp.bfloat16)

    query = (apply(own, scaled_ref[0]) + by_patch(offset_ref[0])).astype(jnp.bfloat16)
    key, value = project(1), project(2)
    bias = bias_ref[...]
    heads = []
    for head in range(cols // HS):
        at = slice(head * HS, (head + 1) * HS)
        scores = lax.dot_general(
            query[:, at], key[:, at], (((1,), (1,)), ((), ())), preferred_element_type=jnp.float32
        )
        scores = scores * own_scale + bias
        expo = jnp.exp(scores - jnp.max(scores, axis=-1, keepdims=True))
        probs = (expo / jnp.sum(expo, axis=-1, keepdims=True)).astype(jnp.bfloat16)
        heads.append(dot(probs, value[:, at]).astype(jnp.bfloat16))
    mine_ref[...] = dot(select_mine_ref[...], latents).astype(jnp.bfloat16)
    heads = jnp.concatenate(heads, axis=1)
    arrival.wait()
    mp, role = lax.axis_index("mp"), lax.axis_index("role")
    members = [
        ((mp + along) % mps) * roles + (role + across) % roles
        for along in range(mps)
        for across in range(roles)
    ]
    for at in range(0, model, STRIP):
        here = slice(at, at + STRIP)
        mixed = dot(heads[:, :half], first_ref[:, here]) + dot(heads[:, half:], second_ref[:, here])
        parts = [mixed[index * share : (index + 1) * share] for index in range(group)]

        def of_member(member):
            found = parts[0]
            for index in range(1, group):
                found = jnp.where(member == index, parts[index], found)
            return found

        keep_ref[:, here] = of_member(members[0])
        for member, send_ref in zip(members[1:], send_refs):
            send_ref[:, here] = of_member(member).astype(jnp.bfloat16)


def residual_kernel(mine_ref, embed_ref, pos_ref, out_ref):
    out_ref[...] = dot(mine_ref[...], embed_ref[...]) + pos_ref[...]


def sum_kernel(residual_ref, keep_ref, *refs):
    *others, out_ref = refs
    total = residual_ref[...] + keep_ref[...]
    for other in others:
        total = total + other[...].astype(jnp.float32)
    out_ref[...] = total.astype(jnp.bfloat16)


def to_member(block, along, across):
    mps, roles = lax.axis_size("mp"), lax.axis_size("role")
    route = [
        (mp * roles + role, ((mp + along) % mps) * roles + (role + across) % roles)
        for mp in range(mps)
        for role in range(roles)
    ]
    return lax.ppermute(block, GROUP, route)


def on_device(
    gen_hidden,
    gen_out_weight,
    patch_order,
    frame_block,
    embed_weight,
    pos_table,
    norm_gain,
    qkv_weight,
    out_weight,
):
    slots, frames, depth = gen_hidden.shape
    channels, model = embed_weight.shape
    cols = qkv_weight.shape[2]
    out_weight = pltpu.with_memory_space_constraint(out_weight, pltpu.HBM)
    seqs = lax.axis_size("seq")
    group = lax.axis_size(GROUP)
    mps, roles = lax.axis_size("mp"), lax.axis_size("role")
    patches = seqs * slots
    frame_dev = frames // seqs
    window = frame_dev + 2 * REACH
    rows = window * patches
    own_rows = frame_dev * patches
    share = own_rows // group
    f32, bf16 = jnp.float32, jnp.bfloat16
    array = jax.ShapeDtypeStruct
    grant = (16 if rows <= STEP_ROWS else 40) * MIB

    windows = pl.pallas_call(
        functools.partial(latent_kernel, frame_dev),
        out_shape=array((group * seqs, slots, window, channels), bf16),
        in_specs=[HBM] * 2,
        out_specs=HBM,
        scratch_shapes=[
            pltpu.VMEM((slots, frames, depth), bf16),
            pltpu.VMEM((depth, channels), bf16),
            pltpu.VMEM((slots, frames + 2 * REACH, channels), f32),
            pltpu.VMEM((group * seqs, slots, window, channels), bf16),
            pltpu.SemaphoreType.DMA((1 + depth // LANES,)),
            pltpu.SemaphoreType.DMA((group,)),
        ],
        compiler_params=pltpu.CompilerParams(vmem_limit_bytes=12 * MIB),
        cost_estimate=pl.CostEstimate(
            flops=20_000_000_000, bytes_accessed=40_000_000, transcendentals=0
        ),
        name="partial_latents",
    )(
        pltpu.with_memory_space_constraint(gen_hidden, pltpu.HBM),
        pltpu.with_memory_space_constraint(gen_out_weight, pltpu.HBM),
    )
    moved = lax.all_to_all(
        windows,
        SCATTERED,
        split_axis=0,
        concat_axis=0,
        tiled=True,
    )

    *products, pos_mine, select, select_mine, bias, first = pl.pallas_call(
        functools.partial(weights_kernel, frame_dev, window),
        out_shape=(
            array((3, 2 * channels, cols), bf16),
            array((3, patches, cols), f32),
            array((2 * channels, channels), bf16),
            array((patches, channels), f32),
            array((patches, channels), f32),
            array((patches, channels), f32),
            array((patches, channels), f32),
            array((share, model), f32),
            array((own_rows, rows), bf16),
            array((share, rows), bf16),
            array((own_rows, rows), f32),
            array((cols // 2, model), bf16),
        ),
        in_specs=[SMEM] * 2 + [VMEM] * 3 + [HBM] * 2,
        out_specs=(VMEM,) * 12,
        scratch_shapes=[
            pltpu.VMEM((3, patches, cols), f32),
            pltpu.VMEM((patches, model), f32),
            pltpu.VMEM((3, model, cols), bf16),
            pltpu.SemaphoreType.DMA((3 * (model // min(model, DEPTH)),)),
            pltpu.SemaphoreType.DMA(()),
        ],
        compiler_params=pltpu.CompilerParams(vmem_limit_bytes=24 * MIB),
        cost_estimate=pl.CostEstimate(
            flops=2 * (channels + patches) * model * 3 * cols,
            bytes_accessed=2 * model * 3 * cols,
            transcendentals=0,
        ),
        name="weight_products",
    )(
        patch_order,
        frame_block,
        embed_weight,
        pos_table,
        norm_gain.reshape(model // LANES, LANES),
        pltpu.with_memory_space_constraint(jnp.transpose(qkv_weight, (1, 0, 2)), pltpu.HBM),
        out_weight,
    )

    mine, keep, *sent = pl.pallas_call(
        functools.partial(attend_kernel, roles),
        out_shape=(
            array((share, channels), bf16),
            array((share, model), f32),
            *[array((share, model), bf16)] * (group - 1),
        ),
        in_specs=[VMEM] * 12 + [HBM],
        out_specs=(VMEM,) * (1 + group),
        scratch_shapes=[
            pltpu.VMEM((cols - cols // 2, model), bf16),
            pltpu.SemaphoreType.DMA(()),
        ],
        compiler_params=pltpu.CompilerParams(vmem_limit_bytes=grant),
        name="attend",
    )(
        moved,
        *products,
        select,
        select_mine,
        bias,
        first,
        out_weight,
    )
    small = pltpu.CompilerParams(vmem_limit_bytes=8 * MIB)
    places = [(along, across) for along in range(mps) for across in range(roles)][1:]
    received = [to_member(block, *place) for place, block in zip(places, sent)]
    residual = pl.pallas_call(
        residual_kernel,
        out_shape=array((share, model), f32),
        in_specs=[VMEM] * 3,
        out_specs=VMEM,
        compiler_params=small,
        cost_estimate=pl.CostEstimate(
            flops=2 * share * channels * model,
            bytes_accessed=2 * channels * model,
            transcendentals=0,
        ),
        name="residual",
    )(mine, embed_weight, pos_mine)
    return pl.pallas_call(
        sum_kernel,
        out_shape=array((share, model), bf16),
        in_specs=[VMEM] * (1 + group),
        out_specs=VMEM,
        compiler_params=small,
        name="final_sum",
    )(residual, keep, *received)


def solution(mesh):
    in_specs = (
        P("seq", None, ("mp", "role")),
        P(("mp", "role"), None),
        P(),
        P(),
        P(),
        P(),
        P(),
        P(None, None, ("mp", "role")),
        P(("mp", "role"), None),
    )
    out_specs = P(("seq", "mp", "role"), None)
    return jax.shard_map(
        on_device, mesh=mesh, in_specs=in_specs, out_specs=out_specs, check_vma=False
    )
```

```python
import functools

import jax
import jax.numpy as jnp
from jax import lax
from jax.experimental import pallas as pl
from jax.experimental.pallas import tpu as pltpu
from jax.sharding import PartitionSpec as P

HS = 128
MOSTB = 4
REACH = MOSTB - 1
GROUP = ("mp", "role")
SCATTERED = ("role", "mp", "seq")
LANES = 128
STEP_ROWS = 256
DEPTH = 1024
AHEAD = 9
STRIP = 512
MIB = 1024 * 1024
VMEM = pl.BlockSpec(memory_space=pltpu.VMEM)
SMEM = pl.BlockSpec(memory_space=pltpu.SMEM)
HBM = pl.BlockSpec(memory_space=pltpu.HBM)


def dot(a, b):
    return jnp.dot(a, b, preferred_element_type=jnp.float32)


def latent_kernel(
    frame_dev,
    hidden_hbm,
    weight_hbm,
    out_hbm,
    hidden_ref,
    weight_ref,
    padded_ref,
    out_ref,
    in_sems,
    out_sems,
):
    slots, frames, depth = hidden_ref.shape
    everyone, _, window, channels = out_ref.shape
    seqs = frames // frame_dev
    arrivals = [pltpu.make_async_copy(hidden_hbm, hidden_ref, in_sems.at[0])]
    for index, at in enumerate(range(0, depth, LANES)):
        piece = pl.ds(at, LANES)
        arrivals.append(
            pltpu.make_async_copy(
                weight_hbm.at[piece], weight_ref.at[piece], in_sems.at[index + 1]
            )
        )
    for copy in arrivals:
        copy.start()
    padded_ref[...] = jnp.zeros_like(padded_ref)
    for copy in arrivals:
        copy.wait()
    for slot in range(slots):
        padded_ref[slot, REACH : REACH + frames] = dot(hidden_ref[slot], weight_ref[...])
    pieces = [
        padded_ref[:, to * frame_dev : to * frame_dev + window].astype(out_ref.dtype)
        for to in range(seqs)
    ]
    leaving = []
    for index, first in enumerate(range(0, everyone, seqs)):
        for to in range(seqs):
            out_ref[first + to] = pieces[to]
        part = pl.ds(first, seqs)
        leaving.append(
            pltpu.make_async_copy(out_ref.at[part], out_hbm.at[part], out_sems.at[index])
        )
        leaving[-1].start()
    for copy in leaving:
        copy.wait()


def weights_kernel(
    frame_dev,
    window,
    order_ref,
    block_ref,
    embed_ref,
    pos_ref,
    gain_ref,
    weight_hbm,
    out_weight_hbm,
    scaled_ref,
    offset_ref,
    gram_ref,
    cross_ref,
    level_ref,
    natural_cross_ref,
    natural_level_ref,
    pos_mine_ref,
    select_ref,
    select_mine_ref,
    bias_ref,
    first_ref,
    natural_ref,
    pos_all_ref,
    weight_ref,
    sems,
    first_sem,
):
    channels, model = embed_ref.shape
    patches = pos_ref.shape[0]
    frames = block_ref.shape[0]
    own_rows, rows = bias_ref.shape
    share = select_mine_ref.shape[0]
    device = lax.axis_index("seq")
    member = lax.axis_index(GROUP)

    deep = min(model, DEPTH)
    parts = [(index, at) for index in range(3) for at in range(0, model, deep)]

    def arrival(part):
        index, at = parts[part]
        place = (index, pl.ds(at, deep))
        return pltpu.make_async_copy(weight_hbm.at[place], weight_ref.at[place], sems.at[part])

    first = pltpu.make_async_copy(
        out_weight_hbm.at[pl.ds(0, first_ref.shape[0])], first_ref, first_sem
    )
    for part in range(min(AHEAD, len(parts))):
        arrival(part).start()
    first.start()

    pos = pos_ref[...].astype(jnp.float32)
    pos_all_ref[...] = pos

    column = lax.broadcasted_iota(jnp.int32, (1, rows), 1)
    column_slot, column_frame = column // window, column % window

    def patch_at(slot, found):
        return jnp.where(column_slot == slot, order_ref[slot], found)

    column_patch = jnp.zeros((1, rows), jnp.int32)
    if patches <= 16:
        for slot in range(patches):
            column_patch = patch_at(slot, column_patch)
    else:
        column_patch = lax.fori_loop(0, patches, patch_at, column_patch)

    def select(count, first):
        row = lax.broadcasted_iota(jnp.int32, (count, rows), 0) + first
        hit = jnp.logical_and(
            column_patch == row % patches, column_frame == row // patches + REACH
        )
        return jnp.where(hit, 1.0, 0.0).astype(jnp.bfloat16)

    select_ref[...] = select(own_rows, 0)
    select_mine_ref[...] = select(share, member * share)
    for frame in range(frame_dev * patches // share):
        row = frame * share

        @pl.when(member == frame)
        def _():
            for at in range(share):
                mine = (row + at) % patches
                pos_mine_ref[at : at + 1, :] = pos_all_ref[mine : mine + 1, :]

    def block_of(frame):
        inside = jnp.logical_and(frame >= 0, frame < frames)
        return jnp.where(inside, block_ref[jnp.clip(frame, 0, frames - 1)], -1)

    column_block = jnp.full((1, rows), -1, jnp.int32)
    for frame in range(window):
        found = block_of(device * frame_dev - REACH + frame)
        column_block = jnp.where(column_frame == frame, found, column_block)
    row_frame = lax.broadcasted_iota(jnp.int32, (own_rows, rows), 0) // patches
    row_block = jnp.full((own_rows, rows), -2, jnp.int32)
    for frame in range(frame_dev):
        row_block = jnp.where(row_frame == frame, block_of(device * frame_dev + frame), row_block)
    bias_ref[...] = jnp.where(row_block == column_block, 0.0, -1e30)

    gain = jnp.concatenate(
        [gain_ref[at : at + 1, :].astype(jnp.float32) for at in range(model // LANES)], axis=1
    )
    left = jnp.concatenate([embed_ref[...].astype(jnp.float32) * gain, pos * gain], axis=0)
    left = left.astype(jnp.bfloat16)
    def keep(ref, scaled):
        high = scaled.astype(jnp.bfloat16)
        ref[:channels] = high
        ref[channels:] = (scaled - high.astype(jnp.float32)).astype(jnp.bfloat16)

    plain = jnp.concatenate([embed_ref[...], pos_ref[...]], axis=0)
    both = lax.dot_general(
        plain, embed_ref[...], (((1,), (1,)), ((), ())), preferred_element_type=jnp.float32
    )
    keep(gram_ref, both[:channels])
    natural_cross_ref[...] = 2.0 * both[channels:]
    level = jnp.sum(pos * pos, axis=-1, keepdims=True) / channels
    natural_level_ref[...] = jnp.broadcast_to(level, (patches, channels))

    for part, (index, at) in enumerate(parts):
        arrival(part).wait()
        if part + AHEAD < len(parts):
            arrival(part + AHEAD).start()
        here = slice(at, at + deep)
        product = dot(left[:, here], weight_ref[index, here])
        both = product if at == 0 else both + product
        if at + deep == model:
            keep(scaled_ref.at[index], both[:channels])
            natural_ref[index] = both[channels:]

    offset_ref[0] = natural_ref[0]

    def place(slot):
        to, at = pl.ds(slot, 1), pl.ds(order_ref[slot], 1)
        cross_ref[to, :] = natural_cross_ref[at, :]
        level_ref[to, :] = natural_level_ref[at, :]
        for index in range(1, 3):
            offset_ref[index, to, :] = natural_ref[index, at, :]

    if patches <= 16:
        for slot in range(patches):
            place(slot)
    else:
        pl.loop(0, patches)(place)
    first.wait()


def attend_kernel(
    roles,
    partial_ref,
    scaled_ref,
    offset_ref,
    gram_ref,
    cross_ref,
    level_ref,
    natural_cross_ref,
    natural_level_ref,
    select_ref,
    select_mine_ref,
    bias_ref,
    first_ref,
    out_weight_hbm,
    mine_ref,
    keep_ref,
    *rest,
):
    *send_refs, early_ref, second_ref, sem = rest
    half = first_ref.shape[0]
    arrival = pltpu.make_async_copy(out_weight_hbm.at[pl.ds(half, half)], second_ref, sem)
    arrival.start()
    everyone, slots, window, channels = partial_ref.shape
    share, model = keep_ref.shape
    group = 1 + len(send_refs)
    mps = group // roles
    seqs = everyone // group
    patches = seqs * slots
    rows = patches * window
    cols = out_weight_hbm.shape[0]

    total = partial_ref[:seqs].astype(jnp.float32)
    for other in range(1, group):
        total = total + partial_ref[other * seqs : (other + 1) * seqs].astype(jnp.float32)
    latents = total.reshape(rows, channels).astype(jnp.bfloat16)
    own = dot(select_ref[...], latents).astype(jnp.bfloat16)

    def apply(part, table):
        return dot(jnp.concatenate([part, part], axis=1), table)

    def by_row(table):
        wide = jnp.broadcast_to(table[:, None], (patches, window, table.shape[1]))
        return wide.reshape(rows, table.shape[1])

    def by_patch(table):
        return jnp.concatenate([table] * (group * share // patches), axis=0)

    def scale_of(part, cross, level):
        slope = apply(part, gram_ref[...]) + cross
        squares = slope * part.astype(jnp.float32) + level
        mean = jnp.maximum(jnp.sum(squares, axis=-1, keepdims=True), 0.0) / model
        return lax.rsqrt(mean + 1e-06)

    scale = scale_of(latents, by_row(cross_ref[...]), by_row(level_ref[...]))
    own_scale = scale_of(own, by_patch(natural_cross_ref[...]), by_patch(natural_level_ref[...]))
    own_scale = own_scale * (HS**-0.5)

    def project(index):
        flat = apply(latents, scaled_ref[index]) + by_row(offset_ref[index])
        return (flat * scale).astype(jnp.bfloat16)

    query = (apply(own, scaled_ref[0]) + by_patch(offset_ref[0])).astype(jnp.bfloat16)
    key, value = project(1), project(2)
    bias = bias_ref[...]
    heads = []
    for head in range(cols // HS):
        at = slice(head * HS, (head + 1) * HS)
        scores = lax.dot_general(
            query[:, at], key[:, at], (((1,), (1,)), ((), ())), preferred_element_type=jnp.float32
        )
        scores = scores * own_scale + bias
        expo = jnp.exp(scores - jnp.max(scores, axis=-1, keepdims=True))
        probs = (expo / jnp.sum(expo, axis=-1, keepdims=True)).astype(jnp.bfloat16)
        heads.append(dot(probs, value[:, at]).astype(jnp.bfloat16))
        if (head + 1) * HS == half:
            done = jnp.concatenate(heads, axis=1)
            for first in range(0, model, STRIP):
                here = slice(first, first + STRIP)
                early_ref[:, here] = dot(done, first_ref[:, here])
            heads = []
    mine_ref[...] = dot(select_mine_ref[...], latents).astype(jnp.bfloat16)
    heads = jnp.concatenate(heads, axis=1)
    arrival.wait()
    mp, role = lax.axis_index("mp"), lax.axis_index("role")
    members = [
        ((mp + along) % mps) * roles + (role + across) % roles
        for along in range(mps)
        for across in range(roles)
    ]
    for at in range(0, model, STRIP):
        here = slice(at, at + STRIP)
        mixed = early_ref[:, here] + dot(heads, second_ref[:, here])
        parts = [mixed[index * share : (index + 1) * share] for index in range(group)]

        def of_member(member):
            found = parts[0]
            for index in range(1, group):
                found = jnp.where(member == index, parts[index], found)
            return found

        keep_ref[:, here] = of_member(members[0])
        for member, send_ref in zip(members[1:], send_refs):
            send_ref[:, here] = of_member(member).astype(jnp.bfloat16)


def residual_kernel(mine_ref, embed_ref, pos_ref, out_ref):
    out_ref[...] = dot(mine_ref[...], embed_ref[...]) + pos_ref[...]


def sum_kernel(residual_ref, keep_ref, *refs):
    *others, out_ref = refs
    total = residual_ref[...] + keep_ref[...]
    for other in others:
        total = total + other[...].astype(jnp.float32)
    out_ref[...] = total.astype(jnp.bfloat16)


def to_member(block, along, across):
    mps, roles = lax.axis_size("mp"), lax.axis_size("role")
    route = [
        (mp * roles + role, ((mp + along) % mps) * roles + (role + across) % roles)
        for mp in range(mps)
        for role in range(roles)
    ]
    return lax.ppermute(block, GROUP, route)


def on_device(
    gen_hidden,
    gen_out_weight,
    patch_order,
    frame_block,
    embed_weight,
    pos_table,
    norm_gain,
    qkv_weight,
    out_weight,
):
    slots, frames, depth = gen_hidden.shape
    channels, model = embed_weight.shape
    cols = qkv_weight.shape[2]
    out_weight = pltpu.with_memory_space_constraint(out_weight, pltpu.HBM)
    seqs = lax.axis_size("seq")
    group = lax.axis_size(GROUP)
    mps, roles = lax.axis_size("mp"), lax.axis_size("role")
    patches = seqs * slots
    frame_dev = frames // seqs
    window = frame_dev + 2 * REACH
    rows = window * patches
    own_rows = frame_dev * patches
    share = own_rows // group
    f32, bf16 = jnp.float32, jnp.bfloat16
    array = jax.ShapeDtypeStruct
    grant = (16 if rows <= STEP_ROWS else 40) * MIB

    windows = pl.pallas_call(
        functools.partial(latent_kernel, frame_dev),
        out_shape=array((group * seqs, slots, window, channels), bf16),
        in_specs=[HBM] * 2,
        out_specs=HBM,
        scratch_shapes=[
            pltpu.VMEM((slots, frames, depth), bf16),
            pltpu.VMEM((depth, channels), bf16),
            pltpu.VMEM((slots, frames + 2 * REACH, channels), f32),
            pltpu.VMEM((group * seqs, slots, window, channels), bf16),
            pltpu.SemaphoreType.DMA((1 + depth // LANES,)),
            pltpu.SemaphoreType.DMA((group,)),
        ],
        compiler_params=pltpu.CompilerParams(vmem_limit_bytes=12 * MIB),
        cost_estimate=pl.CostEstimate(
            flops=20_000_000_000, bytes_accessed=40_000_000, transcendentals=0
        ),
        name="partial_latents",
    )(
        pltpu.with_memory_space_constraint(gen_hidden, pltpu.HBM),
        pltpu.with_memory_space_constraint(gen_out_weight, pltpu.HBM),
    )
    moved = lax.all_to_all(
        windows,
        SCATTERED,
        split_axis=0,
        concat_axis=0,
        tiled=True,
    )

    *products, pos_mine, select, select_mine, bias, first = pl.pallas_call(
        functools.partial(weights_kernel, frame_dev, window),
        out_shape=(
            array((3, 2 * channels, cols), bf16),
            array((3, patches, cols), f32),
            array((2 * channels, channels), bf16),
            array((patches, channels), f32),
            array((patches, channels), f32),
            array((patches, channels), f32),
            array((patches, channels), f32),
            array((share, model), f32),
            array((own_rows, rows), bf16),
            array((share, rows), bf16),
            array((own_rows, rows), f32),
            array((cols // 2, model), bf16),
        ),
        in_specs=[SMEM] * 2 + [VMEM] * 3 + [HBM] * 2,
        out_specs=(VMEM,) * 12,
        scratch_shapes=[
            pltpu.VMEM((3, patches, cols), f32),
            pltpu.VMEM((patches, model), f32),
            pltpu.VMEM((3, model, cols), bf16),
            pltpu.SemaphoreType.DMA((3 * (model // min(model, DEPTH)),)),
            pltpu.SemaphoreType.DMA(()),
        ],
        compiler_params=pltpu.CompilerParams(vmem_limit_bytes=24 * MIB),
        cost_estimate=pl.CostEstimate(
            flops=2 * (channels + patches) * model * 3 * cols,
            bytes_accessed=2 * model * 3 * cols,
            transcendentals=0,
        ),
        name="weight_products",
    )(
        patch_order,
        frame_block,
        embed_weight,
        pos_table,
        norm_gain.reshape(model // LANES, LANES),
        pltpu.with_memory_space_constraint(jnp.transpose(qkv_weight, (1, 0, 2)), pltpu.HBM),
        out_weight,
    )

    mine, keep, *sent = pl.pallas_call(
        functools.partial(attend_kernel, roles),
        out_shape=(
            array((share, channels), bf16),
            array((share, model), f32),
            *[array((share, model), bf16)] * (group - 1),
        ),
        in_specs=[VMEM] * 12 + [HBM],
        out_specs=(VMEM,) * (1 + group),
        scratch_shapes=[
            pltpu.VMEM((own_rows, model), f32),
            pltpu.VMEM((cols - cols // 2, model), bf16),
            pltpu.SemaphoreType.DMA(()),
        ],
        compiler_params=pltpu.CompilerParams(vmem_limit_bytes=grant),
        name="attend",
    )(
        moved,
        *products,
        select,
        select_mine,
        bias,
        first,
        out_weight,
    )
    small = pltpu.CompilerParams(vmem_limit_bytes=8 * MIB)
    places = [(along, across) for along in range(mps) for across in range(roles)][1:]
    received = [to_member(block, *place) for place, block in zip(places, sent)]
    residual = pl.pallas_call(
        residual_kernel,
        out_shape=array((share, model), f32),
        in_specs=[VMEM] * 3,
        out_specs=VMEM,
        compiler_params=small,
        cost_estimate=pl.CostEstimate(
            flops=2 * share * channels * model,
            bytes_accessed=2 * channels * model,
            transcendentals=0,
        ),
        name="residual",
    )(mine, embed_weight, pos_mine)
    return pl.pallas_call(
        sum_kernel,
        out_shape=array((share, model), bf16),
        in_specs=[VMEM] * (1 + group),
        out_specs=VMEM,
        compiler_params=small,
        name="final_sum",
    )(residual, keep, *received)


def solution(mesh):
    in_specs = (
        P("seq", None, ("mp", "role")),
        P(("mp", "role"), None),
        P(),
        P(),
        P(),
        P(),
        P(),
        P(None, None, ("mp", "role")),
        P(("mp", "role"), None),
    )
    out_specs = P(("seq", "mp", "role"), None)
    return jax.shard_map(
        on_device, mesh=mesh, in_specs=in_specs, out_specs=out_specs, check_vma=False
    )
```

```python
import functools

import jax
import jax.numpy as jnp
from jax import lax
from jax.experimental import pallas as pl
from jax.experimental.pallas import tpu as pltpu
from jax.sharding import PartitionSpec as P

HS = 128
MOSTB = 4
REACH = MOSTB - 1
GROUP = ("mp", "role")
SCATTERED = ("mp", "role", "seq")
LANES = 128
STEP_ROWS = 256
DEPTH = 1024
AHEAD = 9
STRIP = 512
MIB = 1024 * 1024
VMEM = pl.BlockSpec(memory_space=pltpu.VMEM)
SMEM = pl.BlockSpec(memory_space=pltpu.SMEM)
HBM = pl.BlockSpec(memory_space=pltpu.HBM)


def dot(a, b):
    return jnp.dot(a, b, preferred_element_type=jnp.float32)


def latent_kernel(
    frame_dev,
    hidden_hbm,
    weight_hbm,
    out_hbm,
    hidden_ref,
    weight_ref,
    padded_ref,
    out_ref,
    in_sems,
    out_sems,
):
    slots, frames, depth = hidden_ref.shape
    everyone, _, window, channels = out_ref.shape
    seqs = frames // frame_dev
    arrivals = [pltpu.make_async_copy(hidden_hbm, hidden_ref, in_sems.at[0])]
    for index, at in enumerate(range(0, depth, LANES)):
        piece = pl.ds(at, LANES)
        arrivals.append(
            pltpu.make_async_copy(
                weight_hbm.at[piece], weight_ref.at[piece], in_sems.at[index + 1]
            )
        )
    for copy in arrivals:
        copy.start()
    padded_ref[...] = jnp.zeros_like(padded_ref)
    for copy in arrivals:
        copy.wait()
    for slot in range(slots):
        padded_ref[slot, REACH : REACH + frames] = dot(hidden_ref[slot], weight_ref[...])
    pieces = [
        padded_ref[:, to * frame_dev : to * frame_dev + window].astype(out_ref.dtype)
        for to in range(seqs)
    ]
    leaving = []
    for index, first in enumerate(range(0, everyone, seqs)):
        for to in range(seqs):
            out_ref[first + to] = pieces[to]
        part = pl.ds(first, seqs)
        leaving.append(
            pltpu.make_async_copy(out_ref.at[part], out_hbm.at[part], out_sems.at[index])
        )
        leaving[-1].start()
    for copy in leaving:
        copy.wait()


def weights_kernel(
    frame_dev,
    window,
    order_ref,
    block_ref,
    embed_ref,
    pos_ref,
    gain_ref,
    weight_hbm,
    out_weight_hbm,
    scaled_ref,
    offset_ref,
    gram_ref,
    cross_ref,
    level_ref,
    natural_cross_ref,
    natural_level_ref,
    pos_mine_ref,
    select_ref,
    select_mine_ref,
    bias_ref,
    first_ref,
    natural_ref,
    pos_all_ref,
    weight_ref,
    sems,
    first_sem,
):
    channels, model = embed_ref.shape
    patches = pos_ref.shape[0]
    frames = block_ref.shape[0]
    own_rows, rows = bias_ref.shape
    share = select_mine_ref.shape[0]
    device = lax.axis_index("seq")
    member = lax.axis_index(GROUP)

    deep = min(model, DEPTH)
    parts = [(index, at) for index in range(3) for at in range(0, model, deep)]

    def arrival(part):
        index, at = parts[part]
        place = (index, pl.ds(at, deep))
        return pltpu.make_async_copy(weight_hbm.at[place], weight_ref.at[place], sems.at[part])

    first = pltpu.make_async_copy(
        out_weight_hbm.at[pl.ds(0, first_ref.shape[0])], first_ref, first_sem
    )
    for part in range(min(AHEAD, len(parts))):
        arrival(part).start()
    first.start()

    pos = pos_ref[...].astype(jnp.float32)
    pos_all_ref[...] = pos

    column = lax.broadcasted_iota(jnp.int32, (1, rows), 1)
    column_slot, column_frame = column // window, column % window

    def patch_at(slot, found):
        return jnp.where(column_slot == slot, order_ref[slot], found)

    column_patch = jnp.zeros((1, rows), jnp.int32)
    if patches <= 16:
        for slot in range(patches):
            column_patch = patch_at(slot, column_patch)
    else:
        column_patch = lax.fori_loop(0, patches, patch_at, column_patch)

    def select(count, first):
        row = lax.broadcasted_iota(jnp.int32, (count, rows), 0) + first
        hit = jnp.logical_and(
            column_patch == row % patches, column_frame == row // patches + REACH
        )
        return jnp.where(hit, 1.0, 0.0).astype(jnp.bfloat16)

    select_ref[...] = select(own_rows, 0)
    select_mine_ref[...] = select(share, member * share)
    for frame in range(frame_dev * patches // share):
        row = frame * share

        @pl.when(member == frame)
        def _():
            for at in range(share):
                mine = (row + at) % patches
                pos_mine_ref[at : at + 1, :] = pos_all_ref[mine : mine + 1, :]

    def block_of(frame):
        inside = jnp.logical_and(frame >= 0, frame < frames)
        return jnp.where(inside, block_ref[jnp.clip(frame, 0, frames - 1)], -1)

    column_block = jnp.full((1, rows), -1, jnp.int32)
    for frame in range(window):
        found = block_of(device * frame_dev - REACH + frame)
        column_block = jnp.where(column_frame == frame, found, column_block)
    row_frame = lax.broadcasted_iota(jnp.int32, (own_rows, rows), 0) // patches
    row_block = jnp.full((own_rows, rows), -2, jnp.int32)
    for frame in range(frame_dev):
        row_block = jnp.where(row_frame == frame, block_of(device * frame_dev + frame), row_block)
    bias_ref[...] = jnp.where(row_block == column_block, 0.0, -1e30)

    gain = jnp.concatenate(
        [gain_ref[at : at + 1, :].astype(jnp.float32) for at in range(model // LANES)], axis=1
    )
    left = jnp.concatenate([embed_ref[...].astype(jnp.float32) * gain, pos * gain], axis=0)
    left = left.astype(jnp.bfloat16)
    def keep(ref, scaled):
        high = scaled.astype(jnp.bfloat16)
        ref[:channels] = high
        ref[channels:] = (scaled - high.astype(jnp.float32)).astype(jnp.bfloat16)

    plain = jnp.concatenate([embed_ref[...], pos_ref[...]], axis=0)
    both = lax.dot_general(
        plain, embed_ref[...], (((1,), (1,)), ((), ())), preferred_element_type=jnp.float32
    )
    keep(gram_ref, both[:channels])
    natural_cross_ref[...] = 2.0 * both[channels:]
    level = jnp.sum(pos * pos, axis=-1, keepdims=True) / channels
    natural_level_ref[...] = jnp.broadcast_to(level, (patches, channels))

    for part, (index, at) in enumerate(parts):
        arrival(part).wait()
        if part + AHEAD < len(parts):
            arrival(part + AHEAD).start()
        here = slice(at, at + deep)
        product = dot(left[:, here], weight_ref[index, here])
        both = product if at == 0 else both + product
        if at + deep == model:
            keep(scaled_ref.at[index], both[:channels])
            natural_ref[index] = both[channels:]

    offset_ref[0] = natural_ref[0]

    def place(slot):
        to, at = pl.ds(slot, 1), pl.ds(order_ref[slot], 1)
        cross_ref[to, :] = natural_cross_ref[at, :]
        level_ref[to, :] = natural_level_ref[at, :]
        for index in range(1, 3):
            offset_ref[index, to, :] = natural_ref[index, at, :]

    if patches <= 16:
        for slot in range(patches):
            place(slot)
    else:
        pl.loop(0, patches)(place)
    first.wait()


def attend_kernel(
    roles,
    partial_ref,
    scaled_ref,
    offset_ref,
    gram_ref,
    cross_ref,
    level_ref,
    natural_cross_ref,
    natural_level_ref,
    select_ref,
    select_mine_ref,
    bias_ref,
    first_ref,
    out_weight_hbm,
    mine_ref,
    keep_ref,
    *rest,
):
    *send_refs, second_ref, sem = rest
    half = first_ref.shape[0]
    arrival = pltpu.make_async_copy(out_weight_hbm.at[pl.ds(half, half)], second_ref, sem)
    arrival.start()
    everyone, slots, window, channels = partial_ref.shape
    share, model = keep_ref.shape
    group = 1 + len(send_refs)
    mps = group // roles
    seqs = everyone // group
    patches = seqs * slots
    rows = patches * window
    cols = out_weight_hbm.shape[0]

    total = partial_ref[:seqs].astype(jnp.float32)
    for other in range(1, group):
        total = total + partial_ref[other * seqs : (other + 1) * seqs].astype(jnp.float32)
    latents = total.reshape(rows, channels).astype(jnp.bfloat16)
    own = dot(select_ref[...], latents).astype(jnp.bfloat16)

    def apply(part, table):
        return dot(jnp.concatenate([part, part], axis=1), table)

    def by_row(table):
        wide = jnp.broadcast_to(table[:, None], (patches, window, table.shape[1]))
        return wide.reshape(rows, table.shape[1])

    def by_patch(table):
        return jnp.concatenate([table] * (group * share // patches), axis=0)

    def scale_of(part, cross, level):
        slope = apply(part, gram_ref[...]) + cross
        squares = slope * part.astype(jnp.float32) + level
        mean = jnp.maximum(jnp.sum(squares, axis=-1, keepdims=True), 0.0) / model
        return lax.rsqrt(mean + 1e-06)

    scale = scale_of(latents, by_row(cross_ref[...]), by_row(level_ref[...]))
    own_scale = scale_of(own, by_patch(natural_cross_ref[...]), by_patch(natural_level_ref[...]))
    own_scale = own_scale * (HS**-0.5)

    def project(index):
        flat = apply(latents, scaled_ref[index]) + by_row(offset_ref[index])
        return (flat * scale).astype(jnp.bfloat16)

    query = (apply(own, scaled_ref[0]) + by_patch(offset_ref[0])).astype(jnp.bfloat16)
    key, value = project(1), project(2)
    bias = bias_ref[...]
    heads = []
    for head in range(cols // HS):
        at = slice(head * HS, (head + 1) * HS)
        scores = lax.dot_general(
            query[:, at], key[:, at], (((1,), (1,)), ((), ())), preferred_element_type=jnp.float32
        )
        scores = scores * own_scale + bias
        expo = jnp.exp(scores - jnp.max(scores, axis=-1, keepdims=True))
        probs = (expo / jnp.sum(expo, axis=-1, keepdims=True)).astype(jnp.bfloat16)
        heads.append(dot(probs, value[:, at]).astype(jnp.bfloat16))
    mine_ref[...] = dot(select_mine_ref[...], latents).astype(jnp.bfloat16)
    heads = jnp.concatenate(heads, axis=1)
    arrival.wait()
    mp, role = lax.axis_index("mp"), lax.axis_index("role")
    members = [
        ((mp + along) % mps) * roles + (role + across) % roles
        for along in range(mps)
        for across in range(roles)
    ]
    for at in range(0, model, STRIP):
        here = slice(at, at + STRIP)
        mixed = dot(heads[:, :half], first_ref[:, here]) + dot(heads[:, half:], second_ref[:, here])
        parts = [mixed[index * share : (index + 1) * share] for index in range(group)]

        def of_member(member):
            found = parts[0]
            for index in range(1, group):
                found = jnp.where(member == index, parts[index], found)
            return found

        keep_ref[:, here] = of_member(members[0])
        for member, send_ref in zip(members[1:], send_refs):
            send_ref[:, here] = of_member(member).astype(jnp.bfloat16)


def residual_kernel(mine_ref, embed_ref, pos_ref, out_ref):
    out_ref[...] = dot(mine_ref[...], embed_ref[...]) + pos_ref[...]


def sum_kernel(residual_ref, keep_ref, *refs):
    *others, out_ref = refs
    total = residual_ref[...] + keep_ref[...]
    for other in others:
        total = total + other[...].astype(jnp.float32)
    out_ref[...] = total.astype(jnp.bfloat16)


def to_member(block, along, across):
    mps, roles = lax.axis_size("mp"), lax.axis_size("role")
    route = [
        (mp * roles + role, ((mp + along) % mps) * roles + (role + across) % roles)
        for mp in range(mps)
        for role in range(roles)
    ]
    return lax.ppermute(block, GROUP, route)


def on_device(
    gen_hidden,
    gen_out_weight,
    patch_order,
    frame_block,
    embed_weight,
    pos_table,
    norm_gain,
    qkv_weight,
    out_weight,
):
    slots, frames, depth = gen_hidden.shape
    channels, model = embed_weight.shape
    cols = qkv_weight.shape[2]
    out_weight = pltpu.with_memory_space_constraint(out_weight, pltpu.HBM)
    seqs = lax.axis_size("seq")
    group = lax.axis_size(GROUP)
    mps, roles = lax.axis_size("mp"), lax.axis_size("role")
    patches = seqs * slots
    frame_dev = frames // seqs
    window = frame_dev + 2 * REACH
    rows = window * patches
    own_rows = frame_dev * patches
    share = own_rows // group
    f32, bf16 = jnp.float32, jnp.bfloat16
    array = jax.ShapeDtypeStruct
    grant = (16 if rows <= STEP_ROWS else 40) * MIB

    windows = pl.pallas_call(
        functools.partial(latent_kernel, frame_dev),
        out_shape=array((group * seqs, slots, window, channels), bf16),
        in_specs=[HBM] * 2,
        out_specs=HBM,
        scratch_shapes=[
            pltpu.VMEM((slots, frames, depth), bf16),
            pltpu.VMEM((depth, channels), bf16),
            pltpu.VMEM((slots, frames + 2 * REACH, channels), f32),
            pltpu.VMEM((group * seqs, slots, window, channels), bf16),
            pltpu.SemaphoreType.DMA((1 + depth // LANES,)),
            pltpu.SemaphoreType.DMA((group,)),
        ],
        compiler_params=pltpu.CompilerParams(vmem_limit_bytes=12 * MIB),
        cost_estimate=pl.CostEstimate(
            flops=20_000_000_000, bytes_accessed=40_000_000, transcendentals=0
        ),
        name="partial_latents",
    )(
        pltpu.with_memory_space_constraint(gen_hidden, pltpu.HBM),
        pltpu.with_memory_space_constraint(gen_out_weight, pltpu.HBM),
    )
    moved = lax.all_to_all(
        windows,
        SCATTERED,
        split_axis=0,
        concat_axis=0,
        tiled=True,
    )

    *products, pos_mine, select, select_mine, bias, first = pl.pallas_call(
        functools.partial(weights_kernel, frame_dev, window),
        out_shape=(
            array((3, 2 * channels, cols), bf16),
            array((3, patches, cols), f32),
            array((2 * channels, channels), bf16),
            array((patches, channels), f32),
            array((patches, channels), f32),
            array((patches, channels), f32),
            array((patches, channels), f32),
            array((share, model), f32),
            array((own_rows, rows), bf16),
            array((share, rows), bf16),
            array((own_rows, rows), f32),
            array((cols // 2, model), bf16),
        ),
        in_specs=[SMEM] * 2 + [VMEM] * 3 + [HBM] * 2,
        out_specs=(VMEM,) * 12,
        scratch_shapes=[
            pltpu.VMEM((3, patches, cols), f32),
            pltpu.VMEM((patches, model), f32),
            pltpu.VMEM((3, model, cols), bf16),
            pltpu.SemaphoreType.DMA((3 * (model // min(model, DEPTH)),)),
            pltpu.SemaphoreType.DMA(()),
        ],
        compiler_params=pltpu.CompilerParams(vmem_limit_bytes=24 * MIB),
        cost_estimate=pl.CostEstimate(
            flops=2 * (channels + patches) * model * 3 * cols,
            bytes_accessed=2 * model * 3 * cols,
            transcendentals=0,
        ),
        name="weight_products",
    )(
        patch_order,
        frame_block,
        embed_weight,
        pos_table,
        norm_gain.reshape(model // LANES, LANES),
        pltpu.with_memory_space_constraint(jnp.transpose(qkv_weight, (1, 0, 2)), pltpu.HBM),
        out_weight,
    )

    mine, keep, *sent = pl.pallas_call(
        functools.partial(attend_kernel, roles),
        out_shape=(
            array((share, channels), bf16),
            array((share, model), f32),
            *[array((share, model), bf16)] * (group - 1),
        ),
        in_specs=[VMEM] * 12 + [HBM],
        out_specs=(VMEM,) * (1 + group),
        scratch_shapes=[
            pltpu.VMEM((cols - cols // 2, model), bf16),
            pltpu.SemaphoreType.DMA(()),
        ],
        compiler_params=pltpu.CompilerParams(vmem_limit_bytes=grant),
        name="attend",
    )(
        moved,
        *products,
        select,
        select_mine,
        bias,
        first,
        out_weight,
    )
    small = pltpu.CompilerParams(vmem_limit_bytes=8 * MIB)
    places = [(along, across) for along in range(mps) for across in range(roles)][1:]
    received = [to_member(block, *place) for place, block in zip(places, sent)]
    residual = pl.pallas_call(
        residual_kernel,
        out_shape=array((share, model), f32),
        in_specs=[VMEM] * 3,
        out_specs=VMEM,
        compiler_params=small,
        cost_estimate=pl.CostEstimate(
            flops=2 * share * channels * model,
            bytes_accessed=2 * channels * model,
            transcendentals=0,
        ),
        name="residual",
    )(mine, embed_weight, pos_mine)
    return pl.pallas_call(
        sum_kernel,
        out_shape=array((share, model), bf16),
        in_specs=[VMEM] * (1 + group),
        out_specs=VMEM,
        compiler_params=small,
        name="final_sum",
    )(residual, keep, *received)


def solution(mesh):
    in_specs = (
        P("seq", None, ("mp", "role")),
        P(("mp", "role"), None),
        P(),
        P(),
        P(),
        P(),
        P(),
        P(None, None, ("mp", "role")),
        P(("mp", "role"), None),
    )
    out_specs = P(("seq", "mp", "role"), None)
    return jax.shard_map(
        on_device, mesh=mesh, in_specs=in_specs, out_specs=out_specs, check_vma=False
    )
```
